32 devices in a mesh: img: 2 (over x), ty: 4 (over y, core), tx: 4 (over z).
Axes of the slice: x: 2, y: 2, z: 4, core: 2. Of those that a mesh axis runs over, the one named last changes fastest.
Arguments:
- tokens: bfloat16 [2, 2048, 1152], P('img', ('ty', 'tx')), may hold values from -6 to 6
- cotangent: bfloat16 [2, 2048, 1152], P('img', ('ty', 'tx')), may hold values from -6 to 6
- class_embed: float32 [2, 1152], P('img'), may hold values from -6 to 6
- timestep: int32 [2], P('img'), may hold values from 0 to 999
- grid_height: int32 [2], P('img'), may hold values from 16 to 32, as said below
- grid_width: int32 [2], P('img'), may hold values from 32 to 64, as said below
- qkv_weight: bfloat16 [1152, 3456], P('img'), may hold values from -0.1875 to 0.1875
- out_weight: bfloat16 [1152, 1152], P('img'), may hold values from -3 to 3
- up_weight: bfloat16 [1152, 6144], P('img'), may hold values from -0.1875 to 0.1875
- down_weight: bfloat16 [3072, 1152], P('img'), may hold values from -0.109375 to 0.109375
- ada_weight: bfloat16 [6912, 1152], P(('img', 'ty', 'tx')), may hold values from -0.1875 to 0.1875
- q_gain: float32 [72], replicated, may hold values from 0.1 to 1.9
- k_gain: float32 [72], replicated, may hold values from 0.1 to 1.9
Outputs:
- mixed: bfloat16 [2, 2048, 1152], P('img', ('ty', 'tx'))
- tokens_grad: bfloat16 [2, 2048, 1152], P('img', ('ty', 'tx'))
- qkv_grad: float32 [1152, 3456], P('img', ('ty', 'tx'))
- out_grad: float32 [1152, 1152], P('img', ('ty', 'tx'))
- up_grad: float32 [1152, 6144], P('img', ('ty', 'tx'))
- down_grad: float32 [3072, 1152], P('img', ('ty', 'tx'))
- ada_grad: float32 [6912, 1152], P(('img', 'ty', 'tx'))
- q_gain_grad: float32 [72], replicated
- k_gain_grad: float32 [72], replicated
The draws below stay inside these ranges and needn't reach their ends.
Inputs may be any that keep to these rules, and one draw needn't show every extreme that they name: `grid_height`: one image, drawn from the seed, has the full grid of 32 by 64 patches; the others are shorter. `grid_width`: as for grid_height; the full image is the same one, and the others are narrower.
All inputs are finite; a program needn't handle non-finite values.
Results may differ from the reference program's by a relative error of at most 0.02.
Values may be sent and summed in bfloat16 or wider, within the bound.
A program may use at most 192 MiB of HBM per device.

```python
import jax
import jax.numpy as jnp
from jax import lax

D = 1152
HEADS = 16
HEAD = 72
FF = 3072
MAX_H = 32
MAX_W = 64
CAP = 128
SLOTS = 2048
IMAGES = 2
N_TY = 4
N_TX = 4


def grid_shapes(key):
    pick_key, height_key, width_key = jax.random.split(key, 3)
    heights = jax.random.randint(height_key, (IMAGES,), MAX_H // 2, MAX_H)
    widths = jax.random.randint(width_key, (IMAGES,), MAX_W // 2, MAX_W)
    chosen = jax.random.randint(pick_key, (), 0, IMAGES)
    full = jnp.arange(IMAGES) == chosen
    return (jnp.where(full, MAX_H, heights).astype(jnp.int32), jnp.where(full, MAX_W, widths).astype(jnp.int32))


def draw_grid_height(key, part):
    return grid_shapes(key)[0]


def draw_grid_width(key, part):
    return grid_shapes(key)[1]


def block_levels(stream_key, dims, cuts, smallest, largest):
    level, own = 1.0, jax.random.fold_in(stream_key, 6)
    for axis_at, blocks in cuts:
        steps = jnp.exp(jax.random.uniform(jax.random.fold_in(own, axis_at), (blocks,), jnp.float32, smallest / len(cuts), largest / len(cuts)))
        level = level * jnp.repeat(steps, dims[axis_at] // blocks).reshape([-1 if axis == axis_at else 1 for axis in range(len(dims))])
    return level


def scatter_about(own_key, dims, scale, most, cuts=(), kind=jnp.bfloat16):
    array = jax.random.normal(own_key, dims, jnp.float32) * scale
    if len(cuts) > 0:
        array = block_levels(own_key, dims, cuts, -0.22, 0.18) * array
    return jnp.clip(array, min=-most, max=most).astype(kind)


def setup_inputs(seed: int = 0) -> dict:
    arg_keys = jax.random.split(jax.random.key(seed), 14)
    return {
        "tokens": scatter_about(arg_keys[0], (IMAGES, SLOTS, D), 1.0, 6.0, ((0, 2), (1, 16))),
        "cotangent": scatter_about(arg_keys[1], (IMAGES, SLOTS, D), 1.0, 6.0, ((0, 2), (1, 16))),
        "class_embed": scatter_about(arg_keys[2], (IMAGES, D), 1.0, 6.0, ((0, 2),), jnp.float32),
        "timestep": jax.random.randint(arg_keys[3], (IMAGES,), 0, 1000).astype(jnp.int32),
        "grid_height": draw_grid_height(jax.random.fold_in(arg_keys[13], 71), 0),
        "grid_width": draw_grid_width(jax.random.fold_in(arg_keys[13], 71), 0),
        "qkv_weight": scatter_about(arg_keys[6], (D, 3 * D), D ** -0.5, 0.1875, ((0, 2),)),
        "out_weight": scatter_about(arg_keys[7], (D, D), (max(D // 256, 2)) ** -0.5, 3.0, ((0, 2),)),
        "up_weight": scatter_about(arg_keys[8], (D, 2 * FF), D ** -0.5, 0.1875, ((0, 2),)),
        "down_weight": scatter_about(arg_keys[9], (FF, D), FF ** -0.5, 0.109375, ((0, 2),)),
        "ada_weight": scatter_about(arg_keys[10], (6 * D, D), D ** -0.5, 0.1875, ((0, 32),)),
        "q_gain": jnp.clip(1.0 + 0.18 * jax.random.normal(arg_keys[11], (HEAD,), jnp.float32), 0.1, 1.9),
        "k_gain": jnp.clip(1.0 + 0.18 * jax.random.normal(arg_keys[12], (HEAD,), jnp.float32), 0.1, 1.9),
    }


EPS = 1e-06
HIGH = lax.Precision.HIGHEST

@jax.custom_vjp
def low(v):
    return lax.optimization_barrier(v.astype(jnp.bfloat16)).astype(jnp.float32)

@jax.custom_vjp
def low_back(v):
    return v

def low_keep(v):
    return (low(v), None)

def low_pass(kept, grad):
    return (grad,)

def back_keep(v):
    return (v, None)

def back_low(kept, grad):
    return (low(grad),)
low.defvjp(low_keep, low_pass)
low_back.defvjp(back_keep, back_low)

def layout(slot, height, width, cap, rows_tiles, cols_tiles):
    tile = slot // cap
    row_tile = tile // cols_tiles
    col_tile = tile % cols_tiles
    local = slot % cap
    top = row_tile * height // rows_tiles
    bottom = (row_tile + 1) * height // rows_tiles
    left = col_tile * width // cols_tiles
    right = (col_tile + 1) * width // cols_tiles
    span = right - left
    valid = local < (bottom - top) * span
    row = jnp.where(valid, top + local // span, 0).astype(jnp.int32)
    col = jnp.where(valid, left + local % span, 0).astype(jnp.int32)
    return (valid, row, col)

def time_embed(step, dim):
    half = dim // 2
    freq = jnp.exp(-jnp.log(10000.0) * jnp.arange(half, dtype=jnp.float32) / half)
    angle = step.astype(jnp.float32)[:, None] * freq
    return jnp.concatenate([jnp.cos(angle), jnp.sin(angle)], axis=-1)

def rotate(part, position):
    quarter = part.shape[-1] // 2
    freq = jnp.exp(-jnp.log(10000.0) * jnp.arange(quarter, dtype=jnp.float32) / quarter)
    angle = position.astype(jnp.float32)[..., None, None] * freq
    first, second = (part[..., :quarter], part[..., quarter:])
    cosine, sine = (jnp.cos(angle), jnp.sin(angle))
    return jnp.concatenate([first * cosine - second * sine, second * cosine + first * sine], axis=-1)

def rope(heads, row, col):
    half = heads.shape[-1] // 2
    return jnp.concatenate([rotate(heads[..., :half], row), rotate(heads[..., half:], col)], axis=-1)

def head_norm(value, gain):
    return value * lax.rsqrt(lax.optimization_barrier(jnp.mean(value * value, axis=-1, keepdims=True)) + EPS) * gain

def rms(value):
    return value * lax.rsqrt(lax.optimization_barrier(jnp.mean(value * value, axis=-1, keepdims=True)) + EPS)

def image_layer(x, cond_row, height, width, wqkv, wout, w12, w3, wada, q_gain, k_gain):
    valid, row, col = layout(jnp.arange(SLOTS, dtype=jnp.int32), height, width, CAP, N_TY, N_TX)
    act = low(jax.nn.silu(cond_row))
    mod = jnp.dot(wada, act, precision=HIGH)
    shift1, scale1, gate1, shift2, scale2, gate2 = jnp.split(mod, 6)
    keep = valid.astype(jnp.float32)[:, None]
    h1 = low(rms(x) * (1.0 + scale1) + shift1)
    qkv = low_back(jnp.dot(h1, wqkv, precision=HIGH)).reshape(SLOTS, 3, HEADS, HEAD)
    query = low(rope(head_norm(qkv[:, 0], q_gain), row, col) * HEAD ** (-0.5))
    key = low(rope(head_norm(qkv[:, 1], k_gain), row, col))
    value = low(qkv[:, 2])
    scores = low_back(jnp.einsum('qhd,khd->hqk', query, key, precision=HIGH))
    scores = jnp.where(valid[None, None, :], scores, -1e+30)
    prob = jax.nn.softmax(scores, axis=-1)
    attn = jnp.einsum('hqk,khd->qhd', low(prob), value, precision=HIGH).reshape(SLOTS, D)
    attn = low(low_back(attn))
    branch = low_back(jnp.dot(attn, wout, precision=HIGH))
    x1 = x + keep * gate1 * branch
    h2 = low(rms(x1) * (1.0 + scale2) + shift2)
    gate_up = low_back(jnp.dot(h2, w12, precision=HIGH))
    mid = low(jax.nn.silu(gate_up[:, :FF]) * gate_up[:, FF:])
    ffn = low_back(jnp.dot(mid, w3, precision=HIGH))
    return x1 + keep * gate2 * ffn

def reference(tokens, cotangent, class_embed, timestep, grid_height, grid_width, qkv_weight, out_weight, up_weight, down_weight, ada_weight, q_gain, k_gain):
    cond = class_embed + time_embed(timestep, D)

    def forward(x, wqkv, wout, w12, w3, wada, qg, kg):

        def one_image(item):
            return image_layer(item[0], item[1], item[2], item[3], wqkv, wout, w12, w3, wada, qg, kg)
        return lax.map(jax.checkpoint(one_image), (x, cond, grid_height, grid_width))
    weights = tuple((w.astype(jnp.float32) for w in (qkv_weight, out_weight, up_weight, down_weight, ada_weight)))
    mixed, pullback = jax.vjp(forward, tokens.astype(jnp.float32), *weights, q_gain, k_gain)
    grads = pullback(cotangent.astype(jnp.float32))
    return (mixed.astype(jnp.bfloat16), grads[0].astype(jnp.bfloat16), grads[1], grads[2], grads[3], grads[4], grads[5], grads[6], grads[7])
```

```python
import functools

import jax
import jax.numpy as jnp
import numpy as np
from jax import lax
from jax.experimental import pallas as pl
from jax.experimental.pallas import tpu as pltpu
from jax.sharding import PartitionSpec as P

HEADS = 16
HEAD = 72


EPS = 1e-06
HIGH = lax.Precision.HIGHEST


def layout(slot, height, width, cap, rows_tiles, cols_tiles):
    tile = slot // cap
    row_tile = tile // cols_tiles
    col_tile = tile % cols_tiles
    local = slot % cap
    top = row_tile * height // rows_tiles
    bottom = (row_tile + 1) * height // rows_tiles
    left = col_tile * width // cols_tiles
    right = (col_tile + 1) * width // cols_tiles
    span = right - left
    valid = local < (bottom - top) * span
    row = jnp.where(valid, top + local // span, 0)
    col = jnp.where(valid, left + local % span, 0)
    return (valid, row, col)


def time_embed(step, dim):
    half = dim // 2
    freq = jnp.exp(-jnp.log(10000.0) * jnp.arange(half, dtype=jnp.float32) / half)
    angle = step.astype(jnp.float32)[:, None] * freq
    return jnp.concatenate([jnp.cos(angle), jnp.sin(angle)], axis=-1)


def rotate(part, position):
    quarter = part.shape[-1] // 2
    freq = jnp.exp(-jnp.log(10000.0) * jnp.arange(quarter, dtype=jnp.float32) / quarter)
    angle = position.astype(jnp.float32)[..., None, None] * freq
    first, second = (part[..., :quarter], part[..., quarter:])
    cosine, sine = (jnp.cos(angle), jnp.sin(angle))
    return jnp.concatenate(
        [first * cosine - second * sine, second * cosine + first * sine], axis=-1
    )


def rope(heads, row, col):
    half = heads.shape[-1] // 2
    return jnp.concatenate(
        [rotate(heads[..., :half], row), rotate(heads[..., half:], col)], axis=-1
    )


def head_norm(value, gain):
    return value * lax.rsqrt(jnp.mean(value * value, axis=-1, keepdims=True) + EPS) * gain


def rms(value):
    return value * lax.rsqrt(jnp.mean(value * value, axis=-1, keepdims=True) + EPS)


def flat_rows(value):
    return value.reshape(-1, value.shape[-1])


def outer_sum(left, right):
    return lax.dot_general(
        flat_rows(left),
        flat_rows(right),
        (((0,), (0,)), ((), ())),
        preferred_element_type=jnp.float32,
    )


def times_transposed(left, weight):
    return lax.dot_general(
        left, weight, (((left.ndim - 1,), (1,)), ((), ())), preferred_element_type=jnp.float32
    )


def masked_scores(query, keys_all, key_valid):
    scores = jnp.einsum("qhd,khd->hqk", query, keys_all, preferred_element_type=jnp.float32)
    return jnp.where(key_valid[None, None, :], scores, -1e30)


def general_body(
    tokens,
    cotangent,
    class_embed,
    timestep,
    grid_height,
    grid_width,
    qkv_weight,
    out_weight,
    up_weight,
    down_weight,
    ada_weight,
    q_gain,
    k_gain,
):
    images, slots_dev, width = tokens.shape
    rows_tiles = lax.axis_size("ty")
    cols_tiles = lax.axis_size("tx")
    slots_all = slots_dev * rows_tiles * cols_tiles
    own_slot = lax.axis_index(("ty", "tx")) * slots_dev + jnp.arange(slots_dev, dtype=jnp.int32)
    all_slot = jnp.arange(slots_all, dtype=jnp.int32)
    valid_q, row_q, col_q = jax.vmap(
        lambda h, w: layout(own_slot, h, w, slots_dev, rows_tiles, cols_tiles)
    )(grid_height, grid_width)
    valid_k = jax.vmap(lambda h, w: layout(all_slot, h, w, slots_dev, rows_tiles, cols_tiles)[0])(
        grid_height, grid_width
    )
    keep = valid_q.astype(jnp.float32)[..., None]
    act = jax.nn.silu(class_embed + time_embed(timestep, width)).astype(jnp.bfloat16)
    mod = lax.dot_general(
        act,
        lax.all_gather(ada_weight, ("img", "ty", "tx"), axis=0, tiled=True),
        (((1,), (1,)), ((), ())),
        preferred_element_type=jnp.float32,
    )
    shift1, scale1, gate1, shift2, scale2, gate2 = [
        part[:, None, :] for part in jnp.split(mod, 6, axis=1)
    ]
    wqkv, wout, w12, w3 = (
        lax.all_gather(qkv_weight, "img", axis=0, tiled=True),
        lax.all_gather(out_weight, "img", axis=0, tiled=True),
        lax.all_gather(up_weight, "img", axis=0, tiled=True),
        lax.all_gather(down_weight, "img", axis=0, tiled=True),
    )
    xf = tokens.astype(jnp.float32)
    norm1, pull_norm1 = jax.vjp(rms, xf)
    h1 = (norm1 * (1.0 + scale1) + shift1).astype(jnp.bfloat16)
    qkv = jnp.dot(h1, wqkv, preferred_element_type=jnp.float32).reshape(
        images, slots_dev, 3, HEADS, HEAD
    )

    def finish(query_raw, key_raw, query_gain, key_gain):
        query = rope(head_norm(query_raw, query_gain), row_q, col_q) * HEAD ** (-0.5)
        return (query, rope(head_norm(key_raw, key_gain), row_q, col_q))

    (query_f, key_f), pull_heads = jax.vjp(finish, qkv[:, :, 0], qkv[:, :, 1], q_gain, k_gain)
    query_b = query_f.astype(jnp.bfloat16)
    key_b = key_f.astype(jnp.bfloat16)
    value_b = qkv[:, :, 2].astype(jnp.bfloat16)
    keys_all, values_all = (
        lax.all_gather(key_b, ("ty", "tx"), axis=1, tiled=True),
        lax.all_gather(value_b, ("ty", "tx"), axis=1, tiled=True),
    )
    index = 0
    scores = masked_scores(query_b[index], keys_all[index], valid_k[index])
    top = jnp.max(scores, axis=-1, keepdims=True)
    lse = top + jnp.log(jnp.sum(jnp.exp(scores - top), axis=-1, keepdims=True))
    prob = jnp.exp(scores - lse).astype(jnp.bfloat16)
    attn_list = [
        jnp.einsum("hqk,khd->qhd", prob, values_all[index], preferred_element_type=jnp.float32)
    ]
    lse_list = [lse]
    attn = jnp.stack(attn_list).reshape(images, slots_dev, width).astype(jnp.bfloat16)
    branch = jnp.dot(attn, wout, preferred_element_type=jnp.float32)
    x1 = xf + keep * gate1 * branch
    norm2, pull_norm2 = jax.vjp(rms, x1)
    h2 = (norm2 * (1.0 + scale2) + shift2).astype(jnp.bfloat16)
    gate_up = jnp.dot(h2, w12, preferred_element_type=jnp.float32)
    hidden = gate_up.shape[-1] // 2
    gate_part, up_part = (gate_up[..., :hidden], gate_up[..., hidden:])
    sig = jax.nn.sigmoid(gate_part)
    silu_gate = gate_part * sig
    mid = (silu_gate * up_part).astype(jnp.bfloat16)
    ffn = jnp.dot(mid, w3, preferred_element_type=jnp.float32)
    mixed = (x1 + keep * gate2 * ffn).astype(jnp.bfloat16)
    grad_out = cotangent.astype(jnp.float32)
    d_gate2 = jnp.sum(grad_out * keep * ffn, axis=1)
    d_ffn = (grad_out * keep * gate2).astype(jnp.bfloat16)
    term_down = outer_sum(mid, d_ffn)
    d_mid = times_transposed(d_ffn, w3)
    d_gate = d_mid * up_part * (sig + gate_part * sig * (1.0 - sig))
    d_up = d_mid * silu_gate
    d_gate_up = jnp.concatenate([d_gate, d_up], axis=-1).astype(jnp.bfloat16)
    term_up = outer_sum(h2, d_gate_up)
    d_h2 = times_transposed(d_gate_up, w12)
    d_scale2 = jnp.sum(d_h2 * norm2, axis=1)
    d_shift2 = jnp.sum(d_h2, axis=1)
    d_x1 = grad_out + pull_norm2(d_h2 * (1.0 + scale2))[0]
    d_gate1 = jnp.sum(d_x1 * keep * branch, axis=1)
    d_branch = (d_x1 * keep * gate1).astype(jnp.bfloat16)
    term_out = outer_sum(attn, d_branch)
    d_attn = (
        times_transposed(d_branch, wout)
        .astype(jnp.bfloat16)
        .reshape(images, slots_dev, HEADS, HEAD)
    )
    keys_back, values_back = (
        lax.all_gather(key_b, ("ty", "tx"), axis=1, tiled=True),
        lax.all_gather(value_b, ("ty", "tx"), axis=1, tiled=True),
    )
    index = 0
    scores = masked_scores(query_b[index], keys_back[index], valid_k[index])
    prob = jnp.exp(scores - lse_list[index])
    d_prob = jnp.einsum(
        "qhd,khd->hqk", d_attn[index], values_back[index], preferred_element_type=jnp.float32
    )
    delta = jnp.sum(prob * d_prob, axis=-1, keepdims=True)
    d_scores = (prob * (d_prob - delta)).astype(jnp.bfloat16)
    dq_list = [
        jnp.einsum("hqk,khd->qhd", d_scores, keys_back[index], preferred_element_type=jnp.float32)
    ]
    dk_list = [
        jnp.einsum("hqk,qhd->khd", d_scores, query_b[index], preferred_element_type=jnp.float32)
    ]
    dv_list = [
        jnp.einsum(
            "hqk,qhd->khd",
            prob.astype(jnp.bfloat16),
            d_attn[index],
            preferred_element_type=jnp.float32,
        )
    ]
    d_key, d_value = (
        lax.psum_scatter(
            jnp.stack(dk_list).astype(jnp.bfloat16), ("ty", "tx"), scatter_dimension=1, tiled=True
        ).astype(jnp.float32),
        lax.psum_scatter(
            jnp.stack(dv_list).astype(jnp.bfloat16), ("ty", "tx"), scatter_dimension=1, tiled=True
        ).astype(jnp.float32),
    )
    d_query_raw, d_key_raw, d_q_gain, d_k_gain = pull_heads((jnp.stack(dq_list), d_key))
    d_qkv = (
        jnp.stack([d_query_raw, d_key_raw, d_value], axis=2)
        .reshape(images, slots_dev, 3 * width)
        .astype(jnp.bfloat16)
    )
    term_qkv = outer_sum(h1, d_qkv)
    d_h1 = times_transposed(d_qkv, wqkv)
    d_scale1 = jnp.sum(d_h1 * norm1, axis=1)
    d_shift1 = jnp.sum(d_h1, axis=1)
    tokens_grad = (d_x1 + pull_norm1(d_h1 * (1.0 + scale1))[0]).astype(jnp.bfloat16)
    d_mod = jnp.concatenate([d_shift1, d_scale1, d_gate1, d_shift2, d_scale2, d_gate2], axis=1)
    act_f = act.astype(jnp.float32)
    ada_grad = lax.psum_scatter(
        lax.dot_general(
            d_mod,
            act_f,
            (((0,), (0,)), ((), ())),
            precision=HIGH,
            preferred_element_type=jnp.float32,
        ),
        ("img", "ty", "tx"),
        scatter_dimension=0,
        tiled=True,
    )
    q_gain_grad, k_gain_grad = lax.psum((d_q_gain, d_k_gain), ("img", "ty", "tx"))
    parts = (
        lax.psum_scatter(
            term_qkv.astype(jnp.bfloat16), ("ty", "tx"), scatter_dimension=1, tiled=True
        ).astype(jnp.float32),
        lax.psum_scatter(
            term_out.astype(jnp.bfloat16), ("ty", "tx"), scatter_dimension=1, tiled=True
        ).astype(jnp.float32),
        lax.psum_scatter(
            term_up.astype(jnp.bfloat16), ("ty", "tx"), scatter_dimension=1, tiled=True
        ).astype(jnp.float32),
        lax.psum_scatter(
            term_down.astype(jnp.bfloat16), ("ty", "tx"), scatter_dimension=1, tiled=True
        ).astype(jnp.float32),
    )
    grads = (
        lax.psum_scatter(
            parts[0].astype(jnp.bfloat16), "img", scatter_dimension=0, tiled=True
        ).astype(jnp.float32),
        lax.psum_scatter(
            parts[1].astype(jnp.bfloat16), "img", scatter_dimension=0, tiled=True
        ).astype(jnp.float32),
        lax.psum_scatter(
            parts[2].astype(jnp.bfloat16), "img", scatter_dimension=0, tiled=True
        ).astype(jnp.float32),
        lax.psum_scatter(
            parts[3].astype(jnp.bfloat16), "img", scatter_dimension=0, tiled=True
        ).astype(jnp.float32),
    )
    return (
        mixed,
        tokens_grad,
        grads[0],
        grads[1],
        grads[2],
        grads[3],
        ada_grad,
        q_gain_grad,
        k_gain_grad,
    )


VMEM_LIMIT = 63 << 20
MESH = pl.DeviceIdType.MESH
PAD = 128
TILE = 128
F32 = jnp.float32
BF16 = jnp.bfloat16


def dot(a, b):
    return lax.dot_general(a, b, (((1,), (0,)), ((), ())), preferred_element_type=F32)


def dot_nt(a, b):
    return lax.dot_general(a, b, (((1,), (1,)), ((), ())), preferred_element_type=F32)


def dot_tn(a, b, precision=None):
    return lax.dot_general(
        a, b, (((0,), (0,)), ((), ())), preferred_element_type=F32, precision=precision
    )


def lanes(shape):
    return lax.broadcasted_iota(jnp.int32, shape, len(shape) - 1)


def split3(value):
    high = value.astype(BF16)
    rest = value - high.astype(F32)
    mid = rest.astype(BF16)
    low = (rest - mid.astype(F32)).astype(BF16)
    return (high, mid, low)


def put_split3(tile, value, lane0):
    at = lanes(tile.shape)
    for k, term in enumerate(split3(value)):
        tile = jnp.where(at == lane0 + k, jnp.broadcast_to(term.astype(F32), tile.shape), tile)
    return tile


OUT, UP, DOWN, QKV = range(4)


def weight_chunks(width, hidden):
    up = []
    step = hidden // 4
    for k in range(4):
        up += [(UP, k * step, step), (UP, hidden + k * step, step)]
    return [(OUT, 0, width)] + up + [(DOWN, 0, width), (QKV, 0, 3 * width)]


def block_kernel(
    tok, cot, act, ada, wh, wout, wup, wdown, wqkv, q_gain, k_gain, tab, hw,
    mixed, tgrad, l_attn, l_h2, l_mid, r_ffn, r_branch, r_gu, qkv_grad, ada_grad, gain_grad, qkv_hbm,
    tok_all, whv, woutv, wupv, wdownv, actbuf, modsend, modbuf, modv,
    cosv, sinv, qraw, kraw, qa, ka, va, kt, qt, onorm, attn_send, attn_in,
    do_in, dot_t, dqt, dkv, dvv, dqkv_send, dqkv_in, dw_send, dw_in, pc_send, pc_in,
    x1v, branchv, ffnv, dh2v, dx1v, dwv, dmod, dsend, dbuf,
    tok_send, tok_recv, tok_loc, w_send, w_recv, w_loc, wh_sem, act_sem, mod_s, mod_r,
    at_s, at_r, do_s, do_r, dq_s, dq_r, dw_sem, pc_s, pc_r, dm_s, dm_r, loc,
):
    img, ty, z = lax.axis_index("img"), lax.axis_index("ty"), lax.axis_index("tx")
    b = ty * 4 + z
    me = img * 16 + b
    width = tok.shape[1]
    half = width // 2
    hidden = wup.shape[1] // 2
    part = ada.shape[0]
    other = 1 - img

    def dev(i=img, t=ty, k=z):
        return {"img": i, "ty": t, "tx": k}

    def dev_flat(p):
        return dev(p // 16, lax.rem(p // 4, 4), lax.rem(p, 4))

    def dev_tile(t):
        return dev(img, t // 4, lax.rem(t, 4))

    def rcopy(src, dst, s, r, d):
        return pltpu.make_async_remote_copy(
            src_ref=src, dst_ref=dst, send_sem=s, recv_sem=r, device_id=d, device_id_type=MESH
        )

    def loop(lo, hi, f):
        def step(k, c):
            f(k)
            return c

        lax.fori_loop(lo, hi, step, 0)

    bar = pltpu.get_barrier_semaphore()
    loop(
        1, 32,
        lambda k: pl.semaphore_signal(
            bar, inc=1, device_id=dev_flat(lax.rem(me + k, 32)), device_id_type=MESH
        ),
    )
    pl.semaphore_wait(bar, 31)

    hbm = (wout, wup, wdown, wqkv)
    vm = (woutv, wupv, wdownv, qkv_hbm)
    chunks = weight_chunks(width, hidden)

    def wregion(i, owner, p):
        m, c0, cn = chunks[i]
        rows = hbm[m].shape[0]
        return vm[m].at[pl.ds(owner * rows + p * (rows // 4), rows // 4), pl.ds(c0, cn)]

    def w_x(i):
        m, c0, cn = chunks[i]
        piece = hbm[m].shape[0] // 4
        return rcopy(
            hbm[m].at[pl.ds(ty * piece, piece), pl.ds(c0, cn)],
            wregion(i, img, ty), w_send.at[i, 0], w_recv.at[i, ty], dev(i=other),
        )

    def w_y(i):
        ref = wregion(i, other, ty)
        return rcopy(ref, ref, w_send.at[i, 1], w_recv.at[i, ty], dev(t=ty ^ 2))

    def w_c(i, p, slot):
        ref = wregion(i, other, p)
        return rcopy(ref, ref, w_send.at[i, slot], w_recv.at[i, p], dev(t=ty ^ 1))

    def w_wait(i, p):
        ref = wregion(i, other, p)
        rcopy(ref, ref, w_send.at[i, 0], w_recv.at[i, p], dev(t=ty ^ 1)).wait_recv()

    def x_arrived(i):
        w_wait(i, ty)
        w_y(i).start()
        w_c(i, ty, 2).start()

    def y_arrived(i):
        w_wait(i, ty ^ 2)
        w_c(i, ty ^ 2, 3).start()

    def w_done(i):
        w_wait(i, ty ^ 1)
        w_wait(i, ty ^ 3)

    def w_drain(i):
        w_x(i).wait_send()
        w_y(i).wait_send()
        w_c(i, ty, 2).wait_send()
        w_c(i, ty ^ 2, 3).wait_send()

    def own(m):
        rows = hbm[m].shape[0]
        return pltpu.make_async_copy(hbm[m], vm[m].at[pl.ds(img * rows, rows)], w_loc.at[m])

    act_copy = rcopy(act, actbuf.at[img], act_sem.at[0], act_sem.at[1], dev(i=other))
    act_copy.start()
    actbuf[img] = act[...]
    wh_copy = rcopy(wh, whv.at[pl.ds(img * half, half)], wh_sem.at[0], wh_sem.at[1], dev(i=other))
    wh_copy.start()
    whv[pl.ds(pl.multiple_of(img * half, 64), half), :] = wh[...]

    def t_send(src, chunk, way, d):
        return rcopy(src, tok_all.at[chunk], tok_send.at[chunk, way], tok_recv.at[chunk], d)

    def t_wait(chunk):
        t_send(tok, chunk, 0, dev(t=ty ^ 1)).wait_recv()

    tok_own = pltpu.make_async_copy(tok, tok_all.at[b], tok_loc)
    tok_own.start()

    def t_forward(src, chunk, up, down):
        if up:

            @pl.when(z < 3)
            def _():
                t_send(src, chunk, 0, dev(k=z + 1)).start()

        if down:

            @pl.when(z > 0)
            def _():
                t_send(src, chunk, 1, dev(k=z - 1)).start()

        t_send(src, chunk, 2, dev(t=ty ^ 2)).start()
        t_send(src, chunk, 3, dev(t=ty ^ 1)).start()

    t_forward(tok, b, True, True)
    for m in range(4):
        own(m).start()
    for i in range(9):
        w_x(i).start()

    act_copy.wait_recv()
    for i in range(2):
        modsend[i, :, 0:part] = dot_nt(actbuf[i].astype(BF16), ada[...])

    def mod_copy(p):
        return rcopy(modsend.at[p // 16], modbuf.at[me], mod_s.at[p], mod_r.at[me], dev_flat(p))

    loop(1, 32, lambda k: mod_copy(lax.rem(me + k, 32)).start())
    modbuf[me] = modsend[img]

    for s in (1, 2, 3):

        @pl.when(z - s >= 0)
        def _():
            t_wait(b - s)
            t_forward(tok_all.at[b - s], b - s, True, False)

        @pl.when(z + s <= 3)
        def _():
            t_wait(b + s)
            t_forward(tok_all.at[b + s], b + s, False, True)

    def t_y(zz):
        chunk = (ty ^ 2) * 4 + zz
        t_wait(chunk)
        t_send(tok_all.at[chunk], chunk, 3, dev(t=ty ^ 1)).start()

    loop(0, 4, t_y)
    x_arrived(0)
    for i in range(1, 5):
        x_arrived(i)
    w_x(9).start()
    loop(0, 4, lambda zz: t_wait((ty ^ 1) * 4 + zz))
    loop(0, 4, lambda zz: t_wait((ty ^ 3) * 4 + zz))

    def t_drain(zz):
        chunk = ty * 4 + zz
        ref = tok_all.at[chunk]

        @pl.when((zz <= z) & (z < 3))
        def _():
            t_send(ref, chunk, 0, dev(t=ty ^ 1)).wait_send()

        @pl.when((zz >= z) & (z > 0))
        def _():
            t_send(ref, chunk, 1, dev(t=ty ^ 1)).wait_send()

        t_send(ref, chunk, 2, dev(t=ty ^ 1)).wait_send()
        t_send(ref, chunk, 3, dev(t=ty ^ 1)).wait_send()
        away = (ty ^ 2) * 4 + zz
        t_send(tok_all.at[away], away, 3, dev(t=ty ^ 1)).wait_send()

    loop(0, 4, t_drain)
    tok_own.wait()

    def mod_wait(k):
        p = lax.rem(me + k, 32)
        rcopy(
            modsend.at[0], modbuf.at[p], mod_s.at[p], mod_r.at[p], dev_flat(p)
        ).wait()

    loop(1, 32, mod_wait)
    for s in range(32):
        modv[:, s * part : (s + 1) * part] = modbuf[s, :, 0:part]
    shift1, scale1, gate1, shift2, scale2, gate2 = [
        functools.partial(lambda k: modv[0:1, k * width : (k + 1) * width], k) for k in range(6)
    ]
    wh_copy.wait()

    height, wide = hw[0], hw[1]
    local = lax.broadcasted_iota(jnp.int32, (TILE, PAD), 0)
    lane = lax.broadcasted_iota(jnp.int32, (TILE, PAD), 1)

    def tile_layout(t):
        row_tile, col_tile = t // 4, lax.rem(t, 4)
        top = row_tile * height // 4
        rows = (row_tile + 1) * height // 4 - top
        left = col_tile * wide // 4
        span = (col_tile + 1) * wide // 4 - left
        spans = jnp.full((TILE, PAD), span, jnp.int32)
        quot = jnp.floor((local.astype(F32) + 0.5) / spans.astype(F32)).astype(jnp.int32)
        valid = local < jnp.full((TILE, PAD), rows * span, jnp.int32)
        row = jnp.where(valid, top + quot, 0)
        col = jnp.where(valid, left + local - quot * spans, 0)
        return valid, row, col

    def rope(n, c, s1, s2):
        return n * c + pltpu.roll(n, PAD - 18, 1) * s1 + pltpu.roll(n, 18, 1) * s2

    def unrope(d, c, s1, s2):
        return d * c + pltpu.roll(d * s1, 18, 1) + pltpu.roll(d * s2, PAD - 18, 1)

    def split_sin(sine):
        first = (lane < 18) | ((lane >= 36) & (lane < 54))
        return jnp.where(first, -sine, 0.0), jnp.where(first, 0.0, sine)

    def head_rows(t):
        valid, row, col = tile_layout(t)
        hot = jnp.where((lane == row) | (lane - 64 == col), 1.0, 0.0)
        angles = lax.dot_general(
            hot, tab[...], (((1,), (0,)), ((), ())),
            precision=HIGH, preferred_element_type=F32,
        )
        c, sine = angles[:, 0:PAD], angles[:, PAD : 2 * PAD]
        cosv[t] = c
        sinv[t] = sine
        s1, s2 = split_sin(sine)
        x = tok_all[t].astype(F32)
        r = lax.rsqrt(jnp.mean(x * x, axis=1, keepdims=True) + EPS)
        h1 = ((x * r) * (1.0 + scale1()) + shift1()).astype(BF16)
        tok_all[t] = h1
        qkv = dot(h1, whv[...])
        q_r, k_r, v_r = qkv[:, 0:PAD], qkv[:, PAD : 2 * PAD], qkv[:, 2 * PAD : 3 * PAD]
        qraw[t] = q_r
        kraw[t] = k_r

        def normed(v, gain):
            rr = lax.rsqrt(jnp.sum(v * v, axis=1, keepdims=True) * (1.0 / HEAD) + EPS)
            return v * rr * gain[0:1, :]

        q_f = rope(normed(q_r, q_gain), c, s1, s2) * HEAD ** (-0.5)
        k_f = rope(normed(k_r, k_gain), c, s1, s2)
        qa[t] = jnp.where(lane == HEAD, 1.0, q_f).astype(BF16)
        k_f = jnp.where(lane == HEAD, jnp.where(valid, 0.0, -30000.0), k_f)
        k_f = jnp.where((lane > HEAD) & (lane < HEAD + 4), 1.0, k_f)
        ka[t] = k_f.astype(BF16)
        kt[:, pl.ds(pl.multiple_of(t * TILE, TILE), TILE)] = k_f.T.astype(BF16)
        va[t] = jnp.where((lane >= HEAD) & (lane < HEAD + 3), 1.0, v_r).astype(BF16)

    loop(0, 16, head_rows)
    for i in range(5, 9):
        x_arrived(i)
    y_arrived(0)

    def at_copy(t):
        return rcopy(attn_send.at[t], attn_in.at[b], at_s.at[t], at_r.at[b], dev_tile(t))

    def attend(k):
        q2 = qa[pl.ds(2 * k, 2)].reshape(2 * TILE, PAD)
        p = jnp.exp(dot(q2, kt[...])).astype(BF16)
        o = dot(p, va[...].reshape(16 * TILE, PAD))
        total = o[:, HEAD : HEAD + 1]
        o = o / total
        lse = jnp.log(total)
        q3 = put_split3(q2.astype(F32), -lse, HEAD + 1)
        o16 = o.astype(BF16)
        for u in range(2):
            t = 2 * k + u
            rows = slice(u * TILE, (u + 1) * TILE)
            onorm[t] = o[rows]
            qa[t] = q3[rows].astype(BF16)
            qt[:, pl.ds(pl.multiple_of(t * TILE, TILE), TILE)] = q3[rows].T.astype(BF16)
            attn_send[t] = o16[rows]

            @pl.when(t != b)
            def _():
                at_copy(t).start()

    loop(0, 8, attend)
    attn_in[b] = attn_send[b]
    for i in range(1, 5):
        y_arrived(i)
    x_arrived(9)
    w_x(10).start()
    for i in range(5, 9):
        y_arrived(i)

    def at_wait(k):
        p = lax.rem(b + k, 16)
        rcopy(attn_send.at[p], attn_in.at[p], at_s.at[p], at_r.at[p], dev_tile(p)).wait()

    loop(1, 16, at_wait)

    attn = jnp.concatenate(
        [attn_in[h].astype(F32)[:, 0:HEAD] for h in range(16)], axis=1
    ).astype(BF16)
    l_attn[...] = attn
    own(OUT).wait()
    w_done(0)
    own_valid = tile_layout(b)[0]
    keep = jnp.where(own_valid, 1.0, 0.0)[:, 0:1]
    cols = width // 3

    def project(k):
        at = pl.ds(pl.multiple_of(k * cols, PAD), cols)
        branchv[:, at] = dot(l_attn[...], woutv[:, at])

    loop(0, 3, project)
    x = tok[...].astype(F32)
    x1 = x + keep * gate1() * branchv[...]
    x1v[...] = x1
    r = lax.rsqrt(jnp.mean(x1 * x1, axis=1, keepdims=True) + EPS)
    l_h2[...] = ((x1 * r) * (1.0 + scale2()) + shift2()).astype(BF16)
    r_ffn[...] = (cot[...].astype(F32) * keep * gate2()).astype(BF16)
    ffnv[...] = jnp.zeros_like(ffnv)
    dh2v[...] = jnp.zeros_like(dh2v)
    y_arrived(9)
    for i in range(1, 10):
        w_done(i)
    own(UP).wait()
    own(DOWN).wait()
    step = 256

    def mlp(j):
        g_at = pl.ds(pl.multiple_of(j * step, step), step)
        u_at = pl.ds(pl.multiple_of(hidden + j * step, step), step)
        h2 = l_h2[...]
        gate = dot(h2, wupv[:, g_at])
        up = dot(h2, wupv[:, u_at])
        sig = 1.0 / (1.0 + jnp.exp(-gate))
        act_g = gate * sig
        mid = (act_g * up).astype(BF16)
        l_mid[:, g_at] = mid
        w3 = wdownv[g_at, :]
        ffnv[...] += dot(mid, w3)
        d_mid = dot_nt(r_ffn[...], w3)
        d_gate = (d_mid * up * (sig + gate * sig * (1.0 - sig))).astype(BF16)
        d_up = (d_mid * act_g).astype(BF16)
        r_gu[:, g_at] = d_gate
        r_gu[:, u_at] = d_up
        dh2v[...] += dot_nt(d_gate, wupv[:, g_at]) + dot_nt(d_up, wupv[:, u_at])

    loop(0, hidden // step, mlp)
    x_arrived(10)
    ffn = ffnv[...]
    g = cot[...].astype(F32)
    x1 = x1v[...]
    mixed[...] = (x1 + keep * gate2() * ffn).astype(BF16)

    def dmod_put(k, row):
        dmod[0:1, k * width : (k + 1) * width] = row

    def colsum(v):
        return jnp.sum(v, axis=0, keepdims=True)

    dmod_put(5, colsum(g * keep * ffn))
    d_h2 = dh2v[...]
    norm2 = x1 * r
    dmod_put(4, colsum(d_h2 * norm2))
    dmod_put(3, colsum(d_h2))
    d_n2 = d_h2 * (1.0 + scale2())
    d_x1 = g + r * (d_n2 - norm2 * jnp.mean(d_n2 * norm2, axis=1, keepdims=True))
    dx1v[...] = d_x1
    dmod_put(2, colsum(d_x1 * keep * branchv[...]))
    r_branch[...] = (d_x1 * keep * gate1()).astype(BF16)

    def unproject(k):
        at = pl.ds(pl.multiple_of(k * cols, PAD), cols)
        branchv[:, at] = dot_nt(r_branch[...], woutv[at, :])

    loop(0, 3, unproject)

    zeros = jnp.zeros((TILE, PAD - HEAD), F32)
    d_attn = branchv[...]
    for h in range(16):
        attn_send[h] = jnp.concatenate(
            [d_attn[:, h * HEAD : (h + 1) * HEAD], zeros], axis=1
        ).astype(BF16)

    def do_copy(t):
        return rcopy(attn_send.at[t], do_in.at[b], do_s.at[t], do_r.at[b], dev_tile(t))

    loop(1, 16, lambda k: do_copy(lax.rem(b + k, 16)).start())
    do_in[b] = attn_send[b]
    y_arrived(10)
    own(QKV).wait()

    def do_wait(k):
        p = lax.rem(b + k, 16)
        rcopy(attn_send.at[p], do_in.at[p], do_s.at[p], do_r.at[p], dev_tile(p)).wait()

    loop(1, 16, do_wait)

    def delta(t):
        d = do_in[t].astype(F32)
        dsum = jnp.sum(jnp.where(lane < HEAD, d * onorm[t], 0.0), axis=1, keepdims=True)
        d = put_split3(d, -dsum, HEAD)
        do_in[t] = d.astype(BF16)
        dot_t[:, pl.ds(pl.multiple_of(t * TILE, TILE), TILE)] = d.T.astype(BF16)

    loop(0, 16, delta)
    dqt[...] = jnp.zeros_like(dqt)

    def attend_back(k):
        two = pl.ds(2 * k, 2)
        p = jnp.exp(dot(ka[two].reshape(2 * TILE, PAD), qt[...]))
        ds = (p * dot(va[two].reshape(2 * TILE, PAD), dot_t[...])).astype(BF16)
        dkv[two] = dot(ds, qa[...].reshape(16 * TILE, PAD)).reshape(2, TILE, PAD)
        dvv[two] = dot(p.astype(BF16), do_in[...].reshape(16 * TILE, PAD)).reshape(2, TILE, PAD)
        at = pl.ds(pl.multiple_of(k * 2 * TILE, 2 * TILE), 2 * TILE)
        dqt[...] += dot(kt[:, at], ds)

    loop(0, 8, attend_back)

    for i in range(11):
        w_drain(i)
    gain_grad[...] = jnp.zeros_like(gain_grad)

    def dq_copy(t):
        return rcopy(dqkv_send.at[t], dqkv_in.at[b], dq_s.at[t], dq_r.at[b], dev_tile(t))

    def heads_back(t):
        c = cosv[t]
        s1, s2 = split_sin(sinv[t])

        def norm_back(d, v, gain, row):
            rr = lax.rsqrt(jnp.sum(v * v, axis=1, keepdims=True) * (1.0 / HEAD) + EPS)
            n = v * rr
            gain_grad[row : row + 1, :] += colsum(d * n)
            dn = d * gain[0:1, :]
            return rr * (dn - n * (jnp.sum(dn * n, axis=1, keepdims=True) * (1.0 / HEAD)))

        d_q = dqt[:, pl.ds(pl.multiple_of(t * TILE, TILE), TILE)].T * HEAD ** (-0.5)
        d_q = norm_back(unrope(d_q, c, s1, s2), qraw[t], q_gain, 0)
        d_k = norm_back(unrope(dkv[t], c, s1, s2), kraw[t], k_gain, 1)
        d_v = jnp.where(lane < HEAD, dvv[t], 0.0)
        at = pl.ds(pl.multiple_of(t * TILE, TILE), TILE)
        wdownv[at, 0 : 3 * PAD] = jnp.concatenate([d_q, d_k, d_v], axis=1).astype(BF16)
        dqkv_send[t] = jnp.concatenate(
            [d_q[:, 0:HEAD], d_k[:, 0:HEAD], d_v[:, 0:HEAD], zeros[:, 0:40]], axis=1
        ).astype(BF16)

        @pl.when(t != b)
        def _():
            dq_copy(t).start()

    loop(0, 16, heads_back)
    dqkv_in[b] = dqkv_send[b]

    dwv[...] = jnp.zeros_like(dwv)

    def dw_rows(k):
        two = pl.ds(2 * k, 2)
        at = pl.ds(pl.multiple_of(k * 2 * TILE, TILE), 2 * TILE)
        dwv[...] += dot_tn(wdownv[at, 0 : 3 * PAD], tok_all[two].reshape(2 * TILE, width))

    loop(0, 8, dw_rows)
    dw = dwv[...].T
    dw_send[0] = dw[0:half].astype(BF16)
    dw_send[1] = dw[half : 2 * half].astype(BF16)
    dw_copy = rcopy(dw_send.at[other], dw_in, dw_sem.at[0], dw_sem.at[1], dev(i=other))
    dw_copy.start()
    w_done(10)

    load = pltpu.make_async_copy(qkv_hbm, wupv.at[:, pl.ds(0, 3 * width)], loc)
    load.start()

    def dq_wait(k):
        p = lax.rem(b + k, 16)
        rcopy(dqkv_send.at[p], dqkv_in.at[p], dq_s.at[p], dq_r.at[p], dev_tile(p)).wait()

    loop(1, 16, dq_wait)
    dw_copy.wait()
    dw_sum = dw_send[img].astype(F32) + dw_in[...].astype(F32)
    for p in range(3):
        pc_send[p] = dw_sum[:, p * PAD : (p + 1) * PAD].astype(BF16)

    def pc_copy(p):
        group = 16 * p + b
        to, slot = group // 3, lax.rem(group, 3)
        return to, rcopy(
            pc_send.at[p], pc_in.at[slot], pc_s.at[p], pc_r.at[slot], dev_tile(to)
        )

    for p in range(3):
        to, copy = pc_copy(p)

        @pl.when(to != b)
        def _():
            copy.start()

        @pl.when(to == b)
        def _():
            pc_in[lax.rem(16 * p + b, 3)] = pc_send[p]

    load.wait()
    dqkv = [dqkv_in[h].astype(F32) for h in range(16)]
    def own_part(p):
        return slice(16 * TILE + p * TILE, 16 * TILE + (p + 1) * TILE)

    for p in range(3):
        wdownv[own_part(p), :] = jnp.concatenate(
            [dqkv[h][:, p * HEAD : (p + 1) * HEAD] for h in range(16)], axis=1
        ).astype(BF16)

    def h1_back(k):
        at = pl.ds(pl.multiple_of(k * cols, PAD), cols)
        dh2v[:, at] = sum(
            dot_nt(wdownv[own_part(p), :], wupv[at, p * width : (p + 1) * width])
            for p in range(3)
        )

    loop(0, 3, h1_back)
    d_h1 = dh2v[...]
    x = tok[...].astype(F32)
    r1 = lax.rsqrt(jnp.mean(x * x, axis=1, keepdims=True) + EPS)
    norm1 = x * r1
    dmod_put(1, colsum(d_h1 * norm1))
    dmod_put(0, colsum(d_h1))
    d_n1 = d_h1 * (1.0 + scale1())
    back = r1 * (d_n1 - norm1 * jnp.mean(d_n1 * norm1, axis=1, keepdims=True))
    tgrad[...] = (dx1v[...] + back).astype(BF16)

    dsend[...] = jnp.zeros_like(dsend)
    for s in range(32):
        dsend[s, 0:1, 0:part] = dmod[0:1, s * part : (s + 1) * part]
        dsend[s, 1:3, 0:PAD] = gain_grad[0:2, :]

    def dm_copy(p):
        return rcopy(dsend.at[p], dbuf.at[me], dm_s.at[p], dm_r.at[me], dev_flat(p))

    loop(1, 32, lambda k: dm_copy(lax.rem(me + k, 32)).start())
    dbuf[me] = dsend[me]

    for slot in range(3):
        group = 3 * b + slot
        src = lax.rem(group, 16)

        @pl.when(src != b)
        def _():
            rcopy(
                pc_send.at[0], pc_in.at[slot], pc_s.at[0], pc_r.at[slot], dev_tile(src)
            ).wait_recv()

    qkv_grad[...] = jnp.concatenate(
        [pc_in[slot].astype(F32)[:, 0:HEAD] for slot in range(3)], axis=1
    )
    for p in range(3):
        to, copy = pc_copy(p)

        @pl.when(to != b)
        def _():
            copy.wait_send()

    def dm_wait(k):
        p = lax.rem(me + k, 32)
        rcopy(dsend.at[p], dbuf.at[p], dm_s.at[p], dm_r.at[p], dev_flat(p)).wait()

    loop(1, 32, dm_wait)
    sums = [
        lax.fori_loop(1, 16, lambda s, a, i=i: a + dbuf[16 * i + s], dbuf[16 * i])
        for i in range(2)
    ]
    gain_grad[...] = jnp.where(
        lax.broadcasted_iota(jnp.int32, (8, PAD), 0) < 2,
        pltpu.roll(sums[0] + sums[1], 7, 0)[:, 0:PAD],
        0.0,
    )
    row = lax.broadcasted_iota(jnp.int32, (8, 2 * PAD), 0)
    d_two = jnp.where(row == 0, sums[0][0:1, :], jnp.where(row == 1, sums[1][0:1, :], 0.0))
    row = lax.broadcasted_iota(jnp.int32, (8, width), 0)
    a_two = jnp.where(row == 0, actbuf[0], jnp.where(row == 1, actbuf[1], 0.0))
    ada_grad[...] = dot_tn(d_two, a_two, HIGH)[0:part, :]
    act_copy.wait_send()


def rope_table():
    table = np.zeros((PAD, 2 * PAD), np.float64)
    angle = np.arange(64)[:, None] * 10000.0 ** (-np.arange(18) / 18)
    for axis in range(2):
        rows = slice(64 * axis, 64 * axis + 64)
        for quarter in range(2):
            at = 36 * axis + 18 * quarter
            table[rows, at : at + 18] = np.cos(angle)
            table[rows, PAD + at : PAD + at + 18] = np.sin(angle)
    return table.astype(np.float32)


def run_block(tokens, cotangent, act, ada, wh, wout, wup, wdown, wqkv, q_gain, k_gain, hw):
    width, hidden = tokens.shape[1], wup.shape[1] // 2
    half, part = width // 2, ada.shape[0]
    vmem, any_ = pl.BlockSpec(memory_space=pltpu.VMEM), pl.BlockSpec(memory_space=pl.ANY)
    smem = pl.BlockSpec(memory_space=pltpu.SMEM)
    sds = jax.ShapeDtypeStruct
    v, dma = pltpu.VMEM, pltpu.SemaphoreType.DMA
    n_chunks = len(weight_chunks(width, hidden))
    tile16 = (16, TILE, PAD)
    out_shape = (
        sds((TILE, width), BF16),
        sds((TILE, width), BF16),
        sds((TILE, width), BF16),
        sds((TILE, width), BF16),
        sds((TILE, hidden), BF16),
        sds((TILE, width), BF16),
        sds((TILE, width), BF16),
        sds((TILE, 2 * hidden), BF16),
        sds((half, 3 * HEAD), F32),
        sds((part, width), F32),
        sds((8, PAD), F32),
        sds((width, 3 * width), BF16),
    )
    scratch = [
        v((16, TILE, width), BF16),
        v((width, 3 * PAD), BF16),
        v((width, width), BF16),
        v((width, 2 * hidden), BF16),
        v((hidden, width), BF16),
        v((2, 8, width), F32),
        v((2, 8, 2 * PAD), F32),
        v((32, 8, 2 * PAD), F32),
        v((8, 6 * width), F32),
        v(tile16, F32),
        v(tile16, F32),
        v(tile16, F32),
        v(tile16, F32),
        v(tile16, BF16),
        v(tile16, BF16),
        v(tile16, BF16),
        v((PAD, 16 * TILE), BF16),
        v((PAD, 16 * TILE), BF16),
        v(tile16, F32),
        v(tile16, BF16),
        v(tile16, BF16),
        v(tile16, BF16),
        v((PAD, 16 * TILE), BF16),
        v((PAD, 16 * TILE), F32),
        v(tile16, F32),
        v(tile16, F32),
        v((16, TILE, 2 * PAD), BF16),
        v((16, TILE, 2 * PAD), BF16),
        v((2, half, 3 * PAD), BF16),
        v((half, 3 * PAD), BF16),
        v((3, half, PAD), BF16),
        v((3, half, PAD), BF16),
        v((TILE, width), F32),
        v((TILE, width), F32),
        v((TILE, width), F32),
        v((TILE, width), F32),
        v((TILE, width), F32),
        v((3 * PAD, width), F32),
        v((8, 6 * width), F32),
        v((32, 8, 2 * PAD), F32),
        v((32, 8, 2 * PAD), F32),
        dma((16, 4)),
        dma((16,)),
        dma,
        dma((n_chunks, 4)),
        dma((n_chunks, 4)),
        dma((4,)),
        dma((2,)),
        dma((2,)),
        dma((32,)),
        dma((32,)),
        dma((16,)),
        dma((16,)),
        dma((16,)),
        dma((16,)),
        dma((16,)),
        dma((16,)),
        dma((2,)),
        dma((3,)),
        dma((3,)),
        dma((32,)),
        dma((32,)),
        dma,
    ]
    return pl.pallas_call(
        block_kernel,
        out_shape=out_shape,
        in_specs=[vmem] * 5 + [any_] * 4 + [vmem] * 3 + [smem],
        out_specs=[vmem] * 11 + [any_],
        scratch_shapes=scratch,
        compiler_params=pltpu.CompilerParams(
            collective_id=0, has_side_effects=True, vmem_limit_bytes=VMEM_LIMIT
        ),
    )(tokens, cotangent, act, ada, wh, wout, wup, wdown, wqkv, q_gain, k_gain, rope_table(), hw)


def swap(value, axis, bit):
    n = lax.axis_size(axis)
    return lax.ppermute(value, axis, [(i, i ^ bit) for i in range(n)])


def pick(value, index, axis):
    return lax.dynamic_index_in_dim(value, index, axis, keepdims=False)


def plane_grad(left, right):
    img, ty, z = lax.axis_index("img"), lax.axis_index("ty"), lax.axis_index("tx")
    rows, kl = left.shape
    n = right.shape[1]
    halves = left.reshape(rows, 2, kl // 2)
    l2 = jnp.concatenate([pick(halves, img, 1), swap(pick(halves, 1 - img, 1), "img", 1)])
    l4 = jnp.concatenate([l2, swap(l2, "ty", 2)])
    l8 = jnp.concatenate([l4, swap(l4, "ty", 1)])
    quarters = right.reshape(rows, 2, 2, n // 4)
    y, c = ty // 2, ty % 2
    mine = pick(quarters, y, 1)
    theirs = swap(pick(quarters, 1 - y, 1), "ty", 2)
    across = swap(jnp.stack([mine, theirs]), "img", 1)
    r4 = jnp.concatenate([mine, across[0], theirs, across[1]])
    r8 = jnp.concatenate([pick(r4, c, 1), swap(pick(r4, 1 - c, 1), "ty", 1)])
    part = outer_sum(l8, r8).reshape(kl // 2, 2, 2, n // 16)
    high, low = z // 2, z % 2
    sent = swap(pick(part, 1 - low, 2).astype(jnp.bfloat16), "tx", 1)
    part = pick(part, low, 2) + sent.astype(jnp.float32)
    sent = swap(pick(part, 1 - high, 1).astype(jnp.bfloat16), "tx", 2)
    return pick(part, high, 1) + sent.astype(jnp.float32)


def head_weight(weight):
    at = lax.axis_index(("ty", "tx")) * HEAD
    width = weight.shape[1] // 3
    parts = [
        lax.dynamic_slice_in_dim(weight, p * width + at, HEAD, axis=1) for p in range(3)
    ]
    return jnp.concatenate([jnp.pad(p, ((0, 0), (0, PAD - HEAD))) for p in parts], axis=1)


def fast_body(
    tokens,
    cotangent,
    class_embed,
    timestep,
    grid_height,
    grid_width,
    qkv_weight,
    out_weight,
    up_weight,
    down_weight,
    ada_weight,
    q_gain,
    k_gain,
):
    width = tokens.shape[2]
    act = jax.nn.silu(class_embed + time_embed(timestep, width)).astype(BF16).astype(F32)
    pad = lambda g: jnp.broadcast_to(jnp.pad(g, (0, PAD - HEAD))[None], (8, PAD))
    (mixed, tgrad, l_attn, l_h2, l_mid, r_ffn, r_branch, r_gu, qkv_grad, ada_grad, gains, _) = (
        run_block(
            tokens[0],
            cotangent[0],
            jnp.broadcast_to(act, (8, width)),
            ada_weight,
            head_weight(qkv_weight),
            out_weight,
            up_weight,
            down_weight,
            qkv_weight,
            pad(q_gain),
            pad(k_gain),
            jnp.concatenate([grid_height, grid_width]),
        )
    )
    down_grad = plane_grad(l_mid, r_ffn)
    up_grad = plane_grad(l_h2, r_gu)
    out_grad = plane_grad(l_attn, r_branch)
    return (
        mixed[None],
        tgrad[None],
        qkv_grad,
        out_grad,
        up_grad,
        down_grad,
        ada_grad,
        gains[0, :HEAD],
        gains[1, :HEAD],
    )


def solution(mesh):
    in_specs = (
        P("img", ("ty", "tx"), None),
        P("img", ("ty", "tx"), None),
        P("img", None),
        P("img"),
        P("img"),
        P("img"),
        P("img", None),
        P("img", None),
        P("img", None),
        P("img", None),
        P(("img", "ty", "tx"), None),
        P(),
        P(),
    )
    out_specs = (
        P("img", ("ty", "tx"), None),
        P("img", ("ty", "tx"), None),
        P("img", ("ty", "tx")),
        P("img", ("ty", "tx")),
        P("img", ("ty", "tx")),
        P("img", ("ty", "tx")),
        P(("img", "ty", "tx"), None),
        P(),
        P(),
    )
    shape = dict(mesh.shape)
    fast = (shape["img"], shape["ty"], shape["tx"]) == (2, 4, 4)
    body = fast_body if fast else general_body
    return jax.shard_map(body, mesh=mesh, in_specs=in_specs, out_specs=out_specs, check_vma=False)
```

```python
import functools

import jax
import jax.numpy as jnp
import numpy as np
from jax import lax
from jax.experimental import pallas as pl
from jax.experimental.pallas import tpu as pltpu
from jax.sharding import PartitionSpec as P

HEADS = 16
HEAD = 72


EPS = 1e-06
HIGH = lax.Precision.HIGHEST


def layout(slot, height, width, cap, rows_tiles, cols_tiles):
    tile = slot // cap
    row_tile = tile // cols_tiles
    col_tile = tile % cols_tiles
    local = slot % cap
    top = row_tile * height // rows_tiles
    bottom = (row_tile + 1) * height // rows_tiles
    left = col_tile * width // cols_tiles
    right = (col_tile + 1) * width // cols_tiles
    span = right - left
    valid = local < (bottom - top) * span
    row = jnp.where(valid, top + local // span, 0)
    col = jnp.where(valid, left + local % span, 0)
    return (valid, row, col)


def time_embed(step, dim):
    half = dim // 2
    freq = jnp.exp(-jnp.log(10000.0) * jnp.arange(half, dtype=jnp.float32) / half)
    angle = step.astype(jnp.float32)[:, None] * freq
    return jnp.concatenate([jnp.cos(angle), jnp.sin(angle)], axis=-1)


def rotate(part, position):
    quarter = part.shape[-1] // 2
    freq = jnp.exp(-jnp.log(10000.0) * jnp.arange(quarter, dtype=jnp.float32) / quarter)
    angle = position.astype(jnp.float32)[..., None, None] * freq
    first, second = (part[..., :quarter], part[..., quarter:])
    cosine, sine = (jnp.cos(angle), jnp.sin(angle))
    return jnp.concatenate(
        [first * cosine - second * sine, second * cosine + first * sine], axis=-1
    )


def rope(heads, row, col):
    half = heads.shape[-1] // 2
    return jnp.concatenate(
        [rotate(heads[..., :half], row), rotate(heads[..., half:], col)], axis=-1
    )


def head_norm(value, gain):
    return value * lax.rsqrt(jnp.mean(value * value, axis=-1, keepdims=True) + EPS) * gain


def rms(value):
    return value * lax.rsqrt(jnp.mean(value * value, axis=-1, keepdims=True) + EPS)


def flat_rows(value):
    return value.reshape(-1, value.shape[-1])


def outer_sum(left, right):
    return lax.dot_general(
        flat_rows(left),
        flat_rows(right),
        (((0,), (0,)), ((), ())),
        preferred_element_type=jnp.float32,
    )


def times_transposed(left, weight):
    return lax.dot_general(
        left, weight, (((left.ndim - 1,), (1,)), ((), ())), preferred_element_type=jnp.float32
    )


def masked_scores(query, keys_all, key_valid):
    scores = jnp.einsum("qhd,khd->hqk", query, keys_all, preferred_element_type=jnp.float32)
    return jnp.where(key_valid[None, None, :], scores, -1e30)


def general_body(
    tokens,
    cotangent,
    class_embed,
    timestep,
    grid_height,
    grid_width,
    qkv_weight,
    out_weight,
    up_weight,
    down_weight,
    ada_weight,
    q_gain,
    k_gain,
):
    images, slots_dev, width = tokens.shape
    rows_tiles = lax.axis_size("ty")
    cols_tiles = lax.axis_size("tx")
    slots_all = slots_dev * rows_tiles * cols_tiles
    own_slot = lax.axis_index(("ty", "tx")) * slots_dev + jnp.arange(slots_dev, dtype=jnp.int32)
    all_slot = jnp.arange(slots_all, dtype=jnp.int32)
    valid_q, row_q, col_q = jax.vmap(
        lambda h, w: layout(own_slot, h, w, slots_dev, rows_tiles, cols_tiles)
    )(grid_height, grid_width)
    valid_k = jax.vmap(lambda h, w: layout(all_slot, h, w, slots_dev, rows_tiles, cols_tiles)[0])(
        grid_height, grid_width
    )
    keep = valid_q.astype(jnp.float32)[..., None]
    act = jax.nn.silu(class_embed + time_embed(timestep, width)).astype(jnp.bfloat16)
    mod = lax.dot_general(
        act,
        lax.all_gather(ada_weight, ("img", "ty", "tx"), axis=0, tiled=True),
        (((1,), (1,)), ((), ())),
        preferred_element_type=jnp.float32,
    )
    shift1, scale1, gate1, shift2, scale2, gate2 = [
        part[:, None, :] for part in jnp.split(mod, 6, axis=1)
    ]
    wqkv, wout, w12, w3 = (
        lax.all_gather(qkv_weight, "img", axis=0, tiled=True),
        lax.all_gather(out_weight, "img", axis=0, tiled=True),
        lax.all_gather(up_weight, "img", axis=0, tiled=True),
        lax.all_gather(down_weight, "img", axis=0, tiled=True),
    )
    xf = tokens.astype(jnp.float32)
    norm1, pull_norm1 = jax.vjp(rms, xf)
    h1 = (norm1 * (1.0 + scale1) + shift1).astype(jnp.bfloat16)
    qkv = jnp.dot(h1, wqkv, preferred_element_type=jnp.float32).reshape(
        images, slots_dev, 3, HEADS, HEAD
    )

    def finish(query_raw, key_raw, query_gain, key_gain):
        query = rope(head_norm(query_raw, query_gain), row_q, col_q) * HEAD ** (-0.5)
        return (query, rope(head_norm(key_raw, key_gain), row_q, col_q))

    (query_f, key_f), pull_heads = jax.vjp(finish, qkv[:, :, 0], qkv[:, :, 1], q_gain, k_gain)
    query_b = query_f.astype(jnp.bfloat16)
    key_b = key_f.astype(jnp.bfloat16)
    value_b = qkv[:, :, 2].astype(jnp.bfloat16)
    keys_all, values_all = (
        lax.all_gather(key_b, ("ty", "tx"), axis=1, tiled=True),
        lax.all_gather(value_b, ("ty", "tx"), axis=1, tiled=True),
    )
    index = 0
    scores = masked_scores(query_b[index], keys_all[index], valid_k[index])
    top = jnp.max(scores, axis=-1, keepdims=True)
    lse = top + jnp.log(jnp.sum(jnp.exp(scores - top), axis=-1, keepdims=True))
    prob = jnp.exp(scores - lse).astype(jnp.bfloat16)
    attn_list = [
        jnp.einsum("hqk,khd->qhd", prob, values_all[index], preferred_element_type=jnp.float32)
    ]
    lse_list = [lse]
    attn = jnp.stack(attn_list).reshape(images, slots_dev, width).astype(jnp.bfloat16)
    branch = jnp.dot(attn, wout, preferred_element_type=jnp.float32)
    x1 = xf + keep * gate1 * branch
    norm2, pull_norm2 = jax.vjp(rms, x1)
    h2 = (norm2 * (1.0 + scale2) + shift2).astype(jnp.bfloat16)
    gate_up = jnp.dot(h2, w12, preferred_element_type=jnp.float32)
    hidden = gate_up.shape[-1] // 2
    gate_part, up_part = (gate_up[..., :hidden], gate_up[..., hidden:])
    sig = jax.nn.sigmoid(gate_part)
    silu_gate = gate_part * sig
    mid = (silu_gate * up_part).astype(jnp.bfloat16)
    ffn = jnp.dot(mid, w3, preferred_element_type=jnp.float32)
    mixed = (x1 + keep * gate2 * ffn).astype(jnp.bfloat16)
    grad_out = cotangent.astype(jnp.float32)
    d_gate2 = jnp.sum(grad_out * keep * ffn, axis=1)
    d_ffn = (grad_out * keep * gate2).astype(jnp.bfloat16)
    term_down = outer_sum(mid, d_ffn)
    d_mid = times_transposed(d_ffn, w3)
    d_gate = d_mid * up_part * (sig + gate_part * sig * (1.0 - sig))
    d_up = d_mid * silu_gate
    d_gate_up = jnp.concatenate([d_gate, d_up], axis=-1).astype(jnp.bfloat16)
    term_up = outer_sum(h2, d_gate_up)
    d_h2 = times_transposed(d_gate_up, w12)
    d_scale2 = jnp.sum(d_h2 * norm2, axis=1)
    d_shift2 = jnp.sum(d_h2, axis=1)
    d_x1 = grad_out + pull_norm2(d_h2 * (1.0 + scale2))[0]
    d_gate1 = jnp.sum(d_x1 * keep * branch, axis=1)
    d_branch = (d_x1 * keep * gate1).astype(jnp.bfloat16)
    term_out = outer_sum(attn, d_branch)
    d_attn = (
        times_transposed(d_branch, wout)
        .astype(jnp.bfloat16)
        .reshape(images, slots_dev, HEADS, HEAD)
    )
    keys_back, values_back = (
        lax.all_gather(key_b, ("ty", "tx"), axis=1, tiled=True),
        lax.all_gather(value_b, ("ty", "tx"), axis=1, tiled=True),
    )
    index = 0
    scores = masked_scores(query_b[index], keys_back[index], valid_k[index])
    prob = jnp.exp(scores - lse_list[index])
    d_prob = jnp.einsum(
        "qhd,khd->hqk", d_attn[index], values_back[index], preferred_element_type=jnp.float32
    )
    delta = jnp.sum(prob * d_prob, axis=-1, keepdims=True)
    d_scores = (prob * (d_prob - delta)).astype(jnp.bfloat16)
    dq_list = [
        jnp.einsum("hqk,khd->qhd", d_scores, keys_back[index], preferred_element_type=jnp.float32)
    ]
    dk_list = [
        jnp.einsum("hqk,qhd->khd", d_scores, query_b[index], preferred_element_type=jnp.float32)
    ]
    dv_list = [
        jnp.einsum(
            "hqk,qhd->khd",
            prob.astype(jnp.bfloat16),
            d_attn[index],
            preferred_element_type=jnp.float32,
        )
    ]
    d_key, d_value = (
        lax.psum_scatter(
            jnp.stack(dk_list).astype(jnp.bfloat16), ("ty", "tx"), scatter_dimension=1, tiled=True
        ).astype(jnp.float32),
        lax.psum_scatter(
            jnp.stack(dv_list).astype(jnp.bfloat16), ("ty", "tx"), scatter_dimension=1, tiled=True
        ).astype(jnp.float32),
    )
    d_query_raw, d_key_raw, d_q_gain, d_k_gain = pull_heads((jnp.stack(dq_list), d_key))
    d_qkv = (
        jnp.stack([d_query_raw, d_key_raw, d_value], axis=2)
        .reshape(images, slots_dev, 3 * width)
        .astype(jnp.bfloat16)
    )
    term_qkv = outer_sum(h1, d_qkv)
    d_h1 = times_transposed(d_qkv, wqkv)
    d_scale1 = jnp.sum(d_h1 * norm1, axis=1)
    d_shift1 = jnp.sum(d_h1, axis=1)
    tokens_grad = (d_x1 + pull_norm1(d_h1 * (1.0 + scale1))[0]).astype(jnp.bfloat16)
    d_mod = jnp.concatenate([d_shift1, d_scale1, d_gate1, d_shift2, d_scale2, d_gate2], axis=1)
    act_f = act.astype(jnp.float32)
    ada_grad = lax.psum_scatter(
        lax.dot_general(
            d_mod,
            act_f,
            (((0,), (0,)), ((), ())),
            precision=HIGH,
            preferred_element_type=jnp.float32,
        ),
        ("img", "ty", "tx"),
        scatter_dimension=0,
        tiled=True,
    )
    q_gain_grad, k_gain_grad = lax.psum((d_q_gain, d_k_gain), ("img", "ty", "tx"))
    parts = (
        lax.psum_scatter(
            term_qkv.astype(jnp.bfloat16), ("ty", "tx"), scatter_dimension=1, tiled=True
        ).astype(jnp.float32),
        lax.psum_scatter(
            term_out.astype(jnp.bfloat16), ("ty", "tx"), scatter_dimension=1, tiled=True
        ).astype(jnp.float32),
        lax.psum_scatter(
            term_up.astype(jnp.bfloat16), ("ty", "tx"), scatter_dimension=1, tiled=True
        ).astype(jnp.float32),
        lax.psum_scatter(
            term_down.astype(jnp.bfloat16), ("ty", "tx"), scatter_dimension=1, tiled=True
        ).astype(jnp.float32),
    )
    grads = (
        lax.psum_scatter(
            parts[0].astype(jnp.bfloat16), "img", scatter_dimension=0, tiled=True
        ).astype(jnp.float32),
        lax.psum_scatter(
            parts[1].astype(jnp.bfloat16), "img", scatter_dimension=0, tiled=True
        ).astype(jnp.float32),
        lax.psum_scatter(
            parts[2].astype(jnp.bfloat16), "img", scatter_dimension=0, tiled=True
        ).astype(jnp.float32),
        lax.psum_scatter(
            parts[3].astype(jnp.bfloat16), "img", scatter_dimension=0, tiled=True
        ).astype(jnp.float32),
    )
    return (
        mixed,
        tokens_grad,
        grads[0],
        grads[1],
        grads[2],
        grads[3],
        ada_grad,
        q_gain_grad,
        k_gain_grad,
    )


VMEM_LIMIT = 63 << 20
MESH = pl.DeviceIdType.MESH
PAD = 128
TILE = 128
F32 = jnp.float32
BF16 = jnp.bfloat16


def dot(a, b):
    return lax.dot_general(a, b, (((1,), (0,)), ((), ())), preferred_element_type=F32)


def dot_nt(a, b):
    return lax.dot_general(a, b, (((1,), (1,)), ((), ())), preferred_element_type=F32)


def dot_tn(a, b, precision=None):
    return lax.dot_general(
        a, b, (((0,), (0,)), ((), ())), preferred_element_type=F32, precision=precision
    )


def lanes(shape):
    return lax.broadcasted_iota(jnp.int32, shape, len(shape) - 1)


def split3(value):
    high = value.astype(BF16)
    rest = value - high.astype(F32)
    mid = rest.astype(BF16)
    low = (rest - mid.astype(F32)).astype(BF16)
    return (high, mid, low)


def put_split3(tile, value, lane0):
    at = lanes(tile.shape)
    for k, term in enumerate(split3(value)):
        tile = jnp.where(at == lane0 + k, jnp.broadcast_to(term.astype(F32), tile.shape), tile)
    return tile


OUT, UP, DOWN, QKV = range(4)


def weight_chunks(width, hidden):
    up = []
    step = hidden // 4
    for k in range(4):
        up += [(UP, k * step, step), (UP, hidden + k * step, step)]
    return [(OUT, 0, width)] + up + [(DOWN, 0, width), (QKV, 0, 3 * width)]


def block_kernel(
    tok, cot, act, ada, wh, wout, wup, wdown, wqkv, q_gain, k_gain, tab, hw,
    mixed, tgrad, qkv_grad, ada_grad, gain_grad, down_grad, up_grad, out_grad, qkv_hbm,
    lb_down, lb_up, lb_out, rb_down, rb_up, rb_out,
    tok_all, whv, woutv, wupv, wdownv, actbuf, modsend, modbuf, modv,
    cosv, sinv, qraw, kraw, qa, ka, va, kt, qt, onorm, attn_send, attn_in,
    do_in, dot_t, dqt, dkv, dvv, dqkv_in, dw_in, pc_in,
    x1v, branchv, ffnv, dh2v, dmod, dsend, dbuf,
    l_attn, l_h2, l_mid, r_ffn, r_branch, r_gu, l_h2s, l_attns, r_branchs,
    za_down, za_up, za_out, zb_down, zb_up, zb_out, z_out,
    gl_s, gl_r, gr_s, gr_r, g_loc, za_s, za_r, zb_s, zb_r, z_loc,
    tok_send, tok_recv, tok_loc, w_send, w_recv, w_loc, wh_sem, act_sem, mod_s, mod_r,
    at_s, at_r, do_s, do_r, dq_s, dq_r, dw_sem, pc_s, pc_r, dm_s, dm_r, loc,
):
    img, ty, z = lax.axis_index("img"), lax.axis_index("ty"), lax.axis_index("tx")
    b = ty * 4 + z
    me = img * 16 + b
    width = tok.shape[1]
    half = width // 2
    hidden = wup.shape[1] // 2
    part = ada.shape[0]
    other = 1 - img

    def dev(i=img, t=ty, k=z):
        return {"img": i, "ty": t, "tx": k}

    def dev_flat(p):
        return dev(p // 16, lax.rem(p // 4, 4), lax.rem(p, 4))

    def dev_tile(t):
        return dev(img, t // 4, lax.rem(t, 4))

    def rcopy(src, dst, s, r, d):
        return pltpu.make_async_remote_copy(
            src_ref=src, dst_ref=dst, send_sem=s, recv_sem=r, device_id=d, device_id_type=MESH
        )

    def loop(lo, hi, f):
        def step(k, c):
            f(k)
            return c

        lax.fori_loop(lo, hi, step, 0)

    bar = pltpu.get_barrier_semaphore()
    loop(
        1, 32,
        lambda k: pl.semaphore_signal(
            bar, inc=1, device_id=dev_flat(lax.rem(me + k, 32)), device_id_type=MESH
        ),
    )
    pl.semaphore_wait(bar, 31)

    hbm = (wout, wup, wdown, wqkv)
    vm = (woutv, wupv, wdownv, qkv_hbm)
    chunks = weight_chunks(width, hidden)

    def wregion(i, owner, p):
        m, c0, cn = chunks[i]
        rows = hbm[m].shape[0]
        return vm[m].at[pl.ds(owner * rows + p * (rows // 4), rows // 4), pl.ds(c0, cn)]

    def w_x(i):
        m, c0, cn = chunks[i]
        piece = hbm[m].shape[0] // 4
        return rcopy(
            hbm[m].at[pl.ds(ty * piece, piece), pl.ds(c0, cn)],
            wregion(i, img, ty), w_send.at[i, 0], w_recv.at[i, ty], dev(i=other),
        )

    def w_y(i):
        ref = wregion(i, other, ty)
        return rcopy(ref, ref, w_send.at[i, 1], w_recv.at[i, ty], dev(t=ty ^ 2))

    def w_c(i, p, slot):
        ref = wregion(i, other, p)
        return rcopy(ref, ref, w_send.at[i, slot], w_recv.at[i, p], dev(t=ty ^ 1))

    def w_wait(i, p):
        ref = wregion(i, other, p)
        rcopy(ref, ref, w_send.at[i, 0], w_recv.at[i, p], dev(t=ty ^ 1)).wait_recv()

    def x_arrived(i):
        w_wait(i, ty)
        w_y(i).start()
        w_c(i, ty, 2).start()

    def y_arrived(i):
        w_wait(i, ty ^ 2)
        w_c(i, ty ^ 2, 3).start()

    def w_done(i):
        w_wait(i, ty ^ 1)
        w_wait(i, ty ^ 3)

    def w_drain(i):
        w_x(i).wait_send()
        w_y(i).wait_send()
        w_c(i, ty, 2).wait_send()
        w_c(i, ty ^ 2, 3).wait_send()

    def own(m):
        rows = hbm[m].shape[0]
        return pltpu.make_async_copy(hbm[m], vm[m].at[pl.ds(img * rows, rows)], w_loc.at[m])

    act_copy = rcopy(act, actbuf.at[img], act_sem.at[0], act_sem.at[1], dev(i=other))
    act_copy.start()
    actbuf[img] = act[...]
    wh_copy = rcopy(wh, whv.at[pl.ds(img * half, half)], wh_sem.at[0], wh_sem.at[1], dev(i=other))
    wh_copy.start()
    whv[pl.ds(pl.multiple_of(img * half, 64), half), :] = wh[...]

    def tok_at(chunk):
        return tok_all.at[pl.ds(pl.multiple_of(chunk * TILE, TILE), TILE)]

    def t_send(src, chunk, way, d):
        return rcopy(src, tok_at(chunk), tok_send.at[chunk, way], tok_recv.at[chunk], d)

    def t_wait(chunk):
        t_send(tok, chunk, 0, dev(t=ty ^ 1)).wait_recv()

    tok_own = pltpu.make_async_copy(tok, tok_at(b), tok_loc)
    tok_own.start()

    def t_forward(src, chunk, up, down):
        if up:

            @pl.when(z < 3)
            def _():
                t_send(src, chunk, 0, dev(k=z + 1)).start()

        if down:

            @pl.when(z > 0)
            def _():
                t_send(src, chunk, 1, dev(k=z - 1)).start()

        t_send(src, chunk, 2, dev(t=ty ^ 2)).start()
        t_send(src, chunk, 3, dev(t=ty ^ 1)).start()

    t_forward(tok, b, True, True)
    for m in range(3):
        own(m).start()
    for i in range(9):
        w_x(i).start()

    act_copy.wait_recv()
    for i in range(2):
        modsend[i, :, 0:part] = dot_nt(actbuf[i].astype(BF16), ada[...])

    def mod_copy(p):
        return rcopy(modsend.at[p // 16], modbuf.at[me], mod_s.at[p], mod_r.at[me], dev_flat(p))

    loop(1, 32, lambda k: mod_copy(lax.rem(me + k, 32)).start())
    modbuf[me] = modsend[img]

    for s in (1, 2, 3):

        @pl.when(z - s >= 0)
        def _():
            t_wait(b - s)
            t_forward(tok_at(b - s), b - s, True, False)

        @pl.when(z + s <= 3)
        def _():
            t_wait(b + s)
            t_forward(tok_at(b + s), b + s, False, True)

    def t_y(zz):
        chunk = (ty ^ 2) * 4 + zz
        t_wait(chunk)
        t_send(tok_at(chunk), chunk, 3, dev(t=ty ^ 1)).start()

    loop(0, 4, t_y)
    x_arrived(0)
    for i in range(1, 5):
        x_arrived(i)
    w_x(9).start()
    loop(0, 4, lambda zz: t_wait((ty ^ 1) * 4 + zz))
    loop(0, 4, lambda zz: t_wait((ty ^ 3) * 4 + zz))

    def t_drain(zz):
        chunk = ty * 4 + zz
        ref = tok_at(chunk)

        @pl.when((zz <= z) & (z < 3))
        def _():
            t_send(ref, chunk, 0, dev(t=ty ^ 1)).wait_send()

        @pl.when((zz >= z) & (z > 0))
        def _():
            t_send(ref, chunk, 1, dev(t=ty ^ 1)).wait_send()

        t_send(ref, chunk, 2, dev(t=ty ^ 1)).wait_send()
        t_send(ref, chunk, 3, dev(t=ty ^ 1)).wait_send()
        away = (ty ^ 2) * 4 + zz
        t_send(tok_at(away), away, 3, dev(t=ty ^ 1)).wait_send()

    loop(0, 4, t_drain)
    tok_own.wait()

    def mod_wait(k):
        p = lax.rem(me + k, 32)
        rcopy(
            modsend.at[0], modbuf.at[p], mod_s.at[p], mod_r.at[p], dev_flat(p)
        ).wait()

    loop(1, 32, mod_wait)
    for s in range(32):
        modv[:, s * part : (s + 1) * part] = modbuf[s, :, 0:part]
    shift1, scale1, gate1, shift2, scale2, gate2 = [
        functools.partial(lambda k: modv[0:1, k * width : (k + 1) * width], k) for k in range(6)
    ]
    wh_copy.wait()

    height, wide = hw[0], hw[1]
    local = lax.broadcasted_iota(jnp.int32, (TILE, PAD), 0)
    lane = lax.broadcasted_iota(jnp.int32, (TILE, PAD), 1)

    def tile_layout(t):
        row_tile, col_tile = t // 4, lax.rem(t, 4)
        top = row_tile * height // 4
        rows = (row_tile + 1) * height // 4 - top
        left = col_tile * wide // 4
        span = (col_tile + 1) * wide // 4 - left
        spans = jnp.full((TILE, PAD), span, jnp.int32)
        quot = jnp.floor((local.astype(F32) + 0.5) / spans.astype(F32)).astype(jnp.int32)
        valid = local < jnp.full((TILE, PAD), rows * span, jnp.int32)
        row = jnp.where(valid, top + quot, 0)
        col = jnp.where(valid, left + local - quot * spans, 0)
        return valid, row, col

    def rope(n, c, s1, s2):
        return n * c + pltpu.roll(n, PAD - 18, 1) * s1 + pltpu.roll(n, 18, 1) * s2

    def unrope(d, c, s1, s2):
        return d * c + pltpu.roll(d * s1, 18, 1) + pltpu.roll(d * s2, PAD - 18, 1)

    def split_sin(sine):
        first = (lane < 18) | ((lane >= 36) & (lane < 54))
        return jnp.where(first, -sine, 0.0), jnp.where(first, 0.0, sine)

    def head_rows(t):
        valid, row, col = tile_layout(t)
        hot = jnp.where((lane == row) | (lane - 64 == col), 1.0, 0.0)
        angles = lax.dot_general(
            hot, tab[...], (((1,), (0,)), ((), ())),
            precision=HIGH, preferred_element_type=F32,
        )
        c, sine = angles[:, 0:PAD], angles[:, PAD : 2 * PAD]
        cosv[t] = c
        sinv[t] = sine
        s1, s2 = split_sin(sine)
        at = pl.ds(pl.multiple_of(t * TILE, TILE), TILE)
        x = tok_all[at, :].astype(F32)
        r = lax.rsqrt(jnp.mean(x * x, axis=1, keepdims=True) + EPS)
        h1 = ((x * r) * (1.0 + scale1()) + shift1()).astype(BF16)
        tok_all[at, :] = h1
        qkv = dot(h1, whv[...])
        q_r, k_r, v_r = qkv[:, 0:PAD], qkv[:, PAD : 2 * PAD], qkv[:, 2 * PAD : 3 * PAD]
        qraw[t] = q_r
        kraw[t] = k_r

        def normed(v, gain):
            rr = lax.rsqrt(jnp.sum(v * v, axis=1, keepdims=True) * (1.0 / HEAD) + EPS)
            return v * rr * gain[0:1, :]

        q_f = rope(normed(q_r, q_gain), c, s1, s2) * HEAD ** (-0.5)
        k_f = rope(normed(k_r, k_gain), c, s1, s2)
        qa[t] = jnp.where(lane == HEAD, 1.0, q_f).astype(BF16)
        k_f = jnp.where(lane == HEAD, jnp.where(valid, 0.0, -30000.0), k_f)
        k_f = jnp.where((lane > HEAD) & (lane < HEAD + 4), 1.0, k_f)
        ka[t] = k_f.astype(BF16)
        kt[:, pl.ds(pl.multiple_of(t * TILE, TILE), TILE)] = k_f.T.astype(BF16)
        va[t] = jnp.where((lane >= HEAD) & (lane < HEAD + 3), 1.0, v_r).astype(BF16)

    loop(0, 16, head_rows)
    for i in range(5, 9):
        x_arrived(i)
    y_arrived(0)

    def head_lanes(h):
        return attn_in.at[:, pl.ds(pl.multiple_of(h * PAD, PAD), PAD)]

    def at_copy(t):
        return rcopy(attn_send.at[t], head_lanes(b), at_s.at[t], at_r.at[b], dev_tile(t))

    def attend(k):
        q2 = qa[pl.ds(2 * k, 2)].reshape(2 * TILE, PAD)
        p = jnp.exp(dot(q2, kt[...])).astype(BF16)
        o = dot(p, va[...].reshape(16 * TILE, PAD))
        total = o[:, HEAD : HEAD + 1]
        o = o / total
        lse = jnp.log(total)
        q3 = put_split3(q2.astype(F32), -lse, HEAD + 1)
        o16 = o.astype(BF16)
        for u in range(2):
            t = 2 * k + u
            rows = slice(u * TILE, (u + 1) * TILE)
            onorm[t] = o[rows]
            qa[t] = q3[rows].astype(BF16)
            qt[:, pl.ds(pl.multiple_of(t * TILE, TILE), TILE)] = q3[rows].T.astype(BF16)
            attn_send[t] = o16[rows]

            @pl.when(t != b)
            def _():
                at_copy(t).start()

    loop(0, 8, attend)
    head_lanes(b)[...] = attn_send[b]
    for i in range(1, 5):
        y_arrived(i)
    x_arrived(9)
    w_x(10).start()
    for i in range(5, 9):
        y_arrived(i)

    def at_wait(k):
        p = lax.rem(b + k, 16)
        rcopy(attn_send.at[p], head_lanes(p), at_s.at[p], at_r.at[p], dev_tile(p)).wait()

    loop(1, 16, at_wait)

    def put_halves(ref, value):
        pad = jnp.zeros((TILE, 5 * PAD - half), F32)
        for k in range(2):
            piece = jnp.concatenate([value[:, k * half : (k + 1) * half], pad], axis=1)
            ref[:, k * 5 * PAD : (k + 1) * 5 * PAD] = piece.astype(BF16)

    def put_blocks(ref, value):
        pad = jnp.zeros((TILE, PAD - HEAD), F32)
        for k in range(16):
            zz = k % 4
            to = 4 * (k // 4) + 2 * (zz % 2) + zz // 2
            piece = jnp.concatenate([value[:, k * HEAD : (k + 1) * HEAD], pad], axis=1)
            ref[:, to * PAD : (to + 1) * PAD] = piece.astype(BF16)

    l_src, l_all = (l_mid, l_h2s, l_attns), (lb_down, lb_up, lb_out)
    r_src, r_all = (attn_in, r_gu, r_branchs), (rb_down, rb_up, rb_out)
    y, c = ty // 2, lax.rem(ty, 2)

    def slot_rows(i, t):
        return pl.ds(pl.multiple_of((i * 4 + t) * TILE, TILE), TILE)

    def lanes_at(k, n):
        return pl.ds(pl.multiple_of(k * n, PAD), n)

    def g_left(m, k, src, i, t, d):
        dst = l_all[m].at[slot_rows(i, t)]
        return rcopy(dst if src is None else src, dst, gl_s.at[m, k], gl_r.at[m, i * 4 + t], d)

    def g_right(m, k, src, i, t, d):
        n = r_src[m].shape[1] // 4
        dst = r_all[m].at[slot_rows(i, t)]
        if k in (2, 4, 5, 6):
            dst = r_all[m].at[slot_rows(i, t), lanes_at(1 - c, n)]
        return rcopy(dst if src is None else src, dst, gr_s.at[m, k], gr_r.at[m, i * 4 + t], d)

    to_x, to_y, to_c = dev(i=other), dev(t=ty ^ 2), dev(t=ty ^ 1)

    def l_part(m, k):
        return l_src[m].at[:, lanes_at(k, l_src[m].shape[1] // 2)]

    def r_part(m, k, n):
        return r_src[m].at[:, lanes_at(k, n * (r_src[m].shape[1] // 4))]

    def g_first(m):
        return [
            g_left(m, 0, l_part(m, other), img, ty, to_x),
            g_right(m, 0, r_part(m, 1 - y, 2), img, ty, to_y),
            g_left(m, 1, l_part(m, img), img, ty, to_y),
            g_right(m, 1, r_part(m, y, 2), img, ty, to_x),
            g_left(m, 2, l_part(m, img), img, ty, to_c),
            g_right(m, 2, r_part(m, ty ^ 1, 1), img, ty, to_c),
        ]

    def g_own(m):
        n = r_src[m].shape[1] // 4
        rows = slot_rows(img, ty)
        return [
            pltpu.make_async_copy(l_part(m, img), l_all[m].at[rows], g_loc.at[m, 0]),
            pltpu.make_async_copy(
                r_part(m, ty, 1), r_all[m].at[rows, lanes_at(c, n)], g_loc.at[m, 1]
            ),
        ]

    def g_start(m):
        for copy in g_first(m) + g_own(m):
            copy.start()

    def g_hop(m):
        g_left(m, 0, None, other, ty, to_x).wait_recv()
        g_left(m, 3, None, other, ty, to_y).start()
        g_left(m, 4, None, other, ty, to_c).start()
        g_right(m, 0, None, img, ty ^ 2, to_y).wait_recv()
        g_right(m, 3, None, img, ty ^ 2, to_x).start()
        g_right(m, 4, None, img, ty ^ 2, to_c).start()
        g_left(m, 1, None, img, ty ^ 2, to_y).wait_recv()
        g_left(m, 5, None, img, ty ^ 2, to_c).start()
        g_right(m, 1, None, other, ty, to_x).wait_recv()
        g_right(m, 5, None, other, ty, to_c).start()

    def g_hop2(m):
        g_left(m, 3, None, other, ty ^ 2, to_y).wait_recv()
        g_left(m, 6, None, other, ty ^ 2, to_c).start()
        g_right(m, 3, None, other, ty ^ 2, to_x).wait_recv()
        g_right(m, 6, None, other, ty ^ 2, to_c).start()

    def g_done(m):
        n = r_src[m].shape[1] // 4
        for i in range(2):
            for t in (ty ^ 1, ty ^ 3):
                g_left(m, 2, None, i, t, to_c).wait_recv()
                ref = r_all[m].at[slot_rows(i, t), lanes_at(c, n)]
                rcopy(ref, ref, gr_s.at[m, 2], gr_r.at[m, i * 4 + t], to_c).wait_recv()
        for copy in g_own(m):
            copy.wait()

    def g_drain(m):
        for copy in g_first(m):
            copy.wait_send()
        for k, i, t in ((3, other, ty), (4, other, ty), (5, img, ty ^ 2), (6, other, ty ^ 2)):
            g_left(m, k, None, i, t, to_c).wait_send()
        for k, i, t in ((3, img, ty ^ 2), (4, img, ty ^ 2), (5, other, ty), (6, other, ty ^ 2)):
            g_right(m, k, None, i, t, to_c).wait_send()

    attn = jnp.concatenate(
        [attn_in[:, h * PAD : h * PAD + HEAD].astype(F32) for h in range(16)], axis=1
    )
    l_attn[...] = attn.astype(BF16)
    put_halves(l_attns, attn)
    own(OUT).wait()
    w_done(0)
    own_valid = tile_layout(b)[0]
    keep = jnp.where(own_valid, 1.0, 0.0)[:, 0:1]
    cols = width // 3

    def project(k):
        at = pl.ds(pl.multiple_of(k * cols, PAD), cols)
        branchv[:, at] = dot(l_attn[...], woutv[:, at])

    loop(0, 3, project)
    x = tok[...].astype(F32)
    x1 = x + keep * gate1() * branchv[...]
    x1v[...] = x1
    r = lax.rsqrt(jnp.mean(x1 * x1, axis=1, keepdims=True) + EPS)
    h2_rows = (x1 * r) * (1.0 + scale2()) + shift2()
    l_h2[...] = h2_rows.astype(BF16)
    put_halves(l_h2s, h2_rows)
    d_ffn = cot[...].astype(F32) * keep * gate2()
    r_ffn[...] = d_ffn.astype(BF16)
    put_blocks(attn_in, d_ffn)
    ffnv[...] = jnp.zeros_like(ffnv)
    dh2v[...] = jnp.zeros_like(dh2v)
    y_arrived(9)
    for i in range(1, 10):
        w_done(i)
    own(UP).wait()
    own(DOWN).wait()
    step = 256

    def mlp(j):
        g_at = pl.ds(pl.multiple_of(j * step, step), step)
        u_at = pl.ds(pl.multiple_of(hidden + j * step, step), step)
        h2 = l_h2[...]
        gate = dot(h2, wupv[:, g_at])
        up = dot(h2, wupv[:, u_at])
        sig = 1.0 / (1.0 + jnp.exp(-gate))
        act_g = gate * sig
        mid = (act_g * up).astype(BF16)
        l_mid[:, g_at] = mid
        w3 = wdownv[g_at, :]
        ffnv[...] += dot(mid, w3)
        d_mid = dot_nt(r_ffn[...], w3)
        d_gate = (d_mid * up * (sig + gate * sig * (1.0 - sig))).astype(BF16)
        d_up = (d_mid * act_g).astype(BF16)
        r_gu[:, g_at] = d_gate
        r_gu[:, u_at] = d_up
        dh2v[...] += dot_nt(d_gate, wupv[:, g_at]) + dot_nt(d_up, wupv[:, u_at])

    loop(0, hidden // step, mlp)
    g_start(0)
    g_start(1)
    x_arrived(10)
    ffn = ffnv[...]
    g = cot[...].astype(F32)
    x1 = x1v[...]
    mixed[...] = (x1 + keep * gate2() * ffn).astype(BF16)

    def dmod_put(k, row):
        dmod[0:1, k * width : (k + 1) * width] = row

    def colsum(v):
        return jnp.sum(v, axis=0, keepdims=True)

    dmod_put(5, colsum(g * keep * ffn))
    d_h2 = dh2v[...]
    norm2 = x1 * r
    dmod_put(4, colsum(d_h2 * norm2))
    dmod_put(3, colsum(d_h2))
    d_n2 = d_h2 * (1.0 + scale2())
    d_x1 = g + r * (d_n2 - norm2 * jnp.mean(d_n2 * norm2, axis=1, keepdims=True))
    dmod_put(2, colsum(d_x1 * keep * branchv[...]))
    x1v[...] = d_x1
    d_branch = d_x1 * keep * gate1()
    r_branch[...] = d_branch.astype(BF16)
    put_blocks(r_branchs, d_branch)

    def unproject(k):
        at = pl.ds(pl.multiple_of(k * cols, PAD), cols)
        branchv[:, at] = dot_nt(r_branch[...], woutv[at, :])

    loop(0, 3, unproject)

    zeros = jnp.zeros((TILE, PAD - HEAD), F32)
    d_attn = branchv[...]
    for h in range(16):
        attn_send[h] = jnp.concatenate(
            [d_attn[:, h * HEAD : (h + 1) * HEAD], zeros], axis=1
        ).astype(BF16)

    def do_copy(t):
        return rcopy(attn_send.at[t], do_in.at[b], do_s.at[t], do_r.at[b], dev_tile(t))

    loop(1, 16, lambda k: do_copy(lax.rem(b + k, 16)).start())
    do_in[b] = attn_send[b]
    g_start(2)
    y_arrived(10)

    def do_wait(k):
        p = lax.rem(b + k, 16)
        rcopy(attn_send.at[p], do_in.at[p], do_s.at[p], do_r.at[p], dev_tile(p)).wait()

    loop(1, 16, do_wait)
    g_hop(0)

    def delta(t):
        d = do_in[t].astype(F32)
        dsum = jnp.sum(jnp.where(lane < HEAD, d * onorm[t], 0.0), axis=1, keepdims=True)
        d = put_split3(d, -dsum, HEAD)
        do_in[t] = d.astype(BF16)
        dot_t[:, pl.ds(pl.multiple_of(t * TILE, TILE), TILE)] = d.T.astype(BF16)

    loop(0, 16, delta)
    dqt[...] = jnp.zeros_like(dqt)

    def attend_back(k):
        two = pl.ds(2 * k, 2)
        p = jnp.exp(dot(ka[two].reshape(2 * TILE, PAD), qt[...]))
        ds = (p * dot(va[two].reshape(2 * TILE, PAD), dot_t[...])).astype(BF16)
        dkv[two] = dot(ds, qa[...].reshape(16 * TILE, PAD)).reshape(2, TILE, PAD)
        dvv[two] = dot(p.astype(BF16), do_in[...].reshape(16 * TILE, PAD)).reshape(2, TILE, PAD)
        at = pl.ds(pl.multiple_of(k * 2 * TILE, 2 * TILE), 2 * TILE)
        dqt[...] += dot(kt[:, at], ds)

    loop(0, 4, attend_back)
    g_hop(1)
    loop(4, 8, attend_back)

    for i in range(11):
        w_drain(i)
    gain_grad[...] = jnp.zeros_like(gain_grad)

    def dq_rows(t):
        return wdownv.at[pl.ds(pl.multiple_of(t * TILE, TILE), TILE), pl.ds(3 * PAD, 2 * PAD)]

    def dq_copy(t):
        return rcopy(dq_rows(t), dqkv_in.at[b], dq_s.at[t], dq_r.at[b], dev_tile(t))

    def heads_back(t):
        c = cosv[t]
        s1, s2 = split_sin(sinv[t])

        def norm_back(d, v, gain, row):
            rr = lax.rsqrt(jnp.sum(v * v, axis=1, keepdims=True) * (1.0 / HEAD) + EPS)
            n = v * rr
            gain_grad[row : row + 1, :] += colsum(d * n)
            dn = d * gain[0:1, :]
            return rr * (dn - n * (jnp.sum(dn * n, axis=1, keepdims=True) * (1.0 / HEAD)))

        d_q = dqt[:, pl.ds(pl.multiple_of(t * TILE, TILE), TILE)].T * HEAD ** (-0.5)
        d_q = norm_back(unrope(d_q, c, s1, s2), qraw[t], q_gain, 0)
        d_k = norm_back(unrope(dkv[t], c, s1, s2), kraw[t], k_gain, 1)
        d_v = jnp.where(lane < HEAD, dvv[t], 0.0)
        at = pl.ds(pl.multiple_of(t * TILE, TILE), TILE)
        wdownv[at, 0 : 3 * PAD] = jnp.concatenate([d_q, d_k, d_v], axis=1).astype(BF16)
        wdownv[at, 3 * PAD : 5 * PAD] = jnp.concatenate(
            [d_q[:, 0:HEAD], d_k[:, 0:HEAD], d_v[:, 0:HEAD], zeros[:, 0:40]], axis=1
        ).astype(BF16)

        @pl.when(t != b)
        def _():
            dq_copy(t).start()

    loop(0, 16, heads_back)
    dqkv_in[b] = dq_rows(b)[...]
    g_hop(2)
    g_hop2(0)

    sums_t = (branchv, ffnv, dqt.at[:, pl.ds(0, width)])
    for ref in sums_t:
        ref[...] = jnp.zeros((PAD, width), F32)

    def dw_rows(k):
        at = pl.ds(pl.multiple_of(k * 2 * TILE, TILE), 2 * TILE)
        term = dot_tn(wdownv[at, 0 : 3 * PAD], tok_all[at, :])
        for p in range(3):
            sums_t[p][...] += term[p * PAD : (p + 1) * PAD]

    loop(0, 8, dw_rows)
    for p in range(3):
        wdownv[0:width, (5 + p) * PAD : (6 + p) * PAD] = sums_t[p][...].T.astype(BF16)

    def dw_half(i):
        return wdownv.at[pl.ds(pl.multiple_of(i * half, 64), half), pl.ds(5 * PAD, 3 * PAD)]

    dw_copy = rcopy(dw_half(other), dw_in, dw_sem.at[0], dw_sem.at[1], dev(i=other))
    dw_copy.start()
    g_hop2(1)
    g_hop2(2)
    w_done(10)

    loads = [
        pltpu.make_async_copy(
            src, wupv.at[pl.ds(owner * half, half), pl.ds(0, 3 * width)], loc.at[k]
        )
        for k, (src, owner) in enumerate(
            ((wqkv, img), (qkv_hbm.at[pl.ds(other * half, half)], other))
        )
    ]
    for load in loads:
        load.start()

    def dq_wait(k):
        p = lax.rem(b + k, 16)
        rcopy(dq_rows(p), dqkv_in.at[p], dq_s.at[p], dq_r.at[p], dev_tile(p)).wait()

    loop(1, 16, dq_wait)
    dw_copy.wait()
    dw_sum = dw_half(img)[...].astype(F32) + dw_in[...].astype(F32)

    def pc_send(p):
        return wdownv.at[pl.ds(width, half), pl.ds((5 + p) * PAD, PAD)]

    for p in range(3):
        pc_send(p)[...] = dw_sum[:, p * PAD : (p + 1) * PAD].astype(BF16)

    def pc_copy(p):
        group = 16 * p + b
        to, slot = group // 3, lax.rem(group, 3)
        return to, rcopy(
            pc_send(p), pc_in.at[slot], pc_s.at[p], pc_r.at[slot], dev_tile(to)
        )

    for p in range(3):
        to, copy = pc_copy(p)

        @pl.when(to != b)
        def _():
            copy.start()

        @pl.when(to == b)
        def _():
            pc_in[lax.rem(16 * p + b, 3)] = pc_send(p)[...]

    for load in loads:
        load.wait()
    dqkv = [dqkv_in[h].astype(F32) for h in range(16)]
    def own_part(p):
        return slice(16 * TILE + p * TILE, 16 * TILE + (p + 1) * TILE)

    for p in range(3):
        wdownv[own_part(p), :] = jnp.concatenate(
            [dqkv[h][:, p * HEAD : (p + 1) * HEAD] for h in range(16)], axis=1
        ).astype(BF16)

    def h1_back(k):
        at = pl.ds(pl.multiple_of(k * cols, PAD), cols)
        dh2v[:, at] = sum(
            dot_nt(wdownv[own_part(p), :], wupv[at, p * width : (p + 1) * width])
            for p in range(3)
        )

    loop(0, 3, h1_back)
    d_h1 = dh2v[...]
    x = tok[...].astype(F32)
    r1 = lax.rsqrt(jnp.mean(x * x, axis=1, keepdims=True) + EPS)
    norm1 = x * r1
    dmod_put(1, colsum(d_h1 * norm1))
    dmod_put(0, colsum(d_h1))
    d_n1 = d_h1 * (1.0 + scale1())
    back = r1 * (d_n1 - norm1 * jnp.mean(d_n1 * norm1, axis=1, keepdims=True))
    tgrad[...] = (x1v[...] + back).astype(BF16)

    high, low = z // 2, lax.rem(z, 2)
    l0 = 3 * width

    def z_load(m):
        kl, n = l_all[m].shape[1], r_src[m].shape[1] // 4
        copies = [
            pltpu.make_async_copy(
                l_all[m], wupv.at[pl.ds(0, 8 * TILE), pl.ds(l0, kl)], z_loc.at[0]
            ),
            pltpu.make_async_copy(
                r_all[m].at[:, lanes_at(c, n)],
                wupv.at[pl.ds(0, 8 * TILE), pl.ds(l0 + kl, n)],
                z_loc.at[1],
            ),
        ]
        for copy in copies:
            copy.start()
        for copy in copies:
            copy.wait()

    def z_copies(m):
        if m == 0:
            sent = [kt.at[pl.ds(0, 80), pl.ds(0, 12 * PAD)], qt.at[pl.ds(0, 80), pl.ds(0, 12 * PAD)]]
        elif m == 1:
            sent = [tok_all.at[pl.ds(0, half), pl.ds(k * 3 * PAD, 3 * PAD)] for k in range(2)]
        else:
            sent = [tok_all.at[pl.ds(640 + 128 * k, 80), pl.ds(0, 5 * PAD)] for k in range(2)]
        return [
            rcopy(sent[k], za[m].at[k], za_s.at[m, k], za_r.at[m, k], dev(k=z ^ 1))
            for k in range(2)
        ]

    za, zb = (za_down, za_up, za_out), (zb_down, zb_up, zb_out)
    z_rest = (
        dot_t.at[pl.ds(0, 80), pl.ds(0, 12 * PAD)],
        tok_all.at[pl.ds(0, half), pl.ds(6 * PAD, 3 * PAD)],
        tok_all.at[pl.ds(896, 80), pl.ds(0, 5 * PAD)],
    )
    z_own = (dqt.at[pl.ds(0, 80), pl.ds(0, 12 * PAD)], up_grad, z_out)

    def z_copy2(m):
        return rcopy(z_rest[m], zb[m], zb_s.at[m], zb_r.at[m], dev(k=z ^ 2))

    def z_product(m):
        kl = l_all[m].shape[1]
        sent = [copy.src_ref for copy in z_copies(m)]
        if m == 1:

            def turn(k):
                at = pl.ds(pl.multiple_of(k * TILE, TILE), TILE)
                woutv[0 : 5 * PAD, at] = wupv[at, l0 : l0 + kl].astype(F32).T.astype(BF16)

            loop(0, 8, turn)

            def block(zz):
                at = pl.ds(pl.multiple_of(l0 + kl + zz * 3 * PAD, PAD), 3 * PAD)
                return dot(woutv[0:half, 0 : 8 * TILE], wupv[0 : 8 * TILE, at])

            for k in range(2):
                sent[k][...] = block(2 * k + 1 - low).astype(BF16)
            for copy in z_copies(m):
                copy.start()
            z_rest[m][...] = block(2 * (1 - high) + low).astype(BF16)
            z_own[m][...] = block(z)
            return

        def pair(k):
            at = pl.ds(pl.multiple_of(l0 + kl + k * 2 * PAD, PAD), 2 * PAD)
            return dot_tn(wupv[0 : 8 * TILE, at], wupv[0 : 8 * TILE, l0 : l0 + kl])

        both = pair(1 - low)
        for k in range(2):
            sent[k][...] = both[k * PAD : k * PAD + 80].astype(BF16)
        for copy in z_copies(m):
            copy.start()
        both = pair(low)
        first, second = both[0:80], both[PAD : PAD + 80]
        z_rest[m][...] = jnp.where(high == 0, second, first).astype(BF16)
        z_own[m][...] = jnp.where(high == 0, first, second)

    def z_second(m):
        for copy in z_copies(m):
            copy.wait()
        rest = z_rest[m][...].astype(F32) + za[m][1 - high].astype(F32)
        z_rest[m][...] = rest.astype(BF16)
        z_copy2(m).start()
        z_own[m][...] += za[m][high].astype(F32)

    def z_last(m):
        z_copy2(m).wait()
        z_own[m][...] += zb[m][...].astype(F32)

    for m in range(3):
        g_done(m)
        z_load(m)
        z_product(m)
    for m in range(3):
        z_second(m)
    for m in range(3):
        z_last(m)
    for m in range(3):
        g_drain(m)
    down_grad[...] = z_own[0][...].T[:, 0:HEAD]
    out_grad[...] = z_own[2][...].T[0:half, 0:HEAD]

    dsend[...] = jnp.zeros_like(dsend)
    for s in range(32):
        dsend[s, 0:1, 0:part] = dmod[0:1, s * part : (s + 1) * part]
        dsend[s, 1:3, 0:PAD] = gain_grad[0:2, :]

    def dm_copy(p):
        return rcopy(dsend.at[p], dbuf.at[me], dm_s.at[p], dm_r.at[me], dev_flat(p))

    loop(1, 32, lambda k: dm_copy(lax.rem(me + k, 32)).start())
    dbuf[me] = dsend[me]

    for slot in range(3):
        group = 3 * b + slot
        src = lax.rem(group, 16)

        @pl.when(src != b)
        def _():
            rcopy(
                pc_send(0), pc_in.at[slot], pc_s.at[0], pc_r.at[slot], dev_tile(src)
            ).wait_recv()

    qkv_grad[...] = jnp.concatenate(
        [pc_in[slot].astype(F32)[:, 0:HEAD] for slot in range(3)], axis=1
    )
    for p in range(3):
        to, copy = pc_copy(p)

        @pl.when(to != b)
        def _():
            copy.wait_send()

    def dm_wait(k):
        p = lax.rem(me + k, 32)
        rcopy(dsend.at[p], dbuf.at[p], dm_s.at[p], dm_r.at[p], dev_flat(p)).wait()

    loop(1, 32, dm_wait)
    sums = [
        lax.fori_loop(1, 16, lambda s, a, i=i: a + dbuf[16 * i + s], dbuf[16 * i])
        for i in range(2)
    ]
    gain_grad[...] = jnp.where(
        lax.broadcasted_iota(jnp.int32, (8, PAD), 0) < 2,
        pltpu.roll(sums[0] + sums[1], 7, 0)[:, 0:PAD],
        0.0,
    )
    row = lax.broadcasted_iota(jnp.int32, (8, 2 * PAD), 0)
    d_two = jnp.where(row == 0, sums[0][0:1, :], jnp.where(row == 1, sums[1][0:1, :], 0.0))
    row = lax.broadcasted_iota(jnp.int32, (8, width), 0)
    a_two = jnp.where(row == 0, actbuf[0], jnp.where(row == 1, actbuf[1], 0.0))
    ada_grad[...] = dot_tn(d_two, a_two, HIGH)[0:part, :]
    act_copy.wait_send()


def rope_table():
    table = np.zeros((PAD, 2 * PAD), np.float64)
    angle = np.arange(64)[:, None] * 10000.0 ** (-np.arange(18) / 18)
    for axis in range(2):
        rows = slice(64 * axis, 64 * axis + 64)
        for quarter in range(2):
            at = 36 * axis + 18 * quarter
            table[rows, at : at + 18] = np.cos(angle)
            table[rows, PAD + at : PAD + at + 18] = np.sin(angle)
    return table.astype(np.float32)


def run_block(tokens, cotangent, act, ada, wh, wout, wup, wdown, wqkv, q_gain, k_gain, hw):
    width, hidden = tokens.shape[1], wup.shape[1] // 2
    half, part = width // 2, ada.shape[0]
    vmem, any_ = pl.BlockSpec(memory_space=pltpu.VMEM), pl.BlockSpec(memory_space=pl.ANY)
    smem = pl.BlockSpec(memory_space=pltpu.SMEM)
    sds = jax.ShapeDtypeStruct
    v, dma = pltpu.VMEM, pltpu.SemaphoreType.DMA
    n_chunks = len(weight_chunks(width, hidden))
    tile16 = (16, TILE, PAD)
    out_shape = (
        sds((TILE, width), BF16),
        sds((TILE, width), BF16),
        sds((half, 3 * HEAD), F32),
        sds((part, width), F32),
        sds((8, PAD), F32),
        sds((hidden // 2, HEAD), F32),
        sds((half, 3 * PAD), F32),
        sds((half, HEAD), F32),
        sds((width, 3 * width), BF16),
        sds((8 * TILE, hidden // 2), BF16),
        sds((8 * TILE, 5 * PAD), BF16),
        sds((8 * TILE, 5 * PAD), BF16),
        sds((8 * TILE, 8 * PAD), BF16),
        sds((8 * TILE, hidden), BF16),
        sds((8 * TILE, 8 * PAD), BF16),
    )
    scratch = [
        v((16 * TILE, width), BF16),
        v((width, 3 * PAD), BF16),
        v((width, width), BF16),
        v((width, 2 * hidden), BF16),
        v((hidden, width), BF16),
        v((2, 8, width), F32),
        v((2, 8, 2 * PAD), F32),
        v((32, 8, 2 * PAD), F32),
        v((8, 6 * width), F32),
        v(tile16, F32),
        v(tile16, F32),
        v(tile16, F32),
        v(tile16, F32),
        v(tile16, BF16),
        v(tile16, BF16),
        v(tile16, BF16),
        v((PAD, 16 * TILE), BF16),
        v((PAD, 16 * TILE), BF16),
        v(tile16, F32),
        v(tile16, BF16),
        v((TILE, 16 * PAD), BF16),
        v(tile16, BF16),
        v((PAD, 16 * TILE), BF16),
        v((PAD, 16 * TILE), F32),
        v(tile16, F32),
        v(tile16, F32),
        v((16, TILE, 2 * PAD), BF16),
        v((half, 3 * PAD), BF16),
        v((3, half, PAD), BF16),
        v((TILE, width), F32),
        v((TILE, width), F32),
        v((TILE, width), F32),
        v((TILE, width), F32),
        v((8, 6 * width), F32),
        v((32, 8, 2 * PAD), F32),
        v((32, 8, 2 * PAD), F32),
        v((TILE, width), BF16),
        v((TILE, width), BF16),
        v((TILE, hidden), BF16),
        v((TILE, width), BF16),
        v((TILE, width), BF16),
        v((TILE, 2 * hidden), BF16),
        v((TILE, 10 * PAD), BF16),
        v((TILE, 10 * PAD), BF16),
        v((TILE, 16 * PAD), BF16),
        v((2, 80, hidden // 2), BF16),
        v((2, half, 3 * PAD), BF16),
        v((2, 80, 5 * PAD), BF16),
        v((80, hidden // 2), BF16),
        v((half, 3 * PAD), BF16),
        v((80, 5 * PAD), BF16),
        v((80, 5 * PAD), F32),
        dma((3, 8)),
        dma((3, 8)),
        dma((3, 8)),
        dma((3, 8)),
        dma((3, 2)),
        dma((3, 2)),
        dma((3, 2)),
        dma((3,)),
        dma((3,)),
        dma((2,)),
        dma((16, 4)),
        dma((16,)),
        dma,
        dma((n_chunks, 4)),
        dma((n_chunks, 4)),
        dma((4,)),
        dma((2,)),
        dma((2,)),
        dma((32,)),
        dma((32,)),
        dma((16,)),
        dma((16,)),
        dma((16,)),
        dma((16,)),
        dma((16,)),
        dma((16,)),
        dma((2,)),
        dma((3,)),
        dma((3,)),
        dma((32,)),
        dma((32,)),
        dma((2,)),
    ]
    return pl.pallas_call(
        block_kernel,
        out_shape=out_shape,
        in_specs=[vmem] * 5 + [any_] * 4 + [vmem] * 3 + [smem],
        out_specs=[vmem] * 8 + [any_] * 7,
        scratch_shapes=scratch,
        compiler_params=pltpu.CompilerParams(
            collective_id=0, has_side_effects=True, vmem_limit_bytes=VMEM_LIMIT
        ),
    )(tokens, cotangent, act, ada, wh, wout, wup, wdown, wqkv, q_gain, k_gain, rope_table(), hw)


def head_weight(weight):
    at = lax.axis_index(("ty", "tx")) * HEAD
    width = weight.shape[1] // 3
    parts = [
        lax.dynamic_slice_in_dim(weight, p * width + at, HEAD, axis=1) for p in range(3)
    ]
    return jnp.concatenate([jnp.pad(p, ((0, 0), (0, PAD - HEAD))) for p in parts], axis=1)


def fast_body(
    tokens,
    cotangent,
    class_embed,
    timestep,
    grid_height,
    grid_width,
    qkv_weight,
    out_weight,
    up_weight,
    down_weight,
    ada_weight,
    q_gain,
    k_gain,
):
    width = tokens.shape[2]
    act = jax.nn.silu(class_embed + time_embed(timestep, width)).astype(BF16).astype(F32)
    pad = lambda g: jnp.broadcast_to(jnp.pad(g, (0, PAD - HEAD))[None], (8, PAD))
    (mixed, tgrad, qkv_grad, ada_grad, gains, down_grad, up_grad, out_grad) = (
        run_block(
            tokens[0],
            cotangent[0],
            jnp.broadcast_to(act, (8, width)),
            ada_weight,
            head_weight(qkv_weight),
            out_weight,
            up_weight,
            down_weight,
            qkv_weight,
            pad(q_gain),
            pad(k_gain),
            jnp.concatenate([grid_height, grid_width]),
        )[:8]
    )
    return (
        mixed[None],
        tgrad[None],
        qkv_grad,
        out_grad,
        up_grad,
        down_grad,
        ada_grad,
        gains[0, :HEAD],
        gains[1, :HEAD],
    )


def solution(mesh):
    in_specs = (
        P("img", ("ty", "tx"), None),
        P("img", ("ty", "tx"), None),
        P("img", None),
        P("img"),
        P("img"),
        P("img"),
        P("img", None),
        P("img", None),
        P("img", None),
        P("img", None),
        P(("img", "ty", "tx"), None),
        P(),
        P(),
    )
    out_specs = (
        P("img", ("ty", "tx"), None),
        P("img", ("ty", "tx"), None),
        P("img", ("ty", "tx")),
        P("img", ("ty", "tx")),
        P("img", ("ty", "tx")),
        P("img", ("ty", "tx")),
        P(("img", "ty", "tx"), None),
        P(),
        P(),
    )
    shape = dict(mesh.shape)
    fast = (shape["img"], shape["ty"], shape["tx"]) == (2, 4, 4)
    body = fast_body if fast else general_body
    return jax.shard_map(body, mesh=mesh, in_specs=in_specs, out_specs=out_specs, check_vma=False)
```

```python
import functools

import jax
import jax.numpy as jnp
import numpy as np
from jax import lax
from jax.experimental import pallas as pl
from jax.experimental.pallas import tpu as pltpu
from jax.sharding import PartitionSpec as P

HEADS = 16
HEAD = 72


EPS = 1e-06
HIGH = lax.Precision.HIGHEST


def layout(slot, height, width, cap, rows_tiles, cols_tiles):
    tile = slot // cap
    row_tile = tile // cols_tiles
    col_tile = tile % cols_tiles
    local = slot % cap
    top = row_tile * height // rows_tiles
    bottom = (row_tile + 1) * height // rows_tiles
    left = col_tile * width // cols_tiles
    right = (col_tile + 1) * width // cols_tiles
    span = right - left
    valid = local < (bottom - top) * span
    row = jnp.where(valid, top + local // span, 0)
    col = jnp.where(valid, left + local % span, 0)
    return (valid, row, col)


def time_embed(step, dim):
    half = dim // 2
    freq = jnp.exp(-jnp.log(10000.0) * jnp.arange(half, dtype=jnp.float32) / half)
    angle = step.astype(jnp.float32)[:, None] * freq
    return jnp.concatenate([jnp.cos(angle), jnp.sin(angle)], axis=-1)


def rotate(part, position):
    quarter = part.shape[-1] // 2
    freq = jnp.exp(-jnp.log(10000.0) * jnp.arange(quarter, dtype=jnp.float32) / quarter)
    angle = position.astype(jnp.float32)[..., None, None] * freq
    first, second = (part[..., :quarter], part[..., quarter:])
    cosine, sine = (jnp.cos(angle), jnp.sin(angle))
    return jnp.concatenate(
        [first * cosine - second * sine, second * cosine + first * sine], axis=-1
    )


def rope(heads, row, col):
    half = heads.shape[-1] // 2
    return jnp.concatenate(
        [rotate(heads[..., :half], row), rotate(heads[..., half:], col)], axis=-1
    )


def head_norm(value, gain):
    return value * lax.rsqrt(jnp.mean(value * value, axis=-1, keepdims=True) + EPS) * gain


def rms(value):
    return value * lax.rsqrt(jnp.mean(value * value, axis=-1, keepdims=True) + EPS)


def flat_rows(value):
    return value.reshape(-1, value.shape[-1])


def outer_sum(left, right):
    return lax.dot_general(
        flat_rows(left),
        flat_rows(right),
        (((0,), (0,)), ((), ())),
        preferred_element_type=jnp.float32,
    )


def times_transposed(left, weight):
    return lax.dot_general(
        left, weight, (((left.ndim - 1,), (1,)), ((), ())), preferred_element_type=jnp.float32
    )


def masked_scores(query, keys_all, key_valid):
    scores = jnp.einsum("qhd,khd->hqk", query, keys_all, preferred_element_type=jnp.float32)
    return jnp.where(key_valid[None, None, :], scores, -1e30)


def general_body(
    tokens,
    cotangent,
    class_embed,
    timestep,
    grid_height,
    grid_width,
    qkv_weight,
    out_weight,
    up_weight,
    down_weight,
    ada_weight,
    q_gain,
    k_gain,
):
    images, slots_dev, width = tokens.shape
    rows_tiles = lax.axis_size("ty")
    cols_tiles = lax.axis_size("tx")
    slots_all = slots_dev * rows_tiles * cols_tiles
    own_slot = lax.axis_index(("ty", "tx")) * slots_dev + jnp.arange(slots_dev, dtype=jnp.int32)
    all_slot = jnp.arange(slots_all, dtype=jnp.int32)
    valid_q, row_q, col_q = jax.vmap(
        lambda h, w: layout(own_slot, h, w, slots_dev, rows_tiles, cols_tiles)
    )(grid_height, grid_width)
    valid_k = jax.vmap(lambda h, w: layout(all_slot, h, w, slots_dev, rows_tiles, cols_tiles)[0])(
        grid_height, grid_width
    )
    keep = valid_q.astype(jnp.float32)[..., None]
    act = jax.nn.silu(class_embed + time_embed(timestep, width)).astype(jnp.bfloat16)
    mod = lax.dot_general(
        act,
        lax.all_gather(ada_weight, ("img", "ty", "tx"), axis=0, tiled=True),
        (((1,), (1,)), ((), ())),
        preferred_element_type=jnp.float32,
    )
    shift1, scale1, gate1, shift2, scale2, gate2 = [
        part[:, None, :] for part in jnp.split(mod, 6, axis=1)
    ]
    wqkv, wout, w12, w3 = (
        lax.all_gather(qkv_weight, "img", axis=0, tiled=True),
        lax.all_gather(out_weight, "img", axis=0, tiled=True),
        lax.all_gather(up_weight, "img", axis=0, tiled=True),
        lax.all_gather(down_weight, "img", axis=0, tiled=True),
    )
    xf = tokens.astype(jnp.float32)
    norm1, pull_norm1 = jax.vjp(rms, xf)
    h1 = (norm1 * (1.0 + scale1) + shift1).astype(jnp.bfloat16)
    qkv = jnp.dot(h1, wqkv, preferred_element_type=jnp.float32).reshape(
        images, slots_dev, 3, HEADS, HEAD
    )

    def finish(query_raw, key_raw, query_gain, key_gain):
        query = rope(head_norm(query_raw, query_gain), row_q, col_q) * HEAD ** (-0.5)
        return (query, rope(head_norm(key_raw, key_gain), row_q, col_q))

    (query_f, key_f), pull_heads = jax.vjp(finish, qkv[:, :, 0], qkv[:, :, 1], q_gain, k_gain)
    query_b = query_f.astype(jnp.bfloat16)
    key_b = key_f.astype(jnp.bfloat16)
    value_b = qkv[:, :, 2].astype(jnp.bfloat16)
    keys_all, values_all = (
        lax.all_gather(key_b, ("ty", "tx"), axis=1, tiled=True),
        lax.all_gather(value_b, ("ty", "tx"), axis=1, tiled=True),
    )
    index = 0
    scores = masked_scores(query_b[index], keys_all[index], valid_k[index])
    top = jnp.max(scores, axis=-1, keepdims=True)
    lse = top + jnp.log(jnp.sum(jnp.exp(scores - top), axis=-1, keepdims=True))
    prob = jnp.exp(scores - lse).astype(jnp.bfloat16)
    attn_list = [
        jnp.einsum("hqk,khd->qhd", prob, values_all[index], preferred_element_type=jnp.float32)
    ]
    lse_list = [lse]
    attn = jnp.stack(attn_list).reshape(images, slots_dev, width).astype(jnp.bfloat16)
    branch = jnp.dot(attn, wout, preferred_element_type=jnp.float32)
    x1 = xf + keep * gate1 * branch
    norm2, pull_norm2 = jax.vjp(rms, x1)
    h2 = (norm2 * (1.0 + scale2) + shift2).astype(jnp.bfloat16)
    gate_up = jnp.dot(h2, w12, preferred_element_type=jnp.float32)
    hidden = gate_up.shape[-1] // 2
    gate_part, up_part = (gate_up[..., :hidden], gate_up[..., hidden:])
    sig = jax.nn.sigmoid(gate_part)
    silu_gate = gate_part * sig
    mid = (silu_gate * up_part).astype(jnp.bfloat16)
    ffn = jnp.dot(mid, w3, preferred_element_type=jnp.float32)
    mixed = (x1 + keep * gate2 * ffn).astype(jnp.bfloat16)
    grad_out = cotangent.astype(jnp.float32)
    d_gate2 = jnp.sum(grad_out * keep * ffn, axis=1)
    d_ffn = (grad_out * keep * gate2).astype(jnp.bfloat16)
    term_down = outer_sum(mid, d_ffn)
    d_mid = times_transposed(d_ffn, w3)
    d_gate = d_mid * up_part * (sig + gate_part * sig * (1.0 - sig))
    d_up = d_mid * silu_gate
    d_gate_up = jnp.concatenate([d_gate, d_up], axis=-1).astype(jnp.bfloat16)
    term_up = outer_sum(h2, d_gate_up)
    d_h2 = times_transposed(d_gate_up, w12)
    d_scale2 = jnp.sum(d_h2 * norm2, axis=1)
    d_shift2 = jnp.sum(d_h2, axis=1)
    d_x1 = grad_out + pull_norm2(d_h2 * (1.0 + scale2))[0]
    d_gate1 = jnp.sum(d_x1 * keep * branch, axis=1)
    d_branch = (d_x1 * keep * gate1).astype(jnp.bfloat16)
    term_out = outer_sum(attn, d_branch)
    d_attn = (
        times_transposed(d_branch, wout)
        .astype(jnp.bfloat16)
        .reshape(images, slots_dev, HEADS, HEAD)
    )
    keys_back, values_back = (
        lax.all_gather(key_b, ("ty", "tx"), axis=1, tiled=True),
        lax.all_gather(value_b, ("ty", "tx"), axis=1, tiled=True),
    )
    index = 0
    scores = masked_scores(query_b[index], keys_back[index], valid_k[index])
    prob = jnp.exp(scores - lse_list[index])
    d_prob = jnp.einsum(
        "qhd,khd->hqk", d_attn[index], values_back[index], preferred_element_type=jnp.float32
    )
    delta = jnp.sum(prob * d_prob, axis=-1, keepdims=True)
    d_scores = (prob * (d_prob - delta)).astype(jnp.bfloat16)
    dq_list = [
        jnp.einsum("hqk,khd->qhd", d_scores, keys_back[index], preferred_element_type=jnp.float32)
    ]
    dk_list = [
        jnp.einsum("hqk,qhd->khd", d_scores, query_b[index], preferred_element_type=jnp.float32)
    ]
    dv_list = [
        jnp.einsum(
            "hqk,qhd->khd",
            prob.astype(jnp.bfloat16),
            d_attn[index],
            preferred_element_type=jnp.float32,
        )
    ]
    d_key, d_value = (
        lax.psum_scatter(
            jnp.stack(dk_list).astype(jnp.bfloat16), ("ty", "tx"), scatter_dimension=1, tiled=True
        ).astype(jnp.float32),
        lax.psum_scatter(
            jnp.stack(dv_list).astype(jnp.bfloat16), ("ty", "tx"), scatter_dimension=1, tiled=True
        ).astype(jnp.float32),
    )
    d_query_raw, d_key_raw, d_q_gain, d_k_gain = pull_heads((jnp.stack(dq_list), d_key))
    d_qkv = (
        jnp.stack([d_query_raw, d_key_raw, d_value], axis=2)
        .reshape(images, slots_dev, 3 * width)
        .astype(jnp.bfloat16)
    )
    term_qkv = outer_sum(h1, d_qkv)
    d_h1 = times_transposed(d_qkv, wqkv)
    d_scale1 = jnp.sum(d_h1 * norm1, axis=1)
    d_shift1 = jnp.sum(d_h1, axis=1)
    tokens_grad = (d_x1 + pull_norm1(d_h1 * (1.0 + scale1))[0]).astype(jnp.bfloat16)
    d_mod = jnp.concatenate([d_shift1, d_scale1, d_gate1, d_shift2, d_scale2, d_gate2], axis=1)
    act_f = act.astype(jnp.float32)
    ada_grad = lax.psum_scatter(
        lax.dot_general(
            d_mod,
            act_f,
            (((0,), (0,)), ((), ())),
            precision=HIGH,
            preferred_element_type=jnp.float32,
        ),
        ("img", "ty", "tx"),
        scatter_dimension=0,
        tiled=True,
    )
    q_gain_grad, k_gain_grad = lax.psum((d_q_gain, d_k_gain), ("img", "ty", "tx"))
    parts = (
        lax.psum_scatter(
            term_qkv.astype(jnp.bfloat16), ("ty", "tx"), scatter_dimension=1, tiled=True
        ).astype(jnp.float32),
        lax.psum_scatter(
            term_out.astype(jnp.bfloat16), ("ty", "tx"), scatter_dimension=1, tiled=True
        ).astype(jnp.float32),
        lax.psum_scatter(
            term_up.astype(jnp.bfloat16), ("ty", "tx"), scatter_dimension=1, tiled=True
        ).astype(jnp.float32),
        lax.psum_scatter(
            term_down.astype(jnp.bfloat16), ("ty", "tx"), scatter_dimension=1, tiled=True
        ).astype(jnp.float32),
    )
    grads = (
        lax.psum_scatter(
            parts[0].astype(jnp.bfloat16), "img", scatter_dimension=0, tiled=True
        ).astype(jnp.float32),
        lax.psum_scatter(
            parts[1].astype(jnp.bfloat16), "img", scatter_dimension=0, tiled=True
        ).astype(jnp.float32),
        lax.psum_scatter(
            parts[2].astype(jnp.bfloat16), "img", scatter_dimension=0, tiled=True
        ).astype(jnp.float32),
        lax.psum_scatter(
            parts[3].astype(jnp.bfloat16), "img", scatter_dimension=0, tiled=True
        ).astype(jnp.float32),
    )
    return (
        mixed,
        tokens_grad,
        grads[0],
        grads[1],
        grads[2],
        grads[3],
        ada_grad,
        q_gain_grad,
        k_gain_grad,
    )


VMEM_LIMIT = 63 << 20
MESH = pl.DeviceIdType.MESH
PAD = 128
TILE = 128
F32 = jnp.float32
BF16 = jnp.bfloat16


def dot(a, b):
    return lax.dot_general(a, b, (((1,), (0,)), ((), ())), preferred_element_type=F32)


def dot_nt(a, b):
    return lax.dot_general(a, b, (((1,), (1,)), ((), ())), preferred_element_type=F32)


def dot_tn(a, b, precision=None):
    return lax.dot_general(
        a, b, (((0,), (0,)), ((), ())), preferred_element_type=F32, precision=precision
    )


def lanes(shape):
    return lax.broadcasted_iota(jnp.int32, shape, len(shape) - 1)


def split3(value):
    high = value.astype(BF16)
    rest = value - high.astype(F32)
    mid = rest.astype(BF16)
    low = (rest - mid.astype(F32)).astype(BF16)
    return (high, mid, low)


def put_split3(tile, value, lane0):
    at = lanes(tile.shape)
    for k, term in enumerate(split3(value)):
        tile = jnp.where(at == lane0 + k, jnp.broadcast_to(term.astype(F32), tile.shape), tile)
    return tile


OUT, UP, DOWN, QKV = range(4)


def weight_chunks(width, hidden):
    half = width // 2
    quarter = hidden // 4
    rows = hidden // 4

    def up(k, along_z):
        return [(UP, 2 * k + u, 0, half, quarter, along_z) for u in range(2)]

    return (
        [(OUT, 0, 0, half, width, True)]
        + up(0, True)
        + up(1, False)
        + up(2, True)
        + [(DOWN, 0, 0, rows, width, False)]
        + up(3, True)
        + [(DOWN, 0, rows, rows, width, False)]
        + [(QKV, 0, 0, half, 14 * PAD, True), (QKV, 1, 0, half, 13 * PAD, False)]
    )


def block_kernel(
    tok, cot, act, ada, wh, wout, wup, wdown, wqkv, q_gain, k_gain, tab, hw,
    mixed, tgrad, qkv_grad, ada_grad, gain_grad, down_grad, up_grad, out_grad, qkv_hbm,
    lb_down, lb_up, lb_out, rb_down, rb_up, rb_out,
    tok_all, whv, woutv, wupv, wdownv, actbuf, modsend, modbuf, modv,
    cosv, sinv, qraw, kraw, qa, ka, va, kt, qt, onorm, attn_send, attn_in,
    do_in, dot_t, dqt, dkv, dvv, dqkv_in, dw_in, pc_in,
    x1v, branchv, ffnv, dh2v, dmod, dsend, dbuf,
    l_attn, l_h2, l_mid, r_ffn, r_branch, r_gu, l_h2s, l_attns, r_branchs,
    za_down, za_up, za_out, zb_down, zb_up, zb_out, z_out,
    gl_s, gl_r, gr_s, gr_r, g_loc, za_s, za_r, zb_s, zb_r, z_loc,
    tok_send, tok_recv, tok_loc, w_send, w_recv, w_loc, wh_sem, act_sem, mod_s, mod_r,
    at_s, at_r, do_s, do_r, dq_s, dq_r, dw_sem, pc_s, pc_r, dm_s, dm_r, loc,
):
    img, ty, z = lax.axis_index("img"), lax.axis_index("ty"), lax.axis_index("tx")
    b = ty * 4 + z
    me = img * 16 + b
    width = tok.shape[1]
    half = width // 2
    hidden = wup.shape[1] // 2
    part = ada.shape[0]
    other = 1 - img

    def dev(i=img, t=ty, k=z):
        return {"img": i, "ty": t, "tx": k}

    def dev_flat(p):
        return dev(p // 16, lax.rem(p // 4, 4), lax.rem(p, 4))

    def dev_tile(t):
        return dev(img, t // 4, lax.rem(t, 4))

    def rcopy(src, dst, s, r, d):
        return pltpu.make_async_remote_copy(
            src_ref=src, dst_ref=dst, send_sem=s, recv_sem=r, device_id=d, device_id_type=MESH
        )

    def loop(lo, hi, f):
        def step(k, c):
            f(k)
            return c

        lax.fori_loop(lo, hi, step, 0)

    bar = pltpu.get_barrier_semaphore()
    loop(
        1, 32,
        lambda k: pl.semaphore_signal(
            bar, inc=1, device_id=dev_flat(lax.rem(me + k, 32)), device_id_type=MESH
        ),
    )
    pl.semaphore_wait(bar, 31)

    hbm = (wout, wup, wdown, wqkv)
    vm = (woutv, wupv, wdownv, qkv_hbm)
    chunks = weight_chunks(width, hidden)

    z_bit = lax.rem(z, 2)

    def w_col(i, im):
        m, k = chunks[i][:2]
        if m == UP:
            return (k % 2) * hidden + lax.rem(2 * im + k // 2, 4) * (hidden // 4)
        return k * 14 * PAD

    def w_own(i):
        return 2 * z_bit + lax.rem(ty, 2) if chunks[i][5] else ty

    def w_hop(i):
        return dev(k=z ^ 1) if chunks[i][5] else dev(t=ty ^ 2)

    def w_piece(ref, i, row0, im, p):
        _, _, r0, rows, cols, _ = chunks[i]
        n = rows // 4
        return ref.at[
            pl.ds(pl.multiple_of(row0 + r0 + p * n, 16), n),
            pl.ds(pl.multiple_of(w_col(i, im), PAD), cols),
        ]

    def wregion(i, owner, im, p):
        m = chunks[i][0]
        return w_piece(vm[m], i, owner * hbm[m].shape[0], im, p)

    def w_x(i):
        p = w_own(i)
        src = w_piece(hbm[chunks[i][0]], i, 0, other, p)
        dst = wregion(i, img, other, p)
        return rcopy(src, dst, w_send.at[i, 0], w_recv.at[i, p], dev(i=other))

    def w_mine(i, p):
        return wregion(i, other, img, p)

    def w_y(i):
        ref = w_mine(i, w_own(i))
        return rcopy(ref, ref, w_send.at[i, 1], w_recv.at[i, w_own(i)], w_hop(i))

    def w_c(i, p, slot):
        ref = w_mine(i, p)
        return rcopy(ref, ref, w_send.at[i, slot], w_recv.at[i, p], dev(t=ty ^ 1))

    def w_wait(i, p):
        ref = w_mine(i, p)
        rcopy(ref, ref, w_send.at[i, 0], w_recv.at[i, p], dev(t=ty ^ 1)).wait_recv()

    def x_arrived(*which):
        for i in which:
            w_wait(i, w_own(i))
            w_y(i).start()
            w_c(i, w_own(i), 2).start()

    def hop_arrived(*which):
        for i in which:
            w_wait(i, w_own(i) ^ 2)
            w_c(i, w_own(i) ^ 2, 3).start()

    def w_done(*which):
        for i in which:
            w_wait(i, w_own(i) ^ 1)
            w_wait(i, w_own(i) ^ 3)

    def w_drain(i):
        w_x(i).wait_send()
        w_y(i).wait_send()
        w_c(i, w_own(i), 2).wait_send()
        w_c(i, w_own(i) ^ 2, 3).wait_send()

    def own(m):
        rows = hbm[m].shape[0]
        return pltpu.make_async_copy(hbm[m], vm[m].at[pl.ds(img * rows, rows)], w_loc.at[m])

    act_copy = rcopy(act, actbuf.at[img], act_sem.at[0], act_sem.at[1], dev(i=other))
    act_copy.start()
    actbuf[img] = act[...]
    wh_copy = rcopy(wh, whv.at[pl.ds(img * half, half)], wh_sem.at[0], wh_sem.at[1], dev(i=other))
    w_x(0).start()
    whv[pl.ds(pl.multiple_of(img * half, 64), half), :] = wh[...]

    def tok_at(chunk):
        return tok_all.at[pl.ds(pl.multiple_of(chunk * TILE, TILE), TILE)]

    def t_send(src, chunk, way, d):
        return rcopy(src, tok_at(chunk), tok_send.at[chunk, way], tok_recv.at[chunk], d)

    def t_wait(chunk):
        t_send(tok, chunk, 0, dev(t=ty ^ 1)).wait_recv()

    tok_own = pltpu.make_async_copy(tok, tok_at(b), tok_loc)
    tok_own.start()

    def t_forward(src, chunk, up, down):
        if up:

            @pl.when(z < 3)
            def _():
                t_send(src, chunk, 0, dev(k=z + 1)).start()

        if down:

            @pl.when(z > 0)
            def _():
                t_send(src, chunk, 1, dev(k=z - 1)).start()

        t_send(src, chunk, 2, dev(t=ty ^ 2)).start()
        t_send(src, chunk, 3, dev(t=ty ^ 1)).start()

    t_forward(tok, b, True, True)
    for m in range(3):
        own(m).start()

    act_copy.wait_recv()
    for i in range(2):
        modsend[i, :, 0:part] = dot_nt(actbuf[i].astype(BF16), ada[...])

    def mod_copy(p):
        return rcopy(modsend.at[p // 16], modbuf.at[me], mod_s.at[p], mod_r.at[me], dev_flat(p))

    loop(1, 32, lambda k: mod_copy(lax.rem(me + k, 32)).start())
    modbuf[me] = modsend[img]
    wh_copy.start()
    for i in range(1, len(chunks)):
        w_x(i).start()

    for s in (1, 2, 3):

        @pl.when(z - s >= 0)
        def _():
            t_wait(b - s)
            t_forward(tok_at(b - s), b - s, True, False)

        @pl.when(z + s <= 3)
        def _():
            t_wait(b + s)
            t_forward(tok_at(b + s), b + s, False, True)

    x_arrived(0)

    def t_y(zz):
        chunk = (ty ^ 2) * 4 + zz
        t_wait(chunk)
        t_send(tok_at(chunk), chunk, 3, dev(t=ty ^ 1)).start()

    loop(0, 4, t_y)
    x_arrived(1, 2)
    loop(0, 4, lambda zz: t_wait((ty ^ 1) * 4 + zz))
    loop(0, 4, lambda zz: t_wait((ty ^ 3) * 4 + zz))

    def t_drain(zz):
        chunk = ty * 4 + zz
        ref = tok_at(chunk)

        @pl.when((zz <= z) & (z < 3))
        def _():
            t_send(ref, chunk, 0, dev(t=ty ^ 1)).wait_send()

        @pl.when((zz >= z) & (z > 0))
        def _():
            t_send(ref, chunk, 1, dev(t=ty ^ 1)).wait_send()

        t_send(ref, chunk, 2, dev(t=ty ^ 1)).wait_send()
        t_send(ref, chunk, 3, dev(t=ty ^ 1)).wait_send()
        away = (ty ^ 2) * 4 + zz
        t_send(tok_at(away), away, 3, dev(t=ty ^ 1)).wait_send()

    loop(0, 4, t_drain)
    tok_own.wait()

    def mod_wait(k):
        p = lax.rem(me + k, 32)
        rcopy(
            modsend.at[0], modbuf.at[p], mod_s.at[p], mod_r.at[p], dev_flat(p)
        ).wait()

    loop(1, 32, mod_wait)
    for s in range(32):
        modv[:, s * part : (s + 1) * part] = modbuf[s, :, 0:part]
    shift1, scale1, gate1, shift2, scale2, gate2 = [
        functools.partial(lambda k: modv[0:1, k * width : (k + 1) * width], k) for k in range(6)
    ]
    wh_copy.wait()

    height, wide = hw[0], hw[1]
    local = lax.broadcasted_iota(jnp.int32, (TILE, PAD), 0)
    lane = lax.broadcasted_iota(jnp.int32, (TILE, PAD), 1)

    def tile_layout(t):
        row_tile, col_tile = t // 4, lax.rem(t, 4)
        top = row_tile * height // 4
        rows = (row_tile + 1) * height // 4 - top
        left = col_tile * wide // 4
        span = (col_tile + 1) * wide // 4 - left
        spans = jnp.full((TILE, PAD), span, jnp.int32)
        quot = jnp.floor((local.astype(F32) + 0.5) / spans.astype(F32)).astype(jnp.int32)
        valid = local < jnp.full((TILE, PAD), rows * span, jnp.int32)
        row = jnp.where(valid, top + quot, 0)
        col = jnp.where(valid, left + local - quot * spans, 0)
        return valid, row, col

    def rope(n, c, s1, s2):
        return n * c + pltpu.roll(n, PAD - 18, 1) * s1 + pltpu.roll(n, 18, 1) * s2

    def unrope(d, c, s1, s2):
        return d * c + pltpu.roll(d * s1, 18, 1) + pltpu.roll(d * s2, PAD - 18, 1)

    def split_sin(sine):
        first = (lane < 18) | ((lane >= 36) & (lane < 54))
        return jnp.where(first, -sine, 0.0), jnp.where(first, 0.0, sine)

    def head_rows(t):
        valid, row, col = tile_layout(t)
        hot = jnp.where((lane == row) | (lane - 64 == col), 1.0, 0.0)
        angles = lax.dot_general(
            hot, tab[...], (((1,), (0,)), ((), ())),
            precision=HIGH, preferred_element_type=F32,
        )
        c, sine = angles[:, 0:PAD], angles[:, PAD : 2 * PAD]
        cosv[t] = c
        sinv[t] = sine
        s1, s2 = split_sin(sine)
        at = pl.ds(pl.multiple_of(t * TILE, TILE), TILE)
        x = tok_all[at, :].astype(F32)
        r = lax.rsqrt(jnp.mean(x * x, axis=1, keepdims=True) + EPS)
        h1 = ((x * r) * (1.0 + scale1()) + shift1()).astype(BF16)
        tok_all[at, :] = h1
        qkv = dot(h1, whv[...])
        q_r, k_r, v_r = qkv[:, 0:PAD], qkv[:, PAD : 2 * PAD], qkv[:, 2 * PAD : 3 * PAD]
        qraw[t] = q_r
        kraw[t] = k_r

        def normed(v, gain):
            rr = lax.rsqrt(jnp.sum(v * v, axis=1, keepdims=True) * (1.0 / HEAD) + EPS)
            return v * rr * gain[0:1, :]

        q_f = rope(normed(q_r, q_gain), c, s1, s2) * HEAD ** (-0.5)
        k_f = rope(normed(k_r, k_gain), c, s1, s2)
        qa[t] = jnp.where(lane == HEAD, 1.0, q_f).astype(BF16)
        k_f = jnp.where(lane == HEAD, jnp.where(valid, 0.0, -30000.0), k_f)
        k_f = jnp.where((lane > HEAD) & (lane < HEAD + 4), 1.0, k_f)
        ka[t] = k_f.astype(BF16)
        kt[:, pl.ds(pl.multiple_of(t * TILE, TILE), TILE)] = k_f.T.astype(BF16)
        va[t] = jnp.where((lane >= HEAD) & (lane < HEAD + 3), 1.0, v_r).astype(BF16)

    hop_arrived(0)
    loop(0, 8, head_rows)
    x_arrived(3, 4)
    loop(8, 16, head_rows)
    hop_arrived(1, 2)
    x_arrived(5, 6)

    def head_lanes(h):
        return attn_in.at[:, pl.ds(pl.multiple_of(h * PAD, PAD), PAD)]

    def at_copy(t):
        return rcopy(attn_send.at[t], head_lanes(b), at_s.at[t], at_r.at[b], dev_tile(t))

    def attend(k):
        q2 = qa[pl.ds(2 * k, 2)].reshape(2 * TILE, PAD)
        p = jnp.exp(dot(q2, kt[...])).astype(BF16)
        o = dot(p, va[...].reshape(16 * TILE, PAD))
        total = o[:, HEAD : HEAD + 1]
        o = o / total
        lse = jnp.log(total)
        q3 = put_split3(q2.astype(F32), -lse, HEAD + 1)
        o16 = o.astype(BF16)
        for u in range(2):
            t = 2 * k + u
            rows = slice(u * TILE, (u + 1) * TILE)
            onorm[t] = o[rows]
            qa[t] = q3[rows].astype(BF16)
            qt[:, pl.ds(pl.multiple_of(t * TILE, TILE), TILE)] = q3[rows].T.astype(BF16)
            attn_send[t] = o16[rows]

            @pl.when(t != b)
            def _():
                at_copy(t).start()

    loop(0, 4, attend)
    x_arrived(7)
    hop_arrived(3, 4)
    loop(4, 8, attend)
    head_lanes(b)[...] = attn_send[b]
    x_arrived(8, 9)

    def at_wait(k):
        p = lax.rem(b + k, 16)
        rcopy(attn_send.at[p], head_lanes(p), at_s.at[p], at_r.at[p], dev_tile(p)).wait()

    loop(1, 16, at_wait)

    def put_halves(ref, value):
        pad = jnp.zeros((TILE, 5 * PAD - half), F32)
        for k in range(2):
            piece = jnp.concatenate([value[:, k * half : (k + 1) * half], pad], axis=1)
            ref[:, k * 5 * PAD : (k + 1) * 5 * PAD] = piece.astype(BF16)

    def put_blocks(ref, value):
        pad = jnp.zeros((TILE, PAD - HEAD), F32)
        for k in range(16):
            zz = k % 4
            to = 4 * (k // 4) + 2 * (zz % 2) + zz // 2
            piece = jnp.concatenate([value[:, k * HEAD : (k + 1) * HEAD], pad], axis=1)
            ref[:, to * PAD : (to + 1) * PAD] = piece.astype(BF16)

    l_src, l_all = (l_mid, l_h2s, l_attns), (lb_down, lb_up, lb_out)
    r_src, r_all = (attn_in, r_gu, r_branchs), (rb_down, rb_up, rb_out)
    y, c = ty // 2, lax.rem(ty, 2)

    def slot_rows(i, t):
        return pl.ds(pl.multiple_of((i * 4 + t) * TILE, TILE), TILE)

    def lanes_at(k, n):
        return pl.ds(pl.multiple_of(k * n, PAD), n)

    def g_left(m, k, src, i, t, d):
        dst = l_all[m].at[slot_rows(i, t)]
        return rcopy(dst if src is None else src, dst, gl_s.at[m, k], gl_r.at[m, i * 4 + t], d)

    def g_right(m, k, src, i, t, d):
        n = r_src[m].shape[1] // 4
        dst = r_all[m].at[slot_rows(i, t)]
        if k in (2, 4, 5, 6):
            dst = r_all[m].at[slot_rows(i, t), lanes_at(1 - c, n)]
        return rcopy(dst if src is None else src, dst, gr_s.at[m, k], gr_r.at[m, i * 4 + t], d)

    to_x, to_y, to_c = dev(i=other), dev(t=ty ^ 2), dev(t=ty ^ 1)

    def l_part(m, k):
        return l_src[m].at[:, lanes_at(k, l_src[m].shape[1] // 2)]

    def r_part(m, k, n):
        return r_src[m].at[:, lanes_at(k, n * (r_src[m].shape[1] // 4))]

    def g_first(m):
        return [
            g_left(m, 0, l_part(m, other), img, ty, to_x),
            g_right(m, 0, r_part(m, 1 - y, 2), img, ty, to_y),
            g_left(m, 1, l_part(m, img), img, ty, to_y),
            g_right(m, 1, r_part(m, y, 2), img, ty, to_x),
            g_left(m, 2, l_part(m, img), img, ty, to_c),
            g_right(m, 2, r_part(m, ty ^ 1, 1), img, ty, to_c),
        ]

    def g_own(m):
        n = r_src[m].shape[1] // 4
        rows = slot_rows(img, ty)
        return [
            pltpu.make_async_copy(l_part(m, img), l_all[m].at[rows], g_loc.at[m, 0]),
            pltpu.make_async_copy(
                r_part(m, ty, 1), r_all[m].at[rows, lanes_at(c, n)], g_loc.at[m, 1]
            ),
        ]

    def g_x(m):
        for k in (0, 3):
            g_first(m)[k].start()

    def g_yc(m):
        for k in (1, 2, 4, 5):
            g_first(m)[k].start()
        for copy in g_own(m):
            copy.start()

    def g_hop(m):
        g_left(m, 0, None, other, ty, to_x).wait_recv()
        g_left(m, 3, None, other, ty, to_y).start()
        g_left(m, 4, None, other, ty, to_c).start()
        g_right(m, 0, None, img, ty ^ 2, to_y).wait_recv()
        g_right(m, 3, None, img, ty ^ 2, to_x).start()
        g_right(m, 4, None, img, ty ^ 2, to_c).start()
        g_left(m, 1, None, img, ty ^ 2, to_y).wait_recv()
        g_left(m, 5, None, img, ty ^ 2, to_c).start()
        g_right(m, 1, None, other, ty, to_x).wait_recv()
        g_right(m, 5, None, other, ty, to_c).start()

    def g_hop2(m):
        g_left(m, 3, None, other, ty ^ 2, to_y).wait_recv()
        g_left(m, 6, None, other, ty ^ 2, to_c).start()
        g_right(m, 3, None, other, ty ^ 2, to_x).wait_recv()
        g_right(m, 6, None, other, ty ^ 2, to_c).start()

    def g_done(m):
        n = r_src[m].shape[1] // 4
        for i in range(2):
            for t in (ty ^ 1, ty ^ 3):
                g_left(m, 2, None, i, t, to_c).wait_recv()
                ref = r_all[m].at[slot_rows(i, t), lanes_at(c, n)]
                rcopy(ref, ref, gr_s.at[m, 2], gr_r.at[m, i * 4 + t], to_c).wait_recv()
        for copy in g_own(m):
            copy.wait()

    def g_drain(m):
        for copy in g_first(m):
            copy.wait_send()
        for k, i, t in ((3, other, ty), (4, other, ty), (5, img, ty ^ 2), (6, other, ty ^ 2)):
            g_left(m, k, None, i, t, to_c).wait_send()
        for k, i, t in ((3, img, ty ^ 2), (4, img, ty ^ 2), (5, other, ty), (6, other, ty ^ 2)):
            g_right(m, k, None, i, t, to_c).wait_send()

    attn = jnp.concatenate(
        [attn_in[:, h * PAD : h * PAD + HEAD].astype(F32) for h in range(16)], axis=1
    )
    l_attn[...] = attn.astype(BF16)
    put_halves(l_attns, attn)
    hop_arrived(5, 6)
    own(OUT).wait()
    w_done(0)
    own_valid = tile_layout(b)[0]
    keep = jnp.where(own_valid, 1.0, 0.0)[:, 0:1]
    cols = width // 3

    def project(k):
        at = pl.ds(pl.multiple_of(k * cols, PAD), cols)
        branchv[:, at] = dot(l_attn[...], woutv[:, at])

    loop(0, 3, project)
    x_arrived(10)
    x = tok[...].astype(F32)
    x1 = x + keep * gate1() * branchv[...]
    x1v[...] = x1
    r = lax.rsqrt(jnp.mean(x1 * x1, axis=1, keepdims=True) + EPS)
    h2_rows = (x1 * r) * (1.0 + scale2()) + shift2()
    l_h2[...] = h2_rows.astype(BF16)
    put_halves(l_h2s, h2_rows)
    d_ffn = cot[...].astype(F32) * keep * gate2()
    r_ffn[...] = d_ffn.astype(BF16)
    put_blocks(attn_in, d_ffn)
    ffnv[...] = jnp.zeros_like(ffnv)
    dh2v[...] = jnp.zeros_like(dh2v)
    own(UP).wait()
    own(DOWN).wait()
    step = 256

    def mlp(j):
        g_at = pl.ds(pl.multiple_of(j, step), step)
        u_at = pl.ds(pl.multiple_of(hidden + j, step), step)
        h2 = l_h2[...]
        gate = dot(h2, wupv[:, g_at])
        up = dot(h2, wupv[:, u_at])
        sig = 1.0 / (1.0 + jnp.exp(-gate))
        act_g = gate * sig
        mid = (act_g * up).astype(BF16)
        l_mid[:, g_at] = mid
        w3 = wdownv[g_at, :]
        ffnv[...] += dot(mid, w3)
        d_mid = dot_nt(r_ffn[...], w3)
        d_gate = (d_mid * up * (sig + gate * sig * (1.0 - sig))).astype(BF16)
        d_up = (d_mid * act_g).astype(BF16)
        r_gu[:, g_at] = d_gate
        r_gu[:, u_at] = d_up
        dh2v[...] += dot_nt(d_gate, wupv[:, g_at]) + dot_nt(d_up, wupv[:, u_at])

    def mlp_quarter(k):
        first = lax.rem(2 * img + k, 4) * (hidden // 4)
        loop(0, hidden // 4 // step, lambda j: mlp(first + j * step))

    w_done(1, 2)
    mlp_quarter(0)
    hop_arrived(7, 8, 9)
    w_done(3, 4)
    mlp_quarter(1)
    hop_arrived(10)
    w_done(5, 6, 7)
    mlp_quarter(2)
    w_done(8, 9, 10)
    mlp_quarter(3)
    g_x(1)
    ffn = ffnv[...]
    g = cot[...].astype(F32)
    x1 = x1v[...]
    mixed[...] = (x1 + keep * gate2() * ffn).astype(BF16)

    def dmod_put(k, row):
        dmod[0:1, k * width : (k + 1) * width] = row

    def colsum(v):
        return jnp.sum(v, axis=0, keepdims=True)

    dmod_put(5, colsum(g * keep * ffn))
    d_h2 = dh2v[...]
    norm2 = x1 * r
    dmod_put(4, colsum(d_h2 * norm2))
    dmod_put(3, colsum(d_h2))
    d_n2 = d_h2 * (1.0 + scale2())
    d_x1 = g + r * (d_n2 - norm2 * jnp.mean(d_n2 * norm2, axis=1, keepdims=True))
    dmod_put(2, colsum(d_x1 * keep * branchv[...]))
    x1v[...] = d_x1
    d_branch = d_x1 * keep * gate1()
    r_branch[...] = d_branch.astype(BF16)
    put_blocks(r_branchs, d_branch)

    def unproject(k):
        at = pl.ds(pl.multiple_of(k * cols, PAD), cols)
        branchv[:, at] = dot_nt(r_branch[...], woutv[at, :])

    loop(0, 3, unproject)

    zeros = jnp.zeros((TILE, PAD - HEAD), F32)
    d_attn = branchv[...]
    for h in range(16):
        attn_send[h] = jnp.concatenate(
            [d_attn[:, h * HEAD : (h + 1) * HEAD], zeros], axis=1
        ).astype(BF16)

    def do_copy(t):
        return rcopy(attn_send.at[t], do_in.at[b], do_s.at[t], do_r.at[b], dev_tile(t))

    loop(1, 16, lambda k: do_copy(lax.rem(b + k, 16)).start())
    do_in[b] = attn_send[b]
    g_yc(1)
    x_arrived(11, 12)

    def do_wait(k):
        p = lax.rem(b + k, 16)
        rcopy(attn_send.at[p], do_in.at[p], do_s.at[p], do_r.at[p], dev_tile(p)).wait()

    loop(1, 16, do_wait)
    hop_arrived(11, 12)

    def delta(t):
        d = do_in[t].astype(F32)
        dsum = jnp.sum(jnp.where(lane < HEAD, d * onorm[t], 0.0), axis=1, keepdims=True)
        d = put_split3(d, -dsum, HEAD)
        do_in[t] = d.astype(BF16)
        dot_t[:, pl.ds(pl.multiple_of(t * TILE, TILE), TILE)] = d.T.astype(BF16)

    loop(0, 16, delta)
    dqt[...] = jnp.zeros_like(dqt)

    def attend_back(k):
        two = pl.ds(2 * k, 2)
        p = jnp.exp(dot(ka[two].reshape(2 * TILE, PAD), qt[...]))
        ds = (p * dot(va[two].reshape(2 * TILE, PAD), dot_t[...])).astype(BF16)
        dkv[two] = dot(ds, qa[...].reshape(16 * TILE, PAD)).reshape(2, TILE, PAD)
        dvv[two] = dot(p.astype(BF16), do_in[...].reshape(16 * TILE, PAD)).reshape(2, TILE, PAD)
        at = pl.ds(pl.multiple_of(k * 2 * TILE, 2 * TILE), 2 * TILE)
        dqt[...] += dot(kt[:, at], ds)

    loop(0, 4, attend_back)
    g_hop(1)
    g_x(0)
    g_x(2)
    loop(4, 8, attend_back)

    w_done(11, 12)
    for i in range(len(chunks)):
        w_drain(i)
    gain_grad[...] = jnp.zeros_like(gain_grad)

    def dq_rows(t):
        return wdownv.at[pl.ds(pl.multiple_of(t * TILE, TILE), TILE), pl.ds(3 * PAD, 2 * PAD)]

    def dq_copy(t):
        return rcopy(dq_rows(t), dqkv_in.at[b], dq_s.at[t], dq_r.at[b], dev_tile(t))

    def heads_back(t):
        c = cosv[t]
        s1, s2 = split_sin(sinv[t])

        def norm_back(d, v, gain, row):
            rr = lax.rsqrt(jnp.sum(v * v, axis=1, keepdims=True) * (1.0 / HEAD) + EPS)
            n = v * rr
            gain_grad[row : row + 1, :] += colsum(d * n)
            dn = d * gain[0:1, :]
            return rr * (dn - n * (jnp.sum(dn * n, axis=1, keepdims=True) * (1.0 / HEAD)))

        d_q = dqt[:, pl.ds(pl.multiple_of(t * TILE, TILE), TILE)].T * HEAD ** (-0.5)
        d_q = norm_back(unrope(d_q, c, s1, s2), qraw[t], q_gain, 0)
        d_k = norm_back(unrope(dkv[t], c, s1, s2), kraw[t], k_gain, 1)
        d_v = jnp.where(lane < HEAD, dvv[t], 0.0)
        at = pl.ds(pl.multiple_of(t * TILE, TILE), TILE)
        wdownv[at, 0 : 3 * PAD] = jnp.concatenate([d_q, d_k, d_v], axis=1).astype(BF16)
        wdownv[at, 3 * PAD : 5 * PAD] = jnp.concatenate(
            [d_q[:, 0:HEAD], d_k[:, 0:HEAD], d_v[:, 0:HEAD], zeros[:, 0:40]], axis=1
        ).astype(BF16)

        @pl.when(t != b)
        def _():
            dq_copy(t).start()

    loop(0, 16, heads_back)
    dqkv_in[b] = dq_rows(b)[...]
    g_yc(0)
    g_yc(2)

    high, low = z // 2, lax.rem(z, 2)
    l0 = 3 * width

    def z_load(m):
        kl, n = l_all[m].shape[1], r_src[m].shape[1] // 4
        copies = [
            pltpu.make_async_copy(
                l_all[m], wupv.at[pl.ds(0, 8 * TILE), pl.ds(l0, kl)], z_loc.at[0]
            ),
            pltpu.make_async_copy(
                r_all[m].at[:, lanes_at(c, n)],
                wupv.at[pl.ds(0, 8 * TILE), pl.ds(l0 + kl, n)],
                z_loc.at[1],
            ),
        ]
        for copy in copies:
            copy.start()
        for copy in copies:
            copy.wait()

    def z_copies(m):
        if m == 0:
            sent = [kt.at[pl.ds(0, 80), pl.ds(0, 12 * PAD)], qt.at[pl.ds(0, 80), pl.ds(0, 12 * PAD)]]
        elif m == 1:
            sent = [tok_all.at[pl.ds(0, half), pl.ds(k * 3 * PAD, 3 * PAD)] for k in range(2)]
        else:
            sent = [tok_all.at[pl.ds(640 + 128 * k, 80), pl.ds(0, 5 * PAD)] for k in range(2)]
        return [
            rcopy(sent[k], za[m].at[k], za_s.at[m, k], za_r.at[m, k], dev(k=z ^ 1))
            for k in range(2)
        ]

    za, zb = (za_down, za_up, za_out), (zb_down, zb_up, zb_out)
    z_rest = (
        dot_t.at[pl.ds(0, 80), pl.ds(0, 12 * PAD)],
        tok_all.at[pl.ds(0, half), pl.ds(6 * PAD, 3 * PAD)],
        tok_all.at[pl.ds(896, 80), pl.ds(0, 5 * PAD)],
    )
    z_own = (dqt.at[pl.ds(0, 80), pl.ds(0, 12 * PAD)], up_grad, z_out)

    def z_copy2(m):
        return rcopy(z_rest[m], zb[m], zb_s.at[m], zb_r.at[m], dev(k=z ^ 2))

    def z_product(m):
        kl = l_all[m].shape[1]
        sent = [copy.src_ref for copy in z_copies(m)]
        if m == 1:

            def turn(k):
                at = pl.ds(pl.multiple_of(k * TILE, TILE), TILE)
                woutv[0 : 5 * PAD, at] = wupv[at, l0 : l0 + kl].astype(F32).T.astype(BF16)

            loop(0, 8, turn)

            def block(zz):
                at = pl.ds(pl.multiple_of(l0 + kl + zz * 3 * PAD, PAD), 3 * PAD)
                return dot(woutv[0:half, 0 : 8 * TILE], wupv[0 : 8 * TILE, at])

            for k in range(2):
                sent[k][...] = block(2 * k + 1 - low).astype(BF16)
            for copy in z_copies(m):
                copy.start()
            z_rest[m][...] = block(2 * (1 - high) + low).astype(BF16)
            z_own[m][...] = block(z)
            return

        def pair(k):
            at = pl.ds(pl.multiple_of(l0 + kl + k * 2 * PAD, PAD), 2 * PAD)
            return dot_tn(wupv[0 : 8 * TILE, at], wupv[0 : 8 * TILE, l0 : l0 + kl])

        both = pair(1 - low)
        for k in range(2):
            sent[k][...] = both[k * PAD : k * PAD + 80].astype(BF16)
        for copy in z_copies(m):
            copy.start()
        both = pair(low)
        first, second = both[0:80], both[PAD : PAD + 80]
        z_rest[m][...] = jnp.where(high == 0, second, first).astype(BF16)
        z_own[m][...] = jnp.where(high == 0, first, second)

    def z_second(m):
        for copy in z_copies(m):
            copy.wait()
        rest = z_rest[m][...].astype(F32) + za[m][1 - high].astype(F32)
        z_rest[m][...] = rest.astype(BF16)
        z_copy2(m).start()
        z_own[m][...] += za[m][high].astype(F32)

    def z_last(m):
        z_copy2(m).wait()
        z_own[m][...] += zb[m][...].astype(F32)

    sums_t = (branchv, ffnv, dh2v)
    for ref in sums_t:
        ref[...] = jnp.zeros((PAD, width), F32)

    def dw_rows(k):
        at = pl.ds(pl.multiple_of(k * 2 * TILE, TILE), 2 * TILE)
        term = dot_tn(wdownv[at, 0 : 3 * PAD], tok_all[at, :])
        for p in range(3):
            sums_t[p][...] += term[p * PAD : (p + 1) * PAD]

    loop(0, 8, dw_rows)
    for p in range(3):
        wdownv[0:width, (5 + p) * PAD : (6 + p) * PAD] = sums_t[p][...].T.astype(BF16)

    def dw_half(i):
        return wdownv.at[pl.ds(pl.multiple_of(i * half, 64), half), pl.ds(5 * PAD, 3 * PAD)]

    dw_copy = rcopy(dw_half(other), dw_in, dw_sem.at[0], dw_sem.at[1], dev(i=other))
    dw_copy.start()
    g_hop2(1)
    g_done(1)
    z_load(1)
    z_product(1)
    g_hop(0)
    g_hop(2)

    loads = [
        pltpu.make_async_copy(
            src, wupv.at[pl.ds(owner * half, half), pl.ds(0, 3 * width)], loc.at[k]
        )
        for k, (src, owner) in enumerate(
            ((wqkv, img), (qkv_hbm.at[pl.ds(other * half, half)], other))
        )
    ]
    for load in loads:
        load.start()

    def dq_wait(k):
        p = lax.rem(b + k, 16)
        rcopy(dq_rows(p), dqkv_in.at[p], dq_s.at[p], dq_r.at[p], dev_tile(p)).wait()

    loop(1, 16, dq_wait)
    for load in loads:
        load.wait()
    dqkv = [dqkv_in[h].astype(F32) for h in range(16)]
    def own_part(p):
        return slice(16 * TILE + p * TILE, 16 * TILE + (p + 1) * TILE)

    for p in range(3):
        wdownv[own_part(p), :] = jnp.concatenate(
            [dqkv[h][:, p * HEAD : (p + 1) * HEAD] for h in range(16)], axis=1
        ).astype(BF16)

    def h1_back(k):
        at = pl.ds(pl.multiple_of(k * cols, PAD), cols)
        dh2v[:, at] = sum(
            dot_nt(wdownv[own_part(p), :], wupv[at, p * width : (p + 1) * width])
            for p in range(3)
        )

    loop(0, 3, h1_back)
    d_h1 = dh2v[...]
    x = tok[...].astype(F32)
    r1 = lax.rsqrt(jnp.mean(x * x, axis=1, keepdims=True) + EPS)
    norm1 = x * r1
    dmod_put(1, colsum(d_h1 * norm1))
    dmod_put(0, colsum(d_h1))
    d_n1 = d_h1 * (1.0 + scale1())
    back = r1 * (d_n1 - norm1 * jnp.mean(d_n1 * norm1, axis=1, keepdims=True))
    tgrad[...] = (x1v[...] + back).astype(BF16)

    dsend[...] = jnp.zeros_like(dsend)
    for s in range(32):
        dsend[s, 0:1, 0:part] = dmod[0:1, s * part : (s + 1) * part]
        dsend[s, 1:3, 0:PAD] = gain_grad[0:2, :]

    def dm_copy(p):
        return rcopy(dsend.at[p], dbuf.at[me], dm_s.at[p], dm_r.at[me], dev_flat(p))

    loop(1, 32, lambda k: dm_copy(lax.rem(me + k, 32)).start())
    dbuf[me] = dsend[me]

    z_second(1)
    for m in (0, 2):
        g_hop2(m)
        g_done(m)
        z_load(m)
        z_product(m)
    dw_copy.wait()
    dw_sum = dw_half(img)[...].astype(F32) + dw_in[...].astype(F32)

    def pc_send(p):
        return wdownv.at[pl.ds(width, half), pl.ds((5 + p) * PAD, PAD)]

    for p in range(3):
        pc_send(p)[...] = dw_sum[:, p * PAD : (p + 1) * PAD].astype(BF16)

    def pc_copy(p):
        group = 16 * p + b
        to, slot = group // 3, lax.rem(group, 3)
        return to, rcopy(
            pc_send(p), pc_in.at[slot], pc_s.at[p], pc_r.at[slot], dev_tile(to)
        )

    for p in range(3):
        to, copy = pc_copy(p)

        @pl.when(to != b)
        def _():
            copy.start()

        @pl.when(to == b)
        def _():
            pc_in[lax.rem(16 * p + b, 3)] = pc_send(p)[...]

    for m in (0, 2):
        z_second(m)
    for m in (1, 0, 2):
        z_last(m)
    for m in range(3):
        g_drain(m)
    down_grad[...] = z_own[0][0:HEAD, :]
    out_grad[...] = z_own[2][0:HEAD, 0:half]
    for slot in range(3):
        group = 3 * b + slot
        src = lax.rem(group, 16)

        @pl.when(src != b)
        def _():
            rcopy(
                pc_send(0), pc_in.at[slot], pc_s.at[0], pc_r.at[slot], dev_tile(src)
            ).wait_recv()

    for slot in range(3):
        at = slice(slot * HEAD, (slot + 1) * HEAD)
        qkv_grad[at, :] = pc_in[slot].astype(F32).T[0:HEAD, :]
    for p in range(3):
        to, copy = pc_copy(p)

        @pl.when(to != b)
        def _():
            copy.wait_send()

    def dm_wait(k):
        p = lax.rem(me + k, 32)
        rcopy(dsend.at[p], dbuf.at[p], dm_s.at[p], dm_r.at[p], dev_flat(p)).wait()

    loop(1, 32, dm_wait)
    sums = [
        lax.fori_loop(1, 16, lambda s, a, i=i: a + dbuf[16 * i + s], dbuf[16 * i])
        for i in range(2)
    ]
    gain_grad[...] = jnp.where(
        lax.broadcasted_iota(jnp.int32, (8, PAD), 0) < 2,
        pltpu.roll(sums[0] + sums[1], 7, 0)[:, 0:PAD],
        0.0,
    )
    row = lax.broadcasted_iota(jnp.int32, (8, 2 * PAD), 0)
    d_two = jnp.where(row == 0, sums[0][0:1, :], jnp.where(row == 1, sums[1][0:1, :], 0.0))
    row = lax.broadcasted_iota(jnp.int32, (8, width), 0)
    a_two = jnp.where(row == 0, actbuf[0], jnp.where(row == 1, actbuf[1], 0.0))
    ada_grad[...] = dot_tn(d_two, a_two, HIGH)[0:part, :]
    act_copy.wait_send()


def rope_table():
    table = np.zeros((PAD, 2 * PAD), np.float64)
    angle = np.arange(64)[:, None] * 10000.0 ** (-np.arange(18) / 18)
    for axis in range(2):
        rows = slice(64 * axis, 64 * axis + 64)
        for quarter in range(2):
            at = 36 * axis + 18 * quarter
            table[rows, at : at + 18] = np.cos(angle)
            table[rows, PAD + at : PAD + at + 18] = np.sin(angle)
    return table.astype(np.float32)


def run_block(tokens, cotangent, act, ada, wh, wout, wup, wdown, wqkv, q_gain, k_gain, hw):
    width, hidden = tokens.shape[1], wup.shape[1] // 2
    half, part = width // 2, ada.shape[0]
    vmem, any_ = pl.BlockSpec(memory_space=pltpu.VMEM), pl.BlockSpec(memory_space=pl.ANY)
    smem = pl.BlockSpec(memory_space=pltpu.SMEM)
    sds = jax.ShapeDtypeStruct
    v, dma = pltpu.VMEM, pltpu.SemaphoreType.DMA
    n_chunks = len(weight_chunks(width, hidden))
    tile16 = (16, TILE, PAD)
    out_shape = (
        sds((TILE, width), BF16),
        sds((TILE, width), BF16),
        sds((3 * HEAD, half), F32),
        sds((part, width), F32),
        sds((8, PAD), F32),
        sds((HEAD, hidden // 2), F32),
        sds((half, 3 * PAD), F32),
        sds((HEAD, half), F32),
        sds((width, 3 * width), BF16),
        sds((8 * TILE, hidden // 2), BF16),
        sds((8 * TILE, 5 * PAD), BF16),
        sds((8 * TILE, 5 * PAD), BF16),
        sds((8 * TILE, 8 * PAD), BF16),
        sds((8 * TILE, hidden), BF16),
        sds((8 * TILE, 8 * PAD), BF16),
    )
    scratch = [
        v((16 * TILE, width), BF16),
        v((width, 3 * PAD), BF16),
        v((width, width), BF16),
        v((width, 2 * hidden), BF16),
        v((hidden, width), BF16),
        v((2, 8, width), F32),
        v((2, 8, 2 * PAD), F32),
        v((32, 8, 2 * PAD), F32),
        v((8, 6 * width), F32),
        v(tile16, F32),
        v(tile16, F32),
        v(tile16, F32),
        v(tile16, F32),
        v(tile16, BF16),
        v(tile16, BF16),
        v(tile16, BF16),
        v((PAD, 16 * TILE), BF16),
        v((PAD, 16 * TILE), BF16),
        v(tile16, F32),
        v(tile16, BF16),
        v((TILE, 16 * PAD), BF16),
        v(tile16, BF16),
        v((PAD, 16 * TILE), BF16),
        v((PAD, 16 * TILE), F32),
        v(tile16, F32),
        v(tile16, F32),
        v((16, TILE, 2 * PAD), BF16),
        v((half, 3 * PAD), BF16),
        v((3, half, PAD), BF16),
        v((TILE, width), F32),
        v((TILE, width), F32),
        v((TILE, width), F32),
        v((TILE, width), F32),
        v((8, 6 * width), F32),
        v((32, 8, 2 * PAD), F32),
        v((32, 8, 2 * PAD), F32),
        v((TILE, width), BF16),
        v((TILE, width), BF16),
        v((TILE, hidden), BF16),
        v((TILE, width), BF16),
        v((TILE, width), BF16),
        v((TILE, 2 * hidden), BF16),
        v((TILE, 10 * PAD), BF16),
        v((TILE, 10 * PAD), BF16),
        v((TILE, 16 * PAD), BF16),
        v((2, 80, hidden // 2), BF16),
        v((2, half, 3 * PAD), BF16),
        v((2, 80, 5 * PAD), BF16),
        v((80, hidden // 2), BF16),
        v((half, 3 * PAD), BF16),
        v((80, 5 * PAD), BF16),
        v((80, 5 * PAD), F32),
        dma((3, 8)),
        dma((3, 8)),
        dma((3, 8)),
        dma((3, 8)),
        dma((3, 2)),
        dma((3, 2)),
        dma((3, 2)),
        dma((3,)),
        dma((3,)),
        dma((2,)),
        dma((16, 4)),
        dma((16,)),
        dma,
        dma((n_chunks, 4)),
        dma((n_chunks, 4)),
        dma((4,)),
        dma((2,)),
        dma((2,)),
        dma((32,)),
        dma((32,)),
        dma((16,)),
        dma((16,)),
        dma((16,)),
        dma((16,)),
        dma((16,)),
        dma((16,)),
        dma((2,)),
        dma((3,)),
        dma((3,)),
        dma((32,)),
        dma((32,)),
        dma((2,)),
    ]
    return pl.pallas_call(
        block_kernel,
        out_shape=out_shape,
        in_specs=[vmem] * 5 + [any_] * 4 + [vmem] * 3 + [smem],
        out_specs=[vmem] * 8 + [any_] * 7,
        scratch_shapes=scratch,
        compiler_params=pltpu.CompilerParams(
            collective_id=0, has_side_effects=True, vmem_limit_bytes=VMEM_LIMIT
        ),
    )(tokens, cotangent, act, ada, wh, wout, wup, wdown, wqkv, q_gain, k_gain, rope_table(), hw)


def head_weight(weight):
    at = lax.axis_index(("ty", "tx")) * HEAD
    width = weight.shape[1] // 3
    parts = [
        lax.dynamic_slice_in_dim(weight, p * width + at, HEAD, axis=1) for p in range(3)
    ]
    return jnp.concatenate([jnp.pad(p, ((0, 0), (0, PAD - HEAD))) for p in parts], axis=1)


def fast_body(
    tokens,
    cotangent,
    class_embed,
    timestep,
    grid_height,
    grid_width,
    qkv_weight,
    out_weight,
    up_weight,
    down_weight,
    ada_weight,
    q_gain,
    k_gain,
):
    width = tokens.shape[2]
    act = jax.nn.silu(class_embed + time_embed(timestep, width)).astype(BF16).astype(F32)
    pad = lambda g: jnp.broadcast_to(jnp.pad(g, (0, PAD - HEAD))[None], (8, PAD))
    (mixed, tgrad, qkv_grad, ada_grad, gains, down_grad, up_grad, out_grad) = (
        run_block(
            tokens[0],
            cotangent[0],
            jnp.broadcast_to(act, (8, width)),
            ada_weight,
            head_weight(qkv_weight),
            out_weight,
            up_weight,
            down_weight,
            qkv_weight,
            pad(q_gain),
            pad(k_gain),
            jnp.concatenate([grid_height, grid_width]),
        )[:8]
    )
    return (
        mixed[None],
        tgrad[None],
        qkv_grad.T,
        out_grad.T,
        up_grad,
        down_grad.T,
        ada_grad,
        gains[0, :HEAD],
        gains[1, :HEAD],
    )


def solution(mesh):
    in_specs = (
        P("img", ("ty", "tx"), None),
        P("img", ("ty", "tx"), None),
        P("img", None),
        P("img"),
        P("img"),
        P("img"),
        P("img", None),
        P("img", None),
        P("img", None),
        P("img", None),
        P(("img", "ty", "tx"), None),
        P(),
        P(),
    )
    out_specs = (
        P("img", ("ty", "tx"), None),
        P("img", ("ty", "tx"), None),
        P("img", ("ty", "tx")),
        P("img", ("ty", "tx")),
        P("img", ("ty", "tx")),
        P("img", ("ty", "tx")),
        P(("img", "ty", "tx"), None),
        P(),
        P(),
    )
    shape = dict(mesh.shape)
    fast = (shape["img"], shape["ty"], shape["tx"]) == (2, 4, 4)
    body = fast_body if fast else general_body
    return jax.shard_map(body, mesh=mesh, in_specs=in_specs, out_specs=out_specs, check_vma=False)
```

```python
import functools

import jax
import jax.numpy as jnp
import numpy as np
from jax import lax
from jax.experimental import pallas as pl
from jax.experimental.pallas import tpu as pltpu
from jax.sharding import PartitionSpec as P

HEADS = 16
HEAD = 72


EPS = 1e-06
HIGH = lax.Precision.HIGHEST


def layout(slot, height, width, cap, rows_tiles, cols_tiles):
    tile = slot // cap
    row_tile = tile // cols_tiles
    col_tile = tile % cols_tiles
    local = slot % cap
    top = row_tile * height // rows_tiles
    bottom = (row_tile + 1) * height // rows_tiles
    left = col_tile * width // cols_tiles
    right = (col_tile + 1) * width // cols_tiles
    span = right - left
    valid = local < (bottom - top) * span
    row = jnp.where(valid, top + local // span, 0)
    col = jnp.where(valid, left + local % span, 0)
    return (valid, row, col)


def time_embed(step, dim):
    half = dim // 2
    freq = jnp.exp(-jnp.log(10000.0) * jnp.arange(half, dtype=jnp.float32) / half)
    angle = step.astype(jnp.float32)[:, None] * freq
    return jnp.concatenate([jnp.cos(angle), jnp.sin(angle)], axis=-1)


def rotate(part, position):
    quarter = part.shape[-1] // 2
    freq = jnp.exp(-jnp.log(10000.0) * jnp.arange(quarter, dtype=jnp.float32) / quarter)
    angle = position.astype(jnp.float32)[..., None, None] * freq
    first, second = (part[..., :quarter], part[..., quarter:])
    cosine, sine = (jnp.cos(angle), jnp.sin(angle))
    return jnp.concatenate(
        [first * cosine - second * sine, second * cosine + first * sine], axis=-1
    )


def rope(heads, row, col):
    half = heads.shape[-1] // 2
    return jnp.concatenate(
        [rotate(heads[..., :half], row), rotate(heads[..., half:], col)], axis=-1
    )


def head_norm(value, gain):
    return value * lax.rsqrt(jnp.mean(value * value, axis=-1, keepdims=True) + EPS) * gain


def rms(value):
    return value * lax.rsqrt(jnp.mean(value * value, axis=-1, keepdims=True) + EPS)


def flat_rows(value):
    return value.reshape(-1, value.shape[-1])


def outer_sum(left, right):
    return lax.dot_general(
        flat_rows(left),
        flat_rows(right),
        (((0,), (0,)), ((), ())),
        preferred_element_type=jnp.float32,
    )


def times_transposed(left, weight):
    return lax.dot_general(
        left, weight, (((left.ndim - 1,), (1,)), ((), ())), preferred_element_type=jnp.float32
    )


def masked_scores(query, keys_all, key_valid):
    scores = jnp.einsum("qhd,khd->hqk", query, keys_all, preferred_element_type=jnp.float32)
    return jnp.where(key_valid[None, None, :], scores, -1e30)


def general_body(
    tokens,
    cotangent,
    class_embed,
    timestep,
    grid_height,
    grid_width,
    qkv_weight,
    out_weight,
    up_weight,
    down_weight,
    ada_weight,
    q_gain,
    k_gain,
):
    images, slots_dev, width = tokens.shape
    rows_tiles = lax.axis_size("ty")
    cols_tiles = lax.axis_size("tx")
    slots_all = slots_dev * rows_tiles * cols_tiles
    own_slot = lax.axis_index(("ty", "tx")) * slots_dev + jnp.arange(slots_dev, dtype=jnp.int32)
    all_slot = jnp.arange(slots_all, dtype=jnp.int32)
    valid_q, row_q, col_q = jax.vmap(
        lambda h, w: layout(own_slot, h, w, slots_dev, rows_tiles, cols_tiles)
    )(grid_height, grid_width)
    valid_k = jax.vmap(lambda h, w: layout(all_slot, h, w, slots_dev, rows_tiles, cols_tiles)[0])(
        grid_height, grid_width
    )
    keep = valid_q.astype(jnp.float32)[..., None]
    act = jax.nn.silu(class_embed + time_embed(timestep, width)).astype(jnp.bfloat16)
    mod = lax.dot_general(
        act,
        lax.all_gather(ada_weight, ("img", "ty", "tx"), axis=0, tiled=True),
        (((1,), (1,)), ((), ())),
        preferred_element_type=jnp.float32,
    )
    shift1, scale1, gate1, shift2, scale2, gate2 = [
        part[:, None, :] for part in jnp.split(mod, 6, axis=1)
    ]
    wqkv, wout, w12, w3 = (
        lax.all_gather(qkv_weight, "img", axis=0, tiled=True),
        lax.all_gather(out_weight, "img", axis=0, tiled=True),
        lax.all_gather(up_weight, "img", axis=0, tiled=True),
        lax.all_gather(down_weight, "img", axis=0, tiled=True),
    )
    xf = tokens.astype(jnp.float32)
    norm1, pull_norm1 = jax.vjp(rms, xf)
    h1 = (norm1 * (1.0 + scale1) + shift1).astype(jnp.bfloat16)
    qkv = jnp.dot(h1, wqkv, preferred_element_type=jnp.float32).reshape(
        images, slots_dev, 3, HEADS, HEAD
    )

    def finish(query_raw, key_raw, query_gain, key_gain):
        query = rope(head_norm(query_raw, query_gain), row_q, col_q) * HEAD ** (-0.5)
        return (query, rope(head_norm(key_raw, key_gain), row_q, col_q))

    (query_f, key_f), pull_heads = jax.vjp(finish, qkv[:, :, 0], qkv[:, :, 1], q_gain, k_gain)
    query_b = query_f.astype(jnp.bfloat16)
    key_b = key_f.astype(jnp.bfloat16)
    value_b = qkv[:, :, 2].astype(jnp.bfloat16)
    keys_all, values_all = (
        lax.all_gather(key_b, ("ty", "tx"), axis=1, tiled=True),
        lax.all_gather(value_b, ("ty", "tx"), axis=1, tiled=True),
    )
    index = 0
    scores = masked_scores(query_b[index], keys_all[index], valid_k[index])
    top = jnp.max(scores, axis=-1, keepdims=True)
    lse = top + jnp.log(jnp.sum(jnp.exp(scores - top), axis=-1, keepdims=True))
    prob = jnp.exp(scores - lse).astype(jnp.bfloat16)
    attn_list = [
        jnp.einsum("hqk,khd->qhd", prob, values_all[index], preferred_element_type=jnp.float32)
    ]
    lse_list = [lse]
    attn = jnp.stack(attn_list).reshape(images, slots_dev, width).astype(jnp.bfloat16)
    branch = jnp.dot(attn, wout, preferred_element_type=jnp.float32)
    x1 = xf + keep * gate1 * branch
    norm2, pull_norm2 = jax.vjp(rms, x1)
    h2 = (norm2 * (1.0 + scale2) + shift2).astype(jnp.bfloat16)
    gate_up = jnp.dot(h2, w12, preferred_element_type=jnp.float32)
    hidden = gate_up.shape[-1] // 2
    gate_part, up_part = (gate_up[..., :hidden], gate_up[..., hidden:])
    sig = jax.nn.sigmoid(gate_part)
    silu_gate = gate_part * sig
    mid = (silu_gate * up_part).astype(jnp.bfloat16)
    ffn = jnp.dot(mid, w3, preferred_element_type=jnp.float32)
    mixed = (x1 + keep * gate2 * ffn).astype(jnp.bfloat16)
    grad_out = cotangent.astype(jnp.float32)
    d_gate2 = jnp.sum(grad_out * keep * ffn, axis=1)
    d_ffn = (grad_out * keep * gate2).astype(jnp.bfloat16)
    term_down = outer_sum(mid, d_ffn)
    d_mid = times_transposed(d_ffn, w3)
    d_gate = d_mid * up_part * (sig + gate_part * sig * (1.0 - sig))
    d_up = d_mid * silu_gate
    d_gate_up = jnp.concatenate([d_gate, d_up], axis=-1).astype(jnp.bfloat16)
    term_up = outer_sum(h2, d_gate_up)
    d_h2 = times_transposed(d_gate_up, w12)
    d_scale2 = jnp.sum(d_h2 * norm2, axis=1)
    d_shift2 = jnp.sum(d_h2, axis=1)
    d_x1 = grad_out + pull_norm2(d_h2 * (1.0 + scale2))[0]
    d_gate1 = jnp.sum(d_x1 * keep * branch, axis=1)
    d_branch = (d_x1 * keep * gate1).astype(jnp.bfloat16)
    term_out = outer_sum(attn, d_branch)
    d_attn = (
        times_transposed(d_branch, wout)
        .astype(jnp.bfloat16)
        .reshape(images, slots_dev, HEADS, HEAD)
    )
    keys_back, values_back = (
        lax.all_gather(key_b, ("ty", "tx"), axis=1, tiled=True),
        lax.all_gather(value_b, ("ty", "tx"), axis=1, tiled=True),
    )
    index = 0
    scores = masked_scores(query_b[index], keys_back[index], valid_k[index])
    prob = jnp.exp(scores - lse_list[index])
    d_prob = jnp.einsum(
        "qhd,khd->hqk", d_attn[index], values_back[index], preferred_element_type=jnp.float32
    )
    delta = jnp.sum(prob * d_prob, axis=-1, keepdims=True)
    d_scores = (prob * (d_prob - delta)).astype(jnp.bfloat16)
    dq_list = [
        jnp.einsum("hqk,khd->qhd", d_scores, keys_back[index], preferred_element_type=jnp.float32)
    ]
    dk_list = [
        jnp.einsum("hqk,qhd->khd", d_scores, query_b[index], preferred_element_type=jnp.float32)
    ]
    dv_list = [
        jnp.einsum(
            "hqk,qhd->khd",
            prob.astype(jnp.bfloat16),
            d_attn[index],
            preferred_element_type=jnp.float32,
        )
    ]
    d_key, d_value = (
        lax.psum_scatter(
            jnp.stack(dk_list).astype(jnp.bfloat16), ("ty", "tx"), scatter_dimension=1, tiled=True
        ).astype(jnp.float32),
        lax.psum_scatter(
            jnp.stack(dv_list).astype(jnp.bfloat16), ("ty", "tx"), scatter_dimension=1, tiled=True
        ).astype(jnp.float32),
    )
    d_query_raw, d_key_raw, d_q_gain, d_k_gain = pull_heads((jnp.stack(dq_list), d_key))
    d_qkv = (
        jnp.stack([d_query_raw, d_key_raw, d_value], axis=2)
        .reshape(images, slots_dev, 3 * width)
        .astype(jnp.bfloat16)
    )
    term_qkv = outer_sum(h1, d_qkv)
    d_h1 = times_transposed(d_qkv, wqkv)
    d_scale1 = jnp.sum(d_h1 * norm1, axis=1)
    d_shift1 = jnp.sum(d_h1, axis=1)
    tokens_grad = (d_x1 + pull_norm1(d_h1 * (1.0 + scale1))[0]).astype(jnp.bfloat16)
    d_mod = jnp.concatenate([d_shift1, d_scale1, d_gate1, d_shift2, d_scale2, d_gate2], axis=1)
    act_f = act.astype(jnp.float32)
    ada_grad = lax.psum_scatter(
        lax.dot_general(
            d_mod,
            act_f,
            (((0,), (0,)), ((), ())),
            precision=HIGH,
            preferred_element_type=jnp.float32,
        ),
        ("img", "ty", "tx"),
        scatter_dimension=0,
        tiled=True,
    )
    q_gain_grad, k_gain_grad = lax.psum((d_q_gain, d_k_gain), ("img", "ty", "tx"))
    parts = (
        lax.psum_scatter(
            term_qkv.astype(jnp.bfloat16), ("ty", "tx"), scatter_dimension=1, tiled=True
        ).astype(jnp.float32),
        lax.psum_scatter(
            term_out.astype(jnp.bfloat16), ("ty", "tx"), scatter_dimension=1, tiled=True
        ).astype(jnp.float32),
        lax.psum_scatter(
            term_up.astype(jnp.bfloat16), ("ty", "tx"), scatter_dimension=1, tiled=True
        ).astype(jnp.float32),
        lax.psum_scatter(
            term_down.astype(jnp.bfloat16), ("ty", "tx"), scatter_dimension=1, tiled=True
        ).astype(jnp.float32),
    )
    grads = (
        lax.psum_scatter(
            parts[0].astype(jnp.bfloat16), "img", scatter_dimension=0, tiled=True
        ).astype(jnp.float32),
        lax.psum_scatter(
            parts[1].astype(jnp.bfloat16), "img", scatter_dimension=0, tiled=True
        ).astype(jnp.float32),
        lax.psum_scatter(
            parts[2].astype(jnp.bfloat16), "img", scatter_dimension=0, tiled=True
        ).astype(jnp.float32),
        lax.psum_scatter(
            parts[3].astype(jnp.bfloat16), "img", scatter_dimension=0, tiled=True
        ).astype(jnp.float32),
    )
    return (
        mixed,
        tokens_grad,
        grads[0],
        grads[1],
        grads[2],
        grads[3],
        ada_grad,
        q_gain_grad,
        k_gain_grad,
    )


VMEM_LIMIT = 63 << 20
MESH = pl.DeviceIdType.MESH
PAD = 128
TILE = 128
F32 = jnp.float32
BF16 = jnp.bfloat16


def dot(a, b):
    return lax.dot_general(a, b, (((1,), (0,)), ((), ())), preferred_element_type=F32)


def dot_nt(a, b):
    return lax.dot_general(a, b, (((1,), (1,)), ((), ())), preferred_element_type=F32)


def dot_tn(a, b, precision=None):
    return lax.dot_general(
        a, b, (((0,), (0,)), ((), ())), preferred_element_type=F32, precision=precision
    )


def lanes(shape):
    return lax.broadcasted_iota(jnp.int32, shape, len(shape) - 1)


def split3(value):
    high = value.astype(BF16)
    rest = value - high.astype(F32)
    mid = rest.astype(BF16)
    low = (rest - mid.astype(F32)).astype(BF16)
    return (high, mid, low)


def put_split3(tile, value, lane0):
    at = lanes(tile.shape)
    for k, term in enumerate(split3(value)):
        tile = jnp.where(at == lane0 + k, jnp.broadcast_to(term.astype(F32), tile.shape), tile)
    return tile


OUT, UP, DOWN, QKV = range(4)


def weight_chunks(width, hidden):
    half = width // 2
    quarter = hidden // 4

    def up(k):
        return [(UP, 2 * k + u, 0, half, quarter, "yz") for u in range(2)]

    return (
        [(OUT, 0, 0, half, width, "z")]
        + up(0)
        + up(1)
        + up(2)
        + [(DOWN, 0, 0, quarter, width, "yz")]
        + up(3)
        + [(DOWN, 0, quarter, quarter, width, "yz")]
        + [(QKV, 0, 0, half, 14 * PAD, "z"), (QKV, 1, 0, half, 13 * PAD, "")]
    )


def block_kernel(
    tok, cot, act, ada, wh, wout, wup, wdown, wqkv, q_gain, k_gain, tab, hw,
    mixed, tgrad, qkv_grad, ada_grad, gain_grad, down_grad, up_grad, out_grad, qkv_hbm,
    lb_down, lb_up, lb_out, rb_down, rb_up, rb_out,
    tok_all, whv, woutv, wupv, wdownv, actbuf, modsend, modbuf, modv,
    cosv, sinv, qraw, kraw, qa, ka, va, kt, qt, onorm, attn_send, attn_in,
    do_in, dot_t, dqt, dkv_in, dq_in, dw_in, pc_in,
    x1v, branchv, ffnv, dh2v, dmod, dsend, dbuf,
    l_attn, l_h2, l_mid, r_ffn, r_branch, r_gu, l_h2s, l_attns, r_branchs,
    za_down, za_up, za_out, zb_down, zb_up, zb_out, z_out,
    gl_s, gl_r, gr_s, gr_r, gu_s, gu_r, g_loc, za_s, za_r, zb_s, zb_r, z_loc,
    tok_send, tok_recv, tok_loc, w_send, w_recv, w_loc, wh_sem, act_sem, mod_s, mod_r,
    at_s, at_r, do_s, do_r, dq_s, dq_r, dkv_s, dkv_r, dw_sem, pc_s, pc_r, dm_s, dm_r, loc,
):
    img, ty, z = lax.axis_index("img"), lax.axis_index("ty"), lax.axis_index("tx")
    b = ty * 4 + z
    me = img * 16 + b
    width = tok.shape[1]
    half = width // 2
    hidden = wup.shape[1] // 2
    part = ada.shape[0]
    other = 1 - img

    def dev(i=img, t=ty, k=z):
        return {"img": i, "ty": t, "tx": k}

    def dev_flat(p):
        return dev(p // 16, lax.rem(p // 4, 4), lax.rem(p, 4))

    def dev_tile(t):
        return dev(img, t // 4, lax.rem(t, 4))

    def rcopy(src, dst, s, r, d):
        return pltpu.make_async_remote_copy(
            src_ref=src, dst_ref=dst, send_sem=s, recv_sem=r, device_id=d, device_id_type=MESH
        )

    def loop(lo, hi, f):
        def step(k, c):
            f(k)
            return c

        lax.fori_loop(lo, hi, step, 0)

    bar = pltpu.get_barrier_semaphore()
    loop(
        1, 32,
        lambda k: pl.semaphore_signal(
            bar, inc=1, device_id=dev_flat(lax.rem(me + k, 32)), device_id_type=MESH
        ),
    )
    pl.semaphore_wait(bar, 31)

    hbm = (wout, wup, wdown, wqkv)
    vm = (woutv, wupv, wdownv, qkv_hbm)
    chunks = weight_chunks(width, hidden)

    y, c, z_bit = ty // 2, lax.rem(ty, 2), lax.rem(z, 2)
    to_x, to_y, to_z, to_c = dev(i=other), dev(t=ty ^ 2), dev(k=z ^ 1), dev(t=ty ^ 1)
    OWN, FROM_Y, FROM_Z, FAR_A, FAR_B, SIBLING = range(6)

    def w_ref(ref, i, row0, im, rel, sib=False):
        m, k, r0, rows, cols, ways = chunks[i]
        yy = 1 - y if rel in (FROM_Y, FAR_A, FAR_B) else y
        zz = 1 - z_bit if rel in (FROM_Z, FAR_A, FAR_B) else z_bit
        cc = 1 - c if sib else c
        col = k * 14 * PAD if m == QKV else 0
        if m == UP:
            col = (k % 2) * hidden + lax.rem(2 * im + k // 2, 4) * (hidden // 4)
        if ways == "yz" and m == UP:
            n, p = rows // 4, 2 * yy + zz
            cols = cols // 2
            col = col + cc * cols
        elif ways == "yz":
            n, p = rows // 8, 4 * yy + 2 * zz + cc
        elif ways == "":
            n, p = rows // 2, cc
        else:
            n, p = rows // 4, 2 * (yy if ways == "y" else zz) + cc
        row, size, first = row0 + r0 + p * n, n, (n // 32 + (n // 16) % 2) * 16
        if rel == FAR_A:
            size = first
        if rel == FAR_B:
            row, size = row + first, n - first
        return ref.at[
            pl.ds(pl.multiple_of(row, 16), size), pl.ds(pl.multiple_of(col, PAD), cols)
        ]

    def w_mine(i, rel, sib=False):
        m = chunks[i][0]
        return w_ref(vm[m], i, other * hbm[m].shape[0], img, rel, sib)

    def w_x(i):
        m = chunks[i][0]
        src = w_ref(hbm[m], i, 0, other, OWN)
        dst = w_ref(vm[m], i, img * hbm[m].shape[0], other, OWN)
        return rcopy(src, dst, w_send.at[i, 0], w_recv.at[i, 0], to_x)

    def w_copy(i, slot, held, rel, to):
        ref = w_mine(i, held)
        return rcopy(ref, ref, w_send.at[i, slot], w_recv.at[i, rel], to)

    def w_wait(i, rel, sib=False):
        ref = w_mine(i, rel, sib)
        at = rel + SIBLING if sib else rel
        rcopy(ref, ref, w_send.at[i, 0], w_recv.at[i, at], to_c).wait_recv()

    def w_sends(i):
        ways = chunks[i][5]
        first = [w_copy(i, 1, OWN, SIBLING + OWN, to_c)]
        if "y" in ways:
            first.append(w_copy(i, 2, OWN, FROM_Y, to_y))
        if "z" in ways:
            first.append(w_copy(i, 3, OWN, FROM_Z, to_z))
        sends = {OWN: first}
        if "z" in ways:
            sends[FROM_Z] = [w_copy(i, 4, FROM_Z, SIBLING + FROM_Z, to_c)]
        if "y" in ways:
            sends[FROM_Y] = [w_copy(i, 5, FROM_Y, SIBLING + FROM_Y, to_c)]
        if ways == "yz":
            far_a, far_b = w_far(i)
            sends[FROM_Z].insert(0, far_a)
            sends[FROM_Y].insert(0, far_b)
            sends[FAR_A] = [w_copy(i, 8, FAR_A, SIBLING + FAR_A, to_c)]
            sends[FAR_B] = [w_copy(i, 9, FAR_B, SIBLING + FAR_B, to_c)]
        return sends

    def w_far(i):
        m, _, _, rows, _, _ = chunks[i]
        n = rows // (4 if m == UP else 8)
        first = (n // 32 + (n // 16) % 2) * 16
        a = w_mine(i, FROM_Z).at[pl.ds(0, first)]
        b_ = w_mine(i, FROM_Y).at[pl.ds(first, n - first)]
        return (
            rcopy(a, a, w_send.at[i, 6], w_recv.at[i, FAR_A], to_y),
            rcopy(b_, b_, w_send.at[i, 7], w_recv.at[i, FAR_B], to_z),
        )

    def w_pass(which, rels):
        for i in which:
            sends = w_sends(i)
            for rel in rels:
                if rel in sends:
                    w_wait(i, rel)
                    for copy in sends[rel]:
                        copy.start()

    def x_arrived(*which):
        w_pass(which, (OWN,))

    def hop_arrived(*which):
        w_pass(which, (FROM_Z, FROM_Y))

    def far_arrived(*which):
        w_pass(which, (FAR_A, FAR_B))

    def w_done(*which):
        for i in which:
            for rel in w_sends(i):
                w_wait(i, rel, True)

    def w_drain(i):
        w_x(i).wait_send()
        for copies in w_sends(i).values():
            for copy in copies:
                copy.wait_send()

    def own(m):
        rows = hbm[m].shape[0]
        return pltpu.make_async_copy(hbm[m], vm[m].at[pl.ds(img * rows, rows)], w_loc.at[m])

    act_copy = rcopy(act, actbuf.at[img], act_sem.at[0], act_sem.at[1], dev(i=other))
    act_copy.start()
    actbuf[img] = act[...]
    wh_copy = rcopy(wh, whv.at[pl.ds(img * half, half)], wh_sem.at[0], wh_sem.at[1], dev(i=other))
    for i in range(3):
        w_x(i).start()
    whv[pl.ds(pl.multiple_of(img * half, 64), half), :] = wh[...]

    def tok_at(chunk):
        return tok_all.at[pl.ds(pl.multiple_of(chunk * TILE, TILE), TILE)]

    def t_send(src, chunk, way, d):
        return rcopy(src, tok_at(chunk), tok_send.at[chunk, way], tok_recv.at[chunk], d)

    def t_wait(chunk):
        t_send(tok, chunk, 0, dev(t=ty ^ 1)).wait_recv()

    tok_own = pltpu.make_async_copy(tok, tok_at(b), tok_loc)
    tok_own.start()

    def t_forward(src, chunk, up, down):
        if up:

            @pl.when(z < 3)
            def _():
                t_send(src, chunk, 0, dev(k=z + 1)).start()

        if down:

            @pl.when(z > 0)
            def _():
                t_send(src, chunk, 1, dev(k=z - 1)).start()

        t_send(src, chunk, 2, dev(t=ty ^ 2)).start()
        t_send(src, chunk, 3, dev(t=ty ^ 1)).start()

    t_forward(tok, b, True, True)
    for m in range(3):
        own(m).start()

    act_copy.wait_recv()
    for i in range(2):
        modsend[i, :, 0:part] = dot_nt(actbuf[i].astype(BF16), ada[...])

    def mod_copy(p):
        return rcopy(modsend.at[p // 16], modbuf.at[me], mod_s.at[p], mod_r.at[me], dev_flat(p))

    loop(1, 32, lambda k: mod_copy(lax.rem(me + k, 32)).start())
    modbuf[me] = modsend[img]
    wh_copy.start()
    for i in range(3, len(chunks)):
        w_x(i).start()

    for s in (1, 2, 3):

        @pl.when(z - s >= 0)
        def _():
            t_wait(b - s)
            t_forward(tok_at(b - s), b - s, True, False)

        @pl.when(z + s <= 3)
        def _():
            t_wait(b + s)
            t_forward(tok_at(b + s), b + s, False, True)

    x_arrived(0, 1, 2)

    def t_y(zz):
        chunk = (ty ^ 2) * 4 + zz
        t_wait(chunk)
        t_send(tok_at(chunk), chunk, 3, dev(t=ty ^ 1)).start()

    loop(0, 4, t_y)
    hop_arrived(0)
    loop(0, 4, lambda zz: t_wait((ty ^ 1) * 4 + zz))
    loop(0, 4, lambda zz: t_wait((ty ^ 3) * 4 + zz))

    def t_drain(zz):
        chunk = ty * 4 + zz
        ref = tok_at(chunk)

        @pl.when((zz <= z) & (z < 3))
        def _():
            t_send(ref, chunk, 0, dev(t=ty ^ 1)).wait_send()

        @pl.when((zz >= z) & (z > 0))
        def _():
            t_send(ref, chunk, 1, dev(t=ty ^ 1)).wait_send()

        t_send(ref, chunk, 2, dev(t=ty ^ 1)).wait_send()
        t_send(ref, chunk, 3, dev(t=ty ^ 1)).wait_send()
        away = (ty ^ 2) * 4 + zz
        t_send(tok_at(away), away, 3, dev(t=ty ^ 1)).wait_send()

    loop(0, 4, t_drain)
    tok_own.wait()

    def mod_wait(k):
        p = lax.rem(me + k, 32)
        rcopy(
            modsend.at[0], modbuf.at[p], mod_s.at[p], mod_r.at[p], dev_flat(p)
        ).wait()

    loop(1, 32, mod_wait)
    for s in range(32):
        modv[:, s * part : (s + 1) * part] = modbuf[s, :, 0:part]
    shift1, scale1, gate1, shift2, scale2, gate2 = [
        functools.partial(lambda k: modv[0:1, k * width : (k + 1) * width], k) for k in range(6)
    ]
    wh_copy.wait()

    height, wide = hw[0], hw[1]
    local = lax.broadcasted_iota(jnp.int32, (TILE, PAD), 0)
    lane = lax.broadcasted_iota(jnp.int32, (TILE, PAD), 1)

    def tile_layout(t):
        row_tile, col_tile = t // 4, lax.rem(t, 4)
        top = row_tile * height // 4
        rows = (row_tile + 1) * height // 4 - top
        left = col_tile * wide // 4
        span = (col_tile + 1) * wide // 4 - left
        spans = jnp.full((TILE, PAD), span, jnp.int32)
        quot = jnp.floor((local.astype(F32) + 0.5) / spans.astype(F32)).astype(jnp.int32)
        valid = local < jnp.full((TILE, PAD), rows * span, jnp.int32)
        row = jnp.where(valid, top + quot, 0)
        col = jnp.where(valid, left + local - quot * spans, 0)
        return valid, row, col

    def rope(n, c, s1, s2):
        return n * c + pltpu.roll(n, PAD - 18, 1) * s1 + pltpu.roll(n, 18, 1) * s2

    def unrope(d, c, s1, s2):
        return d * c + pltpu.roll(d * s1, 18, 1) + pltpu.roll(d * s2, PAD - 18, 1)

    def split_sin(sine):
        first = (lane < 18) | ((lane >= 36) & (lane < 54))
        return jnp.where(first, -sine, 0.0), jnp.where(first, 0.0, sine)

    def head_rows(t):
        valid, row, col = tile_layout(t)
        hot = jnp.where((lane == row) | (lane - 64 == col), 1.0, 0.0)
        angles = lax.dot_general(
            hot, tab[...], (((1,), (0,)), ((), ())),
            precision=HIGH, preferred_element_type=F32,
        )
        c, sine = angles[:, 0:PAD], angles[:, PAD : 2 * PAD]
        cosv[t] = c
        sinv[t] = sine
        s1, s2 = split_sin(sine)
        at = pl.ds(pl.multiple_of(t * TILE, TILE), TILE)
        x = tok_all[at, :].astype(F32)
        r = lax.rsqrt(jnp.mean(x * x, axis=1, keepdims=True) + EPS)
        h1 = ((x * r) * (1.0 + scale1()) + shift1()).astype(BF16)
        tok_all[at, :] = h1
        qkv = dot(h1, whv[...])
        q_r, k_r, v_r = qkv[:, 0:PAD], qkv[:, PAD : 2 * PAD], qkv[:, 2 * PAD : 3 * PAD]
        qraw[t] = q_r
        kraw[t] = k_r

        def normed(v, gain):
            rr = lax.rsqrt(jnp.sum(v * v, axis=1, keepdims=True) * (1.0 / HEAD) + EPS)
            return v * rr * gain[0:1, :]

        q_f = rope(normed(q_r, q_gain), c, s1, s2) * HEAD ** (-0.5)
        k_f = rope(normed(k_r, k_gain), c, s1, s2)
        qa[t] = jnp.where(lane == HEAD, 1.0, q_f).astype(BF16)
        k_f = jnp.where(lane == HEAD, jnp.where(valid, 0.0, -30000.0), k_f)
        k_f = jnp.where((lane > HEAD) & (lane < HEAD + 4), 1.0, k_f)
        ka[t] = k_f.astype(BF16)
        kt[:, pl.ds(pl.multiple_of(t * TILE, TILE), TILE)] = k_f.T.astype(BF16)
        va[t] = jnp.where((lane >= HEAD) & (lane < HEAD + 3), 1.0, v_r).astype(BF16)

    x_arrived(3, 4)
    hop_arrived(1, 2)
    loop(0, 8, head_rows)
    x_arrived(5, 6)
    hop_arrived(3, 4)
    far_arrived(1, 2)
    loop(8, 16, head_rows)
    x_arrived(7)
    hop_arrived(5, 6)
    far_arrived(3, 4)

    def head_lanes(h):
        return attn_in.at[:, pl.ds(pl.multiple_of(h * PAD, PAD), PAD)]

    def at_copy(t):
        return rcopy(attn_send.at[t], head_lanes(b), at_s.at[t], at_r.at[b], dev_tile(t))

    def attend(k):
        q2 = qa[pl.ds(2 * k, 2)].reshape(2 * TILE, PAD)
        p = jnp.exp(dot(q2, kt[...])).astype(BF16)
        o = dot(p, va[...].reshape(16 * TILE, PAD))
        total = o[:, HEAD : HEAD + 1]
        o = o / total
        lse = jnp.log(total)
        q3 = put_split3(q2.astype(F32), -lse, HEAD + 1)
        o16 = o.astype(BF16)
        for u in range(2):
            t = 2 * k + u
            rows = slice(u * TILE, (u + 1) * TILE)
            onorm[t] = o[rows]
            qa[t] = q3[rows].astype(BF16)
            qt[:, pl.ds(pl.multiple_of(t * TILE, TILE), TILE)] = q3[rows].T.astype(BF16)
            attn_send[t] = o16[rows]

            @pl.when(t != b)
            def _():
                at_copy(t).start()

    loop(0, 8, attend)
    head_lanes(b)[...] = attn_send[b]
    x_arrived(8, 9, 10)
    hop_arrived(7)
    far_arrived(5, 6)

    def at_wait(k):
        p = lax.rem(b + k, 16)
        rcopy(attn_send.at[p], head_lanes(p), at_s.at[p], at_r.at[p], dev_tile(p)).wait()

    loop(1, 16, at_wait)

    def put_halves(ref, value):
        pad = jnp.zeros((TILE, 5 * PAD - half), F32)
        for k in range(2):
            piece = jnp.concatenate([value[:, k * half : (k + 1) * half], pad], axis=1)
            ref[:, k * 5 * PAD : (k + 1) * 5 * PAD] = piece.astype(BF16)

    def put_blocks(ref, value):
        pad = jnp.zeros((TILE, PAD - HEAD), F32)
        for k in range(16):
            zz = k % 4
            to = 4 * (k // 4) + 2 * (zz % 2) + zz // 2
            piece = jnp.concatenate([value[:, k * HEAD : (k + 1) * HEAD], pad], axis=1)
            ref[:, to * PAD : (to + 1) * PAD] = piece.astype(BF16)

    l_src, l_all = (l_mid, l_h2s, l_attns), (lb_down, lb_up, lb_out)
    r_src, r_all = (attn_in, r_gu, r_branchs), (rb_down, rb_up, rb_out)

    def slot_rows(i, t):
        return pl.ds(pl.multiple_of((i * 4 + t) * TILE, TILE), TILE)

    def lanes_at(k, n):
        return pl.ds(pl.multiple_of(k * n, PAD), n)

    def g_left(m, k, src, i, t, d):
        dst = l_all[m].at[slot_rows(i, t)]
        return rcopy(dst if src is None else src, dst, gl_s.at[m, k], gl_r.at[m, i * 4 + t], d)

    def g_right(m, k, src, i, t, d):
        n = r_src[m].shape[1] // 4
        dst = r_all[m].at[slot_rows(i, t)]
        if k in (2, 4, 5, 6):
            dst = r_all[m].at[slot_rows(i, t), lanes_at(1 - c, n)]
        return rcopy(dst if src is None else src, dst, gr_s.at[m, k], gr_r.at[m, i * 4 + t], d)

    def l_part(m, k):
        return l_src[m].at[:, lanes_at(k, l_src[m].shape[1] // 2)]

    def r_part(m, k, n):
        return r_src[m].at[:, lanes_at(k, n * (r_src[m].shape[1] // 4))]

    def g_first(m):
        return [
            g_left(m, 0, l_part(m, other), img, ty, to_x),
            g_right(m, 0, r_part(m, 1 - y, 2), img, ty, to_y),
            g_left(m, 1, l_part(m, img), img, ty, to_y),
            g_right(m, 1, r_part(m, y, 2), img, ty, to_x),
            g_left(m, 2, l_part(m, img), img, ty, to_c),
            g_right(m, 2, r_part(m, ty ^ 1, 1), img, ty, to_c),
        ]

    def g_own(m):
        n = r_src[m].shape[1] // 4
        rows = slot_rows(img, ty)
        return [
            pltpu.make_async_copy(l_part(m, img), l_all[m].at[rows], g_loc.at[m, 0]),
            pltpu.make_async_copy(
                r_part(m, ty, 1), r_all[m].at[rows, lanes_at(c, n)], g_loc.at[m, 1]
            ),
        ]

    def gl_x(m):
        g_first(m)[0].start()

    def gl_yc(m):
        g_first(m)[2].start()
        g_first(m)[4].start()
        g_own(m)[0].start()

    def gr_x(m):
        g_first(m)[3].start()

    def gr_yc(m):
        if m != 1:
            g_first(m)[1].start()
        g_first(m)[5].start()
        g_own(m)[1].start()

    def gu_lanes(i, k, base=0):
        n = hidden // 4
        return pl.ds(pl.multiple_of(base + lax.rem(2 * i + k, 4) * n, PAD), n)

    def gu_copy(w, k):
        dst = rb_up.at[slot_rows(img, ty ^ 2 if w == 2 else ty), gu_lanes(img, k)]
        src = dst
        if w < 2:
            src = r_gu.at[:, gu_lanes(img, k, (1 - y if w == 0 else y) * hidden)]
        return rcopy(src, dst, gu_s.at[w, k], gu_r.at[w, k], to_y if w == 0 else to_x)

    def gu_wait(w, k):
        i, t = (img, ty ^ 2) if w == 0 else (other, ty if w == 1 else ty ^ 2)
        ref = rb_up.at[slot_rows(i, t), gu_lanes(i, k)]
        rcopy(ref, ref, gu_s.at[w, k], gu_r.at[w, k], to_x).wait_recv()

    def gu_hop(k):
        gu_wait(0, k)
        gu_copy(2, k).start()

    def gl_hop(m):
        g_left(m, 0, None, other, ty, to_x).wait_recv()
        g_left(m, 3, None, other, ty, to_y).start()
        g_left(m, 4, None, other, ty, to_c).start()

    def gl_across(m):
        g_left(m, 1, None, img, ty ^ 2, to_y).wait_recv()
        g_left(m, 5, None, img, ty ^ 2, to_c).start()

    def gr_hop(m):
        if m != 1:
            g_right(m, 0, None, img, ty ^ 2, to_y).wait_recv()
            g_right(m, 3, None, img, ty ^ 2, to_x).start()
        g_right(m, 4, None, img, ty ^ 2, to_c).start()
        if m != 1:
            g_right(m, 1, None, other, ty, to_x).wait_recv()
        else:
            for k in range(4):
                gu_wait(1, k)
        g_right(m, 5, None, other, ty, to_c).start()

    def gl_hop2(m):
        g_left(m, 3, None, other, ty ^ 2, to_y).wait_recv()
        g_left(m, 6, None, other, ty ^ 2, to_c).start()

    def gr_hop2(m):
        if m != 1:
            g_right(m, 3, None, other, ty ^ 2, to_x).wait_recv()
        else:
            for k in range(4):
                gu_wait(2, k)
        g_right(m, 6, None, other, ty ^ 2, to_c).start()

    def g_done(m):
        n = r_src[m].shape[1] // 4
        for i in range(2):
            for t in (ty ^ 1, ty ^ 3):
                g_left(m, 2, None, i, t, to_c).wait_recv()
                ref = r_all[m].at[slot_rows(i, t), lanes_at(c, n)]
                rcopy(ref, ref, gr_s.at[m, 2], gr_r.at[m, i * 4 + t], to_c).wait_recv()
        for copy in g_own(m):
            copy.wait()

    def g_drain(m):
        for k, copy in enumerate(g_first(m)):
            if m != 1 or k not in (1, 3):
                copy.wait_send()
        for k, i, t in ((3, other, ty), (4, other, ty), (5, img, ty ^ 2), (6, other, ty ^ 2)):
            g_left(m, k, None, i, t, to_c).wait_send()
        for k, i, t in ((3, img, ty ^ 2), (4, img, ty ^ 2), (5, other, ty), (6, other, ty ^ 2)):
            if m != 1 or k != 3:
                g_right(m, k, None, i, t, to_c).wait_send()
        if m == 1:
            for w in range(3):
                for k in range(4):
                    gu_copy(w, k).wait_send()

    attn = jnp.concatenate(
        [attn_in[:, h * PAD : h * PAD + HEAD].astype(F32) for h in range(16)], axis=1
    )
    l_attn[...] = attn.astype(BF16)
    put_halves(l_attns, attn)
    own(OUT).wait()
    w_done(0)
    own_valid = tile_layout(b)[0]
    keep = jnp.where(own_valid, 1.0, 0.0)[:, 0:1]
    cols = width // 3

    def project(k):
        at = pl.ds(pl.multiple_of(k * cols, PAD), cols)
        branchv[:, at] = dot(l_attn[...], woutv[:, at])

    loop(0, 3, project)
    x = tok[...].astype(F32)
    x1 = x + keep * gate1() * branchv[...]
    x1v[...] = x1
    r = lax.rsqrt(jnp.mean(x1 * x1, axis=1, keepdims=True) + EPS)
    h2_rows = (x1 * r) * (1.0 + scale2()) + shift2()
    l_h2[...] = h2_rows.astype(BF16)
    put_halves(l_h2s, h2_rows)
    d_ffn = cot[...].astype(F32) * keep * gate2()
    r_ffn[...] = d_ffn.astype(BF16)
    put_blocks(attn_in, d_ffn)
    ffnv[...] = jnp.zeros_like(ffnv)
    dh2v[...] = jnp.zeros_like(dh2v)
    own(UP).wait()
    own(DOWN).wait()
    step = 256

    def mlp(j):
        g_at = pl.ds(pl.multiple_of(j, step), step)
        u_at = pl.ds(pl.multiple_of(hidden + j, step), step)
        h2 = l_h2[...]
        gate = dot(h2, wupv[:, g_at])
        up = dot(h2, wupv[:, u_at])
        sig = 1.0 / (1.0 + jnp.exp(-gate))
        act_g = gate * sig
        mid = (act_g * up).astype(BF16)
        l_mid[:, g_at] = mid
        w3 = wdownv[g_at, :]
        ffnv[...] += dot(mid, w3)
        d_mid = dot_nt(r_ffn[...], w3)
        d_gate = (d_mid * up * (sig + gate * sig * (1.0 - sig))).astype(BF16)
        d_up = (d_mid * act_g).astype(BF16)
        r_gu[:, g_at] = d_gate
        r_gu[:, u_at] = d_up
        dh2v[...] += dot_nt(d_gate, wupv[:, g_at]) + dot_nt(d_up, wupv[:, u_at])

    def mlp_quarter(k):
        first = lax.rem(2 * img + k, 4) * (hidden // 4)
        loop(0, hidden // 4 // step, lambda j: mlp(first + j * step))

    gl_x(1)
    w_done(1, 2)
    mlp_quarter(0)
    gu_copy(1, 0).start()
    far_arrived(7)
    hop_arrived(8, 9)
    w_done(3, 4)
    mlp_quarter(1)
    gu_copy(1, 1).start()
    hop_arrived(10)
    far_arrived(8, 9)
    w_done(5, 6, 7)
    mlp_quarter(2)
    gu_copy(1, 2).start()
    gu_copy(0, 0).start()
    far_arrived(10)
    w_done(8, 9, 10)
    mlp_quarter(3)
    gu_copy(1, 3).start()
    gu_copy(0, 1).start()
    ffn = ffnv[...]
    g = cot[...].astype(F32)
    x1 = x1v[...]
    mixed[...] = (x1 + keep * gate2() * ffn).astype(BF16)

    def dmod_put(k, row):
        dmod[0:1, k * width : (k + 1) * width] = row

    def colsum(v):
        return jnp.sum(v, axis=0, keepdims=True)

    dmod_put(5, colsum(g * keep * ffn))
    d_h2 = dh2v[...]
    norm2 = x1 * r
    dmod_put(4, colsum(d_h2 * norm2))
    dmod_put(3, colsum(d_h2))
    d_n2 = d_h2 * (1.0 + scale2())
    d_x1 = g + r * (d_n2 - norm2 * jnp.mean(d_n2 * norm2, axis=1, keepdims=True))
    dmod_put(2, colsum(d_x1 * keep * branchv[...]))
    x1v[...] = d_x1
    d_branch = d_x1 * keep * gate1()
    r_branch[...] = d_branch.astype(BF16)
    put_blocks(r_branchs, d_branch)

    def unproject(k):
        at = pl.ds(pl.multiple_of(k * cols, PAD), cols)
        branchv[:, at] = dot_nt(r_branch[...], woutv[at, :])

    loop(0, 3, unproject)

    zeros = jnp.zeros((TILE, PAD - HEAD), F32)
    d_attn = branchv[...]
    for h in range(16):
        attn_send[h] = jnp.concatenate(
            [d_attn[:, h * HEAD : (h + 1) * HEAD], zeros], axis=1
        ).astype(BF16)

    def do_copy(t):
        return rcopy(attn_send.at[t], do_in.at[b], do_s.at[t], do_r.at[b], dev_tile(t))

    loop(1, 16, lambda k: do_copy(lax.rem(b + k, 16)).start())
    do_in[b] = attn_send[b]
    gu_copy(0, 2).start()
    gu_copy(0, 3).start()
    x_arrived(11)
    gl_yc(1)
    gl_hop(1)
    gr_yc(1)
    gu_hop(0)
    gu_hop(1)
    gl_x(2)
    gl_yc(2)
    gr_yc(0)
    gr_yc(2)
    gl_yc(0)

    def do_wait(k):
        p = lax.rem(b + k, 16)
        rcopy(attn_send.at[p], do_in.at[p], do_s.at[p], do_r.at[p], dev_tile(p)).wait()

    loop(1, 16, do_wait)
    gu_hop(2)
    x_arrived(12)

    def delta(t):
        d = do_in[t].astype(F32)
        dsum = jnp.sum(jnp.where(lane < HEAD, d * onorm[t], 0.0), axis=1, keepdims=True)
        d = put_split3(d, -dsum, HEAD)
        do_in[t] = d.astype(BF16)
        dot_t[:, pl.ds(pl.multiple_of(t * TILE, TILE), TILE)] = d.T.astype(BF16)

    loop(0, 16, delta)
    gu_hop(3)
    gr_x(0)
    gl_x(0)
    gr_x(2)
    gl_hop(2)
    dqt[...] = jnp.zeros_like(dqt)

    high, low = z // 2, lax.rem(z, 2)
    l0 = 3 * width

    def z_load(m):
        kl, n = l_all[m].shape[1], r_src[m].shape[1] // 4
        copies = [
            pltpu.make_async_copy(
                l_all[m], wupv.at[pl.ds(0, 8 * TILE), pl.ds(l0, kl)], z_loc.at[0]
            ),
            pltpu.make_async_copy(
                r_all[m].at[:, lanes_at(c, n)],
                wupv.at[pl.ds(0, 8 * TILE), pl.ds(l0 + kl, n)],
                z_loc.at[1],
            ),
        ]
        for copy in copies:
            copy.start()
        for copy in copies:
            copy.wait()

    def z_copies(m):
        if m == 0:
            sent = [kt.at[pl.ds(0, 80), pl.ds(0, 12 * PAD)], qt.at[pl.ds(0, 80), pl.ds(0, 12 * PAD)]]
        elif m == 1:
            sent = [wupv.at[pl.ds(k * half, half), pl.ds(44 * PAD, 3 * PAD)] for k in range(2)]
        else:
            sent = [tok_all.at[pl.ds(640 + 128 * k, 80), pl.ds(0, 5 * PAD)] for k in range(2)]
        return [
            rcopy(sent[k], za[m].at[k], za_s.at[m, k], za_r.at[m, k], dev(k=z ^ 1))
            for k in range(2)
        ]

    za, zb = (za_down, za_up, za_out), (zb_down, zb_up, zb_out)
    z_rest = (
        dot_t.at[pl.ds(0, 80), pl.ds(0, 12 * PAD)],
        wdownv.at[pl.ds(19 * TILE, half), pl.ds(0, 3 * PAD)],
        tok_all.at[pl.ds(896, 80), pl.ds(0, 5 * PAD)],
    )
    z_own = (dqt.at[pl.ds(0, 80), pl.ds(0, 12 * PAD)], up_grad, z_out)

    def z_copy2(m):
        return rcopy(z_rest[m], zb[m], zb_s.at[m], zb_r.at[m], dev(k=z ^ 2))

    def z_product(m):
        kl = l_all[m].shape[1]
        sent = [copy.src_ref for copy in z_copies(m)]
        if m == 1:

            def turn(k):
                at = pl.ds(pl.multiple_of(k * TILE, TILE), TILE)
                woutv[0 : 5 * PAD, at] = wupv[at, l0 : l0 + kl].astype(F32).T.astype(BF16)

            loop(0, 8, turn)

            def block(zz):
                at = pl.ds(pl.multiple_of(l0 + kl + zz * 3 * PAD, PAD), 3 * PAD)
                return dot(woutv[0:half, 0 : 8 * TILE], wupv[0 : 8 * TILE, at])

            for k in range(2):
                sent[k][...] = block(2 * k + 1 - low).astype(BF16)
            for copy in z_copies(m):
                copy.start()
            z_rest[m][...] = block(2 * (1 - high) + low).astype(BF16)
            z_own[m][...] = block(z)
            return

        def pair(k):
            at = pl.ds(pl.multiple_of(l0 + kl + k * 2 * PAD, PAD), 2 * PAD)
            return dot_tn(wupv[0 : 8 * TILE, at], wupv[0 : 8 * TILE, l0 : l0 + kl])

        both = pair(1 - low)
        for k in range(2):
            sent[k][...] = both[k * PAD : k * PAD + 80].astype(BF16)
        for copy in z_copies(m):
            copy.start()
        both = pair(low)
        first, second = both[0:80], both[PAD : PAD + 80]
        z_rest[m][...] = jnp.where(high == 0, second, first).astype(BF16)
        z_own[m][...] = jnp.where(high == 0, first, second)

    def z_second(m):
        for copy in z_copies(m):
            copy.wait()
        rest = z_rest[m][...].astype(F32) + za[m][1 - high].astype(F32)
        z_rest[m][...] = rest.astype(BF16)
        z_copy2(m).start()
        z_own[m][...] += za[m][high].astype(F32)

    def z_last(m):
        z_copy2(m).wait()
        z_own[m][...] += zb[m][...].astype(F32)

    gain_grad[...] = jnp.zeros_like(gain_grad)
    for i in range(11):
        w_drain(i)

    def kv_send(k, u):
        at = pl.ds(pl.multiple_of(k * 2 * HEAD, 16), 2 * HEAD)
        return wdownv.at[at, pl.ds((3 + u) * PAD, PAD)]

    def q_send(k, u):
        at = pl.ds(pl.multiple_of(width + k * 80, 16), 80)
        return wdownv.at[at, pl.ds((3 + u) * PAD, PAD)]

    def kv_copy(k, u):
        t = 2 * k + u
        return rcopy(kv_send(k, u), dkv_in.at[b], dkv_s.at[t], dkv_r.at[b], dev_tile(t))

    def q_copy(k, u):
        t = 2 * k + u
        return rcopy(q_send(k, u), dq_in.at[b], dq_s.at[t], dq_r.at[b], dev_tile(t))

    def head_back(d, v, gain, row, t):
        c_, (s1, s2) = cosv[t], split_sin(sinv[t])
        d = unrope(d, c_, s1, s2)
        rr = lax.rsqrt(jnp.sum(v * v, axis=1, keepdims=True) * (1.0 / HEAD) + EPS)
        n = v * rr
        gain_grad[row : row + 1, :] += colsum(d * n)
        dn = d * gain[0:1, :]
        return rr * (dn - n * (jnp.sum(dn * n, axis=1, keepdims=True) * (1.0 / HEAD)))

    def send_tile(k, u, copy, keep_own):
        copy_ = copy(k, u)

        @pl.when(2 * k + u != b)
        def _():
            copy_.start()

        @pl.when(2 * k + u == b)
        def _():
            keep_own[b] = copy_.src_ref[...]

    def attend_back(k):
        two = pl.ds(2 * k, 2)
        p = jnp.exp(dot(ka[two].reshape(2 * TILE, PAD), qt[...]))
        ds = (p * dot(va[two].reshape(2 * TILE, PAD), dot_t[...])).astype(BF16)
        d_k2 = dot(ds, qa[...].reshape(16 * TILE, PAD))
        d_v2 = dot(p.astype(BF16), do_in[...].reshape(16 * TILE, PAD))
        at = pl.ds(pl.multiple_of(k * 2 * TILE, 2 * TILE), 2 * TILE)
        dqt[...] += dot(kt[:, at], ds)
        for u in range(2):
            t = 2 * k + u
            rows = slice(u * TILE, (u + 1) * TILE)
            d_k = head_back(d_k2[rows], kraw[t], k_gain, 1, t)
            d_v = jnp.where(lane < HEAD, d_v2[rows], 0.0)
            at = pl.ds(pl.multiple_of(t * TILE, TILE), TILE)
            wdownv[at, PAD : 3 * PAD] = jnp.concatenate([d_k, d_v], axis=1).astype(BF16)
            turned = jnp.concatenate([d_k.T[0:HEAD], d_v.T[0:HEAD]], axis=0)
            kv_send(k, u)[...] = turned.astype(BF16)
            send_tile(k, u, kv_copy, dkv_in)

    loop(0, 4, attend_back)
    gl_across(1)
    gr_hop(1)
    hop_arrived(11)
    loop(4, 8, attend_back)
    gl_hop2(1)
    gr_hop2(1)
    g_done(1)
    z_load(1)
    z_product(1)
    gl_hop(0)
    gr_hop(0)

    def heads_back(k):
        for u in range(2):
            t = 2 * k + u
            at = pl.ds(pl.multiple_of(t * TILE, TILE), TILE)
            d_q = dqt[:, at].T * HEAD ** (-0.5)
            d_q = head_back(d_q, qraw[t], q_gain, 0, t)
            wdownv[at, 0:PAD] = d_q.astype(BF16)
            q_send(k, u)[...] = d_q.T[0:80].astype(BF16)
            send_tile(k, u, q_copy, dq_in)

    loop(0, 8, heads_back)
    gr_hop(2)
    w_done(11, 12)
    w_drain(11)
    w_drain(12)


    sums_t = (branchv, ffnv, dh2v)
    for ref in sums_t:
        ref[...] = jnp.zeros((PAD, width), F32)

    def dw_rows(k):
        at = pl.ds(pl.multiple_of(k * 2 * TILE, TILE), 2 * TILE)
        term = dot_tn(wdownv[at, 0 : 3 * PAD], tok_all[at, :])
        for p in range(3):
            sums_t[p][...] += term[p * PAD : (p + 1) * PAD]

    loop(0, 8, dw_rows)
    half_pad = jnp.zeros((80, 5 * PAD - half), F32)
    for p in range(3):
        for i in range(2):
            piece = sums_t[p][0:80, i * half : (i + 1) * half]
            at = slice((3 * i + p) * 80, (3 * i + p + 1) * 80)
            tok_all[at, 0 : 5 * PAD] = jnp.concatenate([piece, half_pad], axis=1).astype(BF16)

    def dw_half(i):
        return tok_all.at[pl.ds(pl.multiple_of(i * 240, 16), 240), pl.ds(0, 5 * PAD)]

    dw_copy = rcopy(dw_half(other), dw_in, dw_sem.at[0], dw_sem.at[1], dev(i=other))
    dw_copy.start()

    loads = [
        pltpu.make_async_copy(
            src, wupv.at[pl.ds(owner * half, half), pl.ds(0, 3 * width)], loc.at[k]
        )
        for k, (src, owner) in enumerate(
            ((wqkv, img), (qkv_hbm.at[pl.ds(other * half, half)], other))
        )
    ]
    for load in loads:
        load.start()

    def dq_wait(k):
        p = lax.rem(b + k, 16)
        kv, q_ = dkv_in.at[p], dq_in.at[p]
        rcopy(kv, kv, dkv_s.at[p], dkv_r.at[p], dev_tile(p)).wait()
        rcopy(q_, q_, dq_s.at[p], dq_r.at[p], dev_tile(p)).wait()

    z_second(1)
    loop(1, 16, dq_wait)
    for m in (0, 2):
        gl_across(m)
        gl_hop2(m)
        gr_hop2(m)
    g_done(0)
    z_load(0)
    z_product(0)
    for load in loads:
        load.wait()

    def own_part(p):
        return slice(16 * TILE + p * TILE, 16 * TILE + (p + 1) * TILE)

    for p in range(3):
        got, r0 = (dq_in, 0) if p == 0 else (dkv_in, (p - 1) * HEAD)
        turned = jnp.concatenate(
            [got[h].astype(F32)[r0 : r0 + HEAD] for h in range(16)], axis=0
        )
        wdownv[own_part(p), :] = turned.T.astype(BF16)

    def h1_back(k):
        at = pl.ds(pl.multiple_of(k * cols, PAD), cols)
        dh2v[:, at] = sum(
            dot_nt(wdownv[own_part(p), :], wupv[at, p * width : (p + 1) * width])
            for p in range(3)
        )

    loop(0, 3, h1_back)
    d_h1 = dh2v[...]
    x = tok[...].astype(F32)
    r1 = lax.rsqrt(jnp.mean(x * x, axis=1, keepdims=True) + EPS)
    norm1 = x * r1
    dmod_put(1, colsum(d_h1 * norm1))
    dmod_put(0, colsum(d_h1))
    d_n1 = d_h1 * (1.0 + scale1())
    back = r1 * (d_n1 - norm1 * jnp.mean(d_n1 * norm1, axis=1, keepdims=True))
    tgrad[...] = (x1v[...] + back).astype(BF16)

    dsend[...] = jnp.zeros_like(dsend)
    for s in range(32):
        dsend[s, 0:1, 0:part] = dmod[0:1, s * part : (s + 1) * part]
        dsend[s, 1:3, 0:PAD] = gain_grad[0:2, :]

    def dm_copy(p):
        return rcopy(dsend.at[p], dbuf.at[me], dm_s.at[p], dm_r.at[me], dev_flat(p))

    loop(1, 32, lambda k: dm_copy(lax.rem(me + k, 32)).start())
    dbuf[me] = dsend[me]

    g_done(2)
    z_load(2)
    z_product(2)
    dw_copy.wait()
    dw_sum = dw_half(img)[...].astype(F32) + dw_in[...].astype(F32)

    def pc_send(p):
        return tok_all.at[pl.ds(1024 + 80 * p, 80), pl.ds(0, 5 * PAD)]

    for p in range(3):
        pc_send(p)[...] = dw_sum[80 * p : 80 * (p + 1)].astype(BF16)

    def pc_copy(p):
        group = 16 * p + b
        to, slot = group // 3, lax.rem(group, 3)
        return to, rcopy(
            pc_send(p), pc_in.at[slot], pc_s.at[p], pc_r.at[slot], dev_tile(to)
        )

    for p in range(3):
        to, copy = pc_copy(p)

        @pl.when(to != b)
        def _():
            copy.start()

        @pl.when(to == b)
        def _():
            pc_in[lax.rem(16 * p + b, 3)] = pc_send(p)[...]

    z_second(0)
    z_second(2)
    z_last(1)
    z_last(0)
    z_last(2)
    g_drain(0)
    g_drain(1)
    g_drain(2)
    down_grad[...] = z_own[0][0:HEAD, :]
    out_grad[...] = z_own[2][0:HEAD, 0:half]
    for slot in range(3):
        group = 3 * b + slot
        src = lax.rem(group, 16)

        @pl.when(src != b)
        def _():
            rcopy(
                pc_send(0), pc_in.at[slot], pc_s.at[0], pc_r.at[slot], dev_tile(src)
            ).wait_recv()

    for slot in range(3):
        at = slice(slot * HEAD, (slot + 1) * HEAD)
        qkv_grad[at, :] = pc_in[slot].astype(F32)[0:HEAD, 0:half]
    for p in range(3):
        to, copy = pc_copy(p)

        @pl.when(to != b)
        def _():
            copy.wait_send()

    def dm_wait(k):
        p = lax.rem(me + k, 32)
        rcopy(dsend.at[p], dbuf.at[p], dm_s.at[p], dm_r.at[p], dev_flat(p)).wait()

    loop(1, 32, dm_wait)
    sums = [
        lax.fori_loop(1, 16, lambda s, a, i=i: a + dbuf[16 * i + s], dbuf[16 * i])
        for i in range(2)
    ]
    gain_grad[...] = jnp.where(
        lax.broadcasted_iota(jnp.int32, (8, PAD), 0) < 2,
        pltpu.roll(sums[0] + sums[1], 7, 0)[:, 0:PAD],
        0.0,
    )
    row = lax.broadcasted_iota(jnp.int32, (8, 2 * PAD), 0)
    d_two = jnp.where(row == 0, sums[0][0:1, :], jnp.where(row == 1, sums[1][0:1, :], 0.0))
    row = lax.broadcasted_iota(jnp.int32, (8, width), 0)
    a_two = jnp.where(row == 0, actbuf[0], jnp.where(row == 1, actbuf[1], 0.0))
    ada_grad[...] = dot_tn(d_two, a_two, HIGH)[0:part, :]
    act_copy.wait_send()


def rope_table():
    table = np.zeros((PAD, 2 * PAD), np.float64)
    angle = np.arange(64)[:, None] * 10000.0 ** (-np.arange(18) / 18)
    for axis in range(2):
        rows = slice(64 * axis, 64 * axis + 64)
        for quarter in range(2):
            at = 36 * axis + 18 * quarter
            table[rows, at : at + 18] = np.cos(angle)
            table[rows, PAD + at : PAD + at + 18] = np.sin(angle)
    return table.astype(np.float32)


def run_block(tokens, cotangent, act, ada, wh, wout, wup, wdown, wqkv, q_gain, k_gain, hw):
    width, hidden = tokens.shape[1], wup.shape[1] // 2
    half, part = width // 2, ada.shape[0]
    vmem, any_ = pl.BlockSpec(memory_space=pltpu.VMEM), pl.BlockSpec(memory_space=pl.ANY)
    smem = pl.BlockSpec(memory_space=pltpu.SMEM)
    sds = jax.ShapeDtypeStruct
    v, dma = pltpu.VMEM, pltpu.SemaphoreType.DMA
    n_chunks = len(weight_chunks(width, hidden))
    tile16 = (16, TILE, PAD)
    out_shape = (
        sds((TILE, width), BF16),
        sds((TILE, width), BF16),
        sds((3 * HEAD, half), F32),
        sds((part, width), F32),
        sds((8, PAD), F32),
        sds((HEAD, hidden // 2), F32),
        sds((half, 3 * PAD), F32),
        sds((HEAD, half), F32),
        sds((width, 3 * width), BF16),
        sds((8 * TILE, hidden // 2), BF16),
        sds((8 * TILE, 5 * PAD), BF16),
        sds((8 * TILE, 5 * PAD), BF16),
        sds((8 * TILE, 8 * PAD), BF16),
        sds((8 * TILE, hidden), BF16),
        sds((8 * TILE, 8 * PAD), BF16),
    )
    scratch = [
        v((16 * TILE, width), BF16),
        v((width, 3 * PAD), BF16),
        v((width, width), BF16),
        v((width, 2 * hidden), BF16),
        v((hidden, width), BF16),
        v((2, 8, width), F32),
        v((2, 8, 2 * PAD), F32),
        v((32, 8, 2 * PAD), F32),
        v((8, 6 * width), F32),
        v(tile16, F32),
        v(tile16, F32),
        v(tile16, F32),
        v(tile16, F32),
        v(tile16, BF16),
        v(tile16, BF16),
        v(tile16, BF16),
        v((PAD, 16 * TILE), BF16),
        v((PAD, 16 * TILE), BF16),
        v(tile16, F32),
        v(tile16, BF16),
        v((TILE, 16 * PAD), BF16),
        v(tile16, BF16),
        v((PAD, 16 * TILE), BF16),
        v((PAD, 16 * TILE), F32),
        v((16, 2 * HEAD, PAD), BF16),
        v((16, 80, PAD), BF16),
        v((240, 5 * PAD), BF16),
        v((3, 80, 5 * PAD), BF16),
        v((TILE, width), F32),
        v((TILE, width), F32),
        v((TILE, width), F32),
        v((TILE, width), F32),
        v((8, 6 * width), F32),
        v((32, 8, 2 * PAD), F32),
        v((32, 8, 2 * PAD), F32),
        v((TILE, width), BF16),
        v((TILE, width), BF16),
        v((TILE, hidden), BF16),
        v((TILE, width), BF16),
        v((TILE, width), BF16),
        v((TILE, 2 * hidden), BF16),
        v((TILE, 10 * PAD), BF16),
        v((TILE, 10 * PAD), BF16),
        v((TILE, 16 * PAD), BF16),
        v((2, 80, hidden // 2), BF16),
        v((2, half, 3 * PAD), BF16),
        v((2, 80, 5 * PAD), BF16),
        v((80, hidden // 2), BF16),
        v((half, 3 * PAD), BF16),
        v((80, 5 * PAD), BF16),
        v((80, 5 * PAD), F32),
        dma((3, 8)),
        dma((3, 8)),
        dma((3, 8)),
        dma((3, 8)),
        dma((3, 4)),
        dma((3, 4)),
        dma((3, 2)),
        dma((3, 2)),
        dma((3, 2)),
        dma((3,)),
        dma((3,)),
        dma((2,)),
        dma((16, 4)),
        dma((16,)),
        dma,
        dma((n_chunks, 10)),
        dma((n_chunks, 10)),
        dma((4,)),
        dma((2,)),
        dma((2,)),
        dma((32,)),
        dma((32,)),
        dma((16,)),
        dma((16,)),
        dma((16,)),
        dma((16,)),
        dma((16,)),
        dma((16,)),
        dma((16,)),
        dma((16,)),
        dma((2,)),
        dma((3,)),
        dma((3,)),
        dma((32,)),
        dma((32,)),
        dma((2,)),
    ]
    return pl.pallas_call(
        block_kernel,
        out_shape=out_shape,
        in_specs=[vmem] * 5 + [any_] * 4 + [vmem] * 3 + [smem],
        out_specs=[vmem] * 8 + [any_] * 7,
        scratch_shapes=scratch,
        compiler_params=pltpu.CompilerParams(
            collective_id=0, has_side_effects=True, vmem_limit_bytes=VMEM_LIMIT
        ),
    )(tokens, cotangent, act, ada, wh, wout, wup, wdown, wqkv, q_gain, k_gain, rope_table(), hw)


def head_weight(weight):
    at = lax.axis_index(("ty", "tx")) * HEAD
    width = weight.shape[1] // 3
    parts = [
        lax.dynamic_slice_in_dim(weight, p * width + at, HEAD, axis=1) for p in range(3)
    ]
    return jnp.concatenate([jnp.pad(p, ((0, 0), (0, PAD - HEAD))) for p in parts], axis=1)


def fast_body(
    tokens,
    cotangent,
    class_embed,
    timestep,
    grid_height,
    grid_width,
    qkv_weight,
    out_weight,
    up_weight,
    down_weight,
    ada_weight,
    q_gain,
    k_gain,
):
    width = tokens.shape[2]
    act = jax.nn.silu(class_embed + time_embed(timestep, width)).astype(BF16).astype(F32)
    pad = lambda g: jnp.broadcast_to(jnp.pad(g, (0, PAD - HEAD))[None], (8, PAD))
    (mixed, tgrad, qkv_grad, ada_grad, gains, down_grad, up_grad, out_grad) = (
        run_block(
            tokens[0],
            cotangent[0],
            jnp.broadcast_to(act, (8, width)),
            ada_weight,
            head_weight(qkv_weight),
            out_weight,
            up_weight,
            down_weight,
            qkv_weight,
            pad(q_gain),
            pad(k_gain),
            jnp.concatenate([grid_height, grid_width]),
        )[:8]
    )
    return (
        mixed[None],
        tgrad[None],
        qkv_grad.T,
        out_grad.T,
        up_grad,
        down_grad.T,
        ada_grad,
        gains[0, :HEAD],
        gains[1, :HEAD],
    )


def solution(mesh):
    in_specs = (
        P("img", ("ty", "tx"), None),
        P("img", ("ty", "tx"), None),
        P("img", None),
        P("img"),
        P("img"),
        P("img"),
        P("img", None),
        P("img", None),
        P("img", None),
        P("img", None),
        P(("img", "ty", "tx"), None),
        P(),
        P(),
    )
    out_specs = (
        P("img", ("ty", "tx"), None),
        P("img", ("ty", "tx"), None),
        P("img", ("ty", "tx")),
        P("img", ("ty", "tx")),
        P("img", ("ty", "tx")),
        P("img", ("ty", "tx")),
        P(("img", "ty", "tx"), None),
        P(),
        P(),
    )
    shape = dict(mesh.shape)
    fast = (shape["img"], shape["ty"], shape["tx"]) == (2, 4, 4)
    body = fast_body if fast else general_body
    return jax.shard_map(body, mesh=mesh, in_specs=in_specs, out_specs=out_specs, check_vma=False)
```

```python
import functools

import jax
import jax.numpy as jnp
import numpy as np
from jax import lax
from jax.experimental import pallas as pl
from jax.experimental.pallas import tpu as pltpu
from jax.sharding import PartitionSpec as P

HEADS = 16
HEAD = 72


EPS = 1e-06
HIGH = lax.Precision.HIGHEST


def layout(slot, height, width, cap, rows_tiles, cols_tiles):
    tile = slot // cap
    row_tile = tile // cols_tiles
    col_tile = tile % cols_tiles
    local = slot % cap
    top = row_tile * height // rows_tiles
    bottom = (row_tile + 1) * height // rows_tiles
    left = col_tile * width // cols_tiles
    right = (col_tile + 1) * width // cols_tiles
    span = right - left
    valid = local < (bottom - top) * span
    row = jnp.where(valid, top + local // span, 0)
    col = jnp.where(valid, left + local % span, 0)
    return (valid, row, col)


def time_embed(step, dim):
    half = dim // 2
    freq = jnp.exp(-jnp.log(10000.0) * jnp.arange(half, dtype=jnp.float32) / half)
    angle = step.astype(jnp.float32)[:, None] * freq
    return jnp.concatenate([jnp.cos(angle), jnp.sin(angle)], axis=-1)


def rotate(part, position):
    quarter = part.shape[-1] // 2
    freq = jnp.exp(-jnp.log(10000.0) * jnp.arange(quarter, dtype=jnp.float32) / quarter)
    angle = position.astype(jnp.float32)[..., None, None] * freq
    first, second = (part[..., :quarter], part[..., quarter:])
    cosine, sine = (jnp.cos(angle), jnp.sin(angle))
    return jnp.concatenate(
        [first * cosine - second * sine, second * cosine + first * sine], axis=-1
    )


def rope(heads, row, col):
    half = heads.shape[-1] // 2
    return jnp.concatenate(
        [rotate(heads[..., :half], row), rotate(heads[..., half:], col)], axis=-1
    )


def head_norm(value, gain):
    return value * lax.rsqrt(jnp.mean(value * value, axis=-1, keepdims=True) + EPS) * gain


def rms(value):
    return value * lax.rsqrt(jnp.mean(value * value, axis=-1, keepdims=True) + EPS)


def flat_rows(value):
    return value.reshape(-1, value.shape[-1])


def outer_sum(left, right):
    return lax.dot_general(
        flat_rows(left),
        flat_rows(right),
        (((0,), (0,)), ((), ())),
        preferred_element_type=jnp.float32,
    )


def times_transposed(left, weight):
    return lax.dot_general(
        left, weight, (((left.ndim - 1,), (1,)), ((), ())), preferred_element_type=jnp.float32
    )


def masked_scores(query, keys_all, key_valid):
    scores = jnp.einsum("qhd,khd->hqk", query, keys_all, preferred_element_type=jnp.float32)
    return jnp.where(key_valid[None, None, :], scores, -1e30)


def general_body(
    tokens,
    cotangent,
    class_embed,
    timestep,
    grid_height,
    grid_width,
    qkv_weight,
    out_weight,
    up_weight,
    down_weight,
    ada_weight,
    q_gain,
    k_gain,
):
    images, slots_dev, width = tokens.shape
    rows_tiles = lax.axis_size("ty")
    cols_tiles = lax.axis_size("tx")
    slots_all = slots_dev * rows_tiles * cols_tiles
    own_slot = lax.axis_index(("ty", "tx")) * slots_dev + jnp.arange(slots_dev, dtype=jnp.int32)
    all_slot = jnp.arange(slots_all, dtype=jnp.int32)
    valid_q, row_q, col_q = jax.vmap(
        lambda h, w: layout(own_slot, h, w, slots_dev, rows_tiles, cols_tiles)
    )(grid_height, grid_width)
    valid_k = jax.vmap(lambda h, w: layout(all_slot, h, w, slots_dev, rows_tiles, cols_tiles)[0])(
        grid_height, grid_width
    )
    keep = valid_q.astype(jnp.float32)[..., None]
    act = jax.nn.silu(class_embed + time_embed(timestep, width)).astype(jnp.bfloat16)
    mod = lax.dot_general(
        act,
        lax.all_gather(ada_weight, ("img", "ty", "tx"), axis=0, tiled=True),
        (((1,), (1,)), ((), ())),
        preferred_element_type=jnp.float32,
    )
    shift1, scale1, gate1, shift2, scale2, gate2 = [
        part[:, None, :] for part in jnp.split(mod, 6, axis=1)
    ]
    wqkv, wout, w12, w3 = (
        lax.all_gather(qkv_weight, "img", axis=0, tiled=True),
        lax.all_gather(out_weight, "img", axis=0, tiled=True),
        lax.all_gather(up_weight, "img", axis=0, tiled=True),
        lax.all_gather(down_weight, "img", axis=0, tiled=True),
    )
    xf = tokens.astype(jnp.float32)
    norm1, pull_norm1 = jax.vjp(rms, xf)
    h1 = (norm1 * (1.0 + scale1) + shift1).astype(jnp.bfloat16)
    qkv = jnp.dot(h1, wqkv, preferred_element_type=jnp.float32).reshape(
        images, slots_dev, 3, HEADS, HEAD
    )

    def finish(query_raw, key_raw, query_gain, key_gain):
        query = rope(head_norm(query_raw, query_gain), row_q, col_q) * HEAD ** (-0.5)
        return (query, rope(head_norm(key_raw, key_gain), row_q, col_q))

    (query_f, key_f), pull_heads = jax.vjp(finish, qkv[:, :, 0], qkv[:, :, 1], q_gain, k_gain)
    query_b = query_f.astype(jnp.bfloat16)
    key_b = key_f.astype(jnp.bfloat16)
    value_b = qkv[:, :, 2].astype(jnp.bfloat16)
    keys_all, values_all = (
        lax.all_gather(key_b, ("ty", "tx"), axis=1, tiled=True),
        lax.all_gather(value_b, ("ty", "tx"), axis=1, tiled=True),
    )
    index = 0
    scores = masked_scores(query_b[index], keys_all[index], valid_k[index])
    top = jnp.max(scores, axis=-1, keepdims=True)
    lse = top + jnp.log(jnp.sum(jnp.exp(scores - top), axis=-1, keepdims=True))
    prob = jnp.exp(scores - lse).astype(jnp.bfloat16)
    attn_list = [
        jnp.einsum("hqk,khd->qhd", prob, values_all[index], preferred_element_type=jnp.float32)
    ]
    lse_list = [lse]
    attn = jnp.stack(attn_list).reshape(images, slots_dev, width).astype(jnp.bfloat16)
    branch = jnp.dot(attn, wout, preferred_element_type=jnp.float32)
    x1 = xf + keep * gate1 * branch
    norm2, pull_norm2 = jax.vjp(rms, x1)
    h2 = (norm2 * (1.0 + scale2) + shift2).astype(jnp.bfloat16)
    gate_up = jnp.dot(h2, w12, preferred_element_type=jnp.float32)
    hidden = gate_up.shape[-1] // 2
    gate_part, up_part = (gate_up[..., :hidden], gate_up[..., hidden:])
    sig = jax.nn.sigmoid(gate_part)
    silu_gate = gate_part * sig
    mid = (silu_gate * up_part).astype(jnp.bfloat16)
    ffn = jnp.dot(mid, w3, preferred_element_type=jnp.float32)
    mixed = (x1 + keep * gate2 * ffn).astype(jnp.bfloat16)
    grad_out = cotangent.astype(jnp.float32)
    d_gate2 = jnp.sum(grad_out * keep * ffn, axis=1)
    d_ffn = (grad_out * keep * gate2).astype(jnp.bfloat16)
    term_down = outer_sum(mid, d_ffn)
    d_mid = times_transposed(d_ffn, w3)
    d_gate = d_mid * up_part * (sig + gate_part * sig * (1.0 - sig))
    d_up = d_mid * silu_gate
    d_gate_up = jnp.concatenate([d_gate, d_up], axis=-1).astype(jnp.bfloat16)
    term_up = outer_sum(h2, d_gate_up)
    d_h2 = times_transposed(d_gate_up, w12)
    d_scale2 = jnp.sum(d_h2 * norm2, axis=1)
    d_shift2 = jnp.sum(d_h2, axis=1)
    d_x1 = grad_out + pull_norm2(d_h2 * (1.0 + scale2))[0]
    d_gate1 = jnp.sum(d_x1 * keep * branch, axis=1)
    d_branch = (d_x1 * keep * gate1).astype(jnp.bfloat16)
    term_out = outer_sum(attn, d_branch)
    d_attn = (
        times_transposed(d_branch, wout)
        .astype(jnp.bfloat16)
        .reshape(images, slots_dev, HEADS, HEAD)
    )
    keys_back, values_back = (
        lax.all_gather(key_b, ("ty", "tx"), axis=1, tiled=True),
        lax.all_gather(value_b, ("ty", "tx"), axis=1, tiled=True),
    )
    index = 0
    scores = masked_scores(query_b[index], keys_back[index], valid_k[index])
    prob = jnp.exp(scores - lse_list[index])
    d_prob = jnp.einsum(
        "qhd,khd->hqk", d_attn[index], values_back[index], preferred_element_type=jnp.float32
    )
    delta = jnp.sum(prob * d_prob, axis=-1, keepdims=True)
    d_scores = (prob * (d_prob - delta)).astype(jnp.bfloat16)
    dq_list = [
        jnp.einsum("hqk,khd->qhd", d_scores, keys_back[index], preferred_element_type=jnp.float32)
    ]
    dk_list = [
        jnp.einsum("hqk,qhd->khd", d_scores, query_b[index], preferred_element_type=jnp.float32)
    ]
    dv_list = [
        jnp.einsum(
            "hqk,qhd->khd",
            prob.astype(jnp.bfloat16),
            d_attn[index],
            preferred_element_type=jnp.float32,
        )
    ]
    d_key, d_value = (
        lax.psum_scatter(
            jnp.stack(dk_list).astype(jnp.bfloat16), ("ty", "tx"), scatter_dimension=1, tiled=True
        ).astype(jnp.float32),
        lax.psum_scatter(
            jnp.stack(dv_list).astype(jnp.bfloat16), ("ty", "tx"), scatter_dimension=1, tiled=True
        ).astype(jnp.float32),
    )
    d_query_raw, d_key_raw, d_q_gain, d_k_gain = pull_heads((jnp.stack(dq_list), d_key))
    d_qkv = (
        jnp.stack([d_query_raw, d_key_raw, d_value], axis=2)
        .reshape(images, slots_dev, 3 * width)
        .astype(jnp.bfloat16)
    )
    term_qkv = outer_sum(h1, d_qkv)
    d_h1 = times_transposed(d_qkv, wqkv)
    d_scale1 = jnp.sum(d_h1 * norm1, axis=1)
    d_shift1 = jnp.sum(d_h1, axis=1)
    tokens_grad = (d_x1 + pull_norm1(d_h1 * (1.0 + scale1))[0]).astype(jnp.bfloat16)
    d_mod = jnp.concatenate([d_shift1, d_scale1, d_gate1, d_shift2, d_scale2, d_gate2], axis=1)
    act_f = act.astype(jnp.float32)
    ada_grad = lax.psum_scatter(
        lax.dot_general(
            d_mod,
            act_f,
            (((0,), (0,)), ((), ())),
            precision=HIGH,
            preferred_element_type=jnp.float32,
        ),
        ("img", "ty", "tx"),
        scatter_dimension=0,
        tiled=True,
    )
    q_gain_grad, k_gain_grad = lax.psum((d_q_gain, d_k_gain), ("img", "ty", "tx"))
    parts = (
        lax.psum_scatter(
            term_qkv.astype(jnp.bfloat16), ("ty", "tx"), scatter_dimension=1, tiled=True
        ).astype(jnp.float32),
        lax.psum_scatter(
            term_out.astype(jnp.bfloat16), ("ty", "tx"), scatter_dimension=1, tiled=True
        ).astype(jnp.float32),
        lax.psum_scatter(
            term_up.astype(jnp.bfloat16), ("ty", "tx"), scatter_dimension=1, tiled=True
        ).astype(jnp.float32),
        lax.psum_scatter(
            term_down.astype(jnp.bfloat16), ("ty", "tx"), scatter_dimension=1, tiled=True
        ).astype(jnp.float32),
    )
    grads = (
        lax.psum_scatter(
            parts[0].astype(jnp.bfloat16), "img", scatter_dimension=0, tiled=True
        ).astype(jnp.float32),
        lax.psum_scatter(
            parts[1].astype(jnp.bfloat16), "img", scatter_dimension=0, tiled=True
        ).astype(jnp.float32),
        lax.psum_scatter(
            parts[2].astype(jnp.bfloat16), "img", scatter_dimension=0, tiled=True
        ).astype(jnp.float32),
        lax.psum_scatter(
            parts[3].astype(jnp.bfloat16), "img", scatter_dimension=0, tiled=True
        ).astype(jnp.float32),
    )
    return (
        mixed,
        tokens_grad,
        grads[0],
        grads[1],
        grads[2],
        grads[3],
        ada_grad,
        q_gain_grad,
        k_gain_grad,
    )


VMEM_LIMIT = 63 << 20
MESH = pl.DeviceIdType.MESH
PAD = 128
TILE = 128
F32 = jnp.float32
BF16 = jnp.bfloat16


def dot(a, b):
    return lax.dot_general(a, b, (((1,), (0,)), ((), ())), preferred_element_type=F32)


def dot_nt(a, b):
    return lax.dot_general(a, b, (((1,), (1,)), ((), ())), preferred_element_type=F32)


def dot_tn(a, b, precision=None):
    return lax.dot_general(
        a, b, (((0,), (0,)), ((), ())), preferred_element_type=F32, precision=precision
    )


def lanes(shape):
    return lax.broadcasted_iota(jnp.int32, shape, len(shape) - 1)


def split3(value):
    high = value.astype(BF16)
    rest = value - high.astype(F32)
    mid = rest.astype(BF16)
    low = (rest - mid.astype(F32)).astype(BF16)
    return (high, mid, low)


def put_split3(tile, value, lane0):
    at = lanes(tile.shape)
    for k, term in enumerate(split3(value)):
        tile = jnp.where(at == lane0 + k, jnp.broadcast_to(term.astype(F32), tile.shape), tile)
    return tile


OUT, UP, DOWN, QKV = range(4)


def weight_chunks(width, hidden):
    half = width // 2
    quarter = hidden // 4

    def up(k):
        return [(UP, 2 * k + u, 0, half, quarter, "yz") for u in range(2)]

    return (
        [(OUT, 0, 0, half, width, "z")]
        + up(0)
        + up(1)
        + up(2)
        + [(DOWN, 0, 0, quarter, width, "yz")]
        + up(3)
        + [(DOWN, 0, quarter, quarter, width, "yz")]
        + [(QKV, 0, 0, half, 14 * PAD, "z"), (QKV, 1, 0, half, 13 * PAD, "")]
    )


def block_kernel(
    tok, cot, act_row, ada, wout, wup, wdown, wqkv, q_gain_row, k_gain_row, tab, grid_h, grid_w,
    mixed, tgrad, qkv_grad, ada_grad, gain_grad, down_grad, up_grad, out_grad, qkv_hbm,
    lb_down, lb_up, lb_out, rb_down, rb_up, rb_out,
    act, q_gain, k_gain, win, win_sem, tok_all, whv, woutv, wupv, wdownv, actbuf, modsend, modbuf, modv,
    cosv, sinv, qraw, kraw, qa, ka, va, kt, qt, onorm, attn_send, attn_in,
    do_in, dot_t, dqt, dkv_in, dq_in, dw_in, pc_in,
    x1v, branchv, ffnv, dh2v, dmod, dsend, dbuf,
    l_attn, l_h2, l_mid, r_ffn, r_branch, r_gu, l_h2s, l_attns, r_branchs,
    za_down, za_up, za_out, zb_down, zb_up, zb_out, z_out,
    gl_s, gl_r, gr_s, gr_r, gu_s, gu_r, g_loc, za_s, za_r, zb_s, zb_r, z_loc,
    tok_send, tok_recv, tok_loc, w_send, w_recv, w_loc, wh_sem, act_sem, mod_s, mod_r,
    at_s, at_r, do_s, do_r, dq_s, dq_r, dkv_s, dkv_r, dw_sem, pc_s, pc_r, dm_s, dm_r, loc,
):
    img, ty, z = lax.axis_index("img"), lax.axis_index("ty"), lax.axis_index("tx")
    b = ty * 4 + z
    me = img * 16 + b
    width = tok.shape[1]
    half = width // 2
    hidden = wup.shape[1] // 2
    part = ada.shape[0]
    other = 1 - img

    def dev(i=img, t=ty, k=z):
        return {"img": i, "ty": t, "tx": k}

    def dev_flat(p):
        return dev(p // 16, lax.rem(p // 4, 4), lax.rem(p, 4))

    def dev_tile(t):
        return dev(img, t // 4, lax.rem(t, 4))

    def rcopy(src, dst, s, r, d):
        return pltpu.make_async_remote_copy(
            src_ref=src, dst_ref=dst, send_sem=s, recv_sem=r, device_id=d, device_id_type=MESH
        )

    def loop(lo, hi, f):
        def step(k, c):
            f(k)
            return c

        lax.fori_loop(lo, hi, step, 0)

    bar = pltpu.get_barrier_semaphore()
    loop(
        1, 32,
        lambda k: pl.semaphore_signal(
            bar, inc=1, device_id=dev_flat(lax.rem(me + k, 32)), device_id_type=MESH
        ),
    )
    pl.semaphore_wait(bar, 31)

    hbm = (wout, wup, wdown, wqkv)
    vm = (woutv, wupv, wdownv, qkv_hbm)
    chunks = weight_chunks(width, hidden)

    y, c, z_bit = ty // 2, lax.rem(ty, 2), lax.rem(z, 2)
    to_x, to_y, to_z, to_c = dev(i=other), dev(t=ty ^ 2), dev(k=z ^ 1), dev(t=ty ^ 1)
    OWN, FROM_Y, FROM_Z, FAR_A, FAR_B, SIBLING = range(6)

    def w_ref(ref, i, row0, im, rel, sib=False):
        m, k, r0, rows, cols, ways = chunks[i]
        yy = 1 - y if rel in (FROM_Y, FAR_A, FAR_B) else y
        zz = 1 - z_bit if rel in (FROM_Z, FAR_A, FAR_B) else z_bit
        cc = 1 - c if sib else c
        col = k * 14 * PAD if m == QKV else 0
        if m == UP:
            col = (k % 2) * hidden + lax.rem(2 * im + k // 2, 4) * (hidden // 4)
        if ways == "yz" and m == UP:
            n, p = rows // 4, 2 * yy + zz
            cols = cols // 2
            col = col + cc * cols
        elif ways == "yz":
            n, p = rows // 8, 4 * yy + 2 * zz + cc
        elif ways == "":
            n, p = rows // 2, cc
        else:
            n, p = rows // 4, 2 * (yy if ways == "y" else zz) + cc
        row, size, first = row0 + r0 + p * n, n, (n // 32 + (n // 16) % 2) * 16
        if rel == FAR_A:
            size = first
        if rel == FAR_B:
            row, size = row + first, n - first
        return ref.at[
            pl.ds(pl.multiple_of(row, 16), size), pl.ds(pl.multiple_of(col, PAD), cols)
        ]

    def w_mine(i, rel, sib=False):
        m = chunks[i][0]
        return w_ref(vm[m], i, other * hbm[m].shape[0], img, rel, sib)

    def w_x(i):
        m = chunks[i][0]
        src = w_ref(hbm[m], i, 0, other, OWN)
        dst = w_ref(vm[m], i, img * hbm[m].shape[0], other, OWN)
        return rcopy(src, dst, w_send.at[i, 0], w_recv.at[i, 0], to_x)

    def w_copy(i, slot, held, rel, to):
        ref = w_mine(i, held)
        return rcopy(ref, ref, w_send.at[i, slot], w_recv.at[i, rel], to)

    def w_wait(i, rel, sib=False):
        ref = w_mine(i, rel, sib)
        at = rel + SIBLING if sib else rel
        rcopy(ref, ref, w_send.at[i, 0], w_recv.at[i, at], to_c).wait_recv()

    def w_sends(i):
        ways = chunks[i][5]
        first = [w_copy(i, 1, OWN, SIBLING + OWN, to_c)]
        if "y" in ways:
            first.append(w_copy(i, 2, OWN, FROM_Y, to_y))
        if "z" in ways:
            first.append(w_copy(i, 3, OWN, FROM_Z, to_z))
        sends = {OWN: first}
        if "z" in ways:
            sends[FROM_Z] = [w_copy(i, 4, FROM_Z, SIBLING + FROM_Z, to_c)]
        if "y" in ways:
            sends[FROM_Y] = [w_copy(i, 5, FROM_Y, SIBLING + FROM_Y, to_c)]
        if ways == "yz":
            far_a, far_b = w_far(i)
            sends[FROM_Z].insert(0, far_a)
            sends[FROM_Y].insert(0, far_b)
            sends[FAR_A] = [w_copy(i, 8, FAR_A, SIBLING + FAR_A, to_c)]
            sends[FAR_B] = [w_copy(i, 9, FAR_B, SIBLING + FAR_B, to_c)]
        return sends

    def w_far(i):
        m, _, _, rows, _, _ = chunks[i]
        n = rows // (4 if m == UP else 8)
        first = (n // 32 + (n // 16) % 2) * 16
        a = w_mine(i, FROM_Z).at[pl.ds(0, first)]
        b_ = w_mine(i, FROM_Y).at[pl.ds(first, n - first)]
        return (
            rcopy(a, a, w_send.at[i, 6], w_recv.at[i, FAR_A], to_y),
            rcopy(b_, b_, w_send.at[i, 7], w_recv.at[i, FAR_B], to_z),
        )

    def w_pass(which, rels):
        for i in which:
            sends = w_sends(i)
            for rel in rels:
                if rel in sends:
                    w_wait(i, rel)
                    for copy in sends[rel]:
                        copy.start()

    def x_arrived(*which):
        w_pass(which, (OWN,))

    def hop_arrived(*which):
        w_pass(which, (FROM_Z, FROM_Y))

    def far_arrived(*which):
        w_pass(which, (FAR_A, FAR_B))

    def w_done(*which):
        for i in which:
            for rel in w_sends(i):
                w_wait(i, rel, True)

    def w_drain(i):
        w_x(i).wait_send()
        for copies in w_sends(i).values():
            for copy in copies:
                copy.wait_send()

    def own(m):
        rows = hbm[m].shape[0]
        return pltpu.make_async_copy(hbm[m], vm[m].at[pl.ds(img * rows, rows)], w_loc.at[m])

    act[...] = jnp.broadcast_to(act_row[...], (8, width))
    gain_pad = jnp.zeros((1, PAD - HEAD), F32)
    q_gain[...] = jnp.concatenate([q_gain_row[...], gain_pad], axis=1)
    k_gain[...] = jnp.concatenate([k_gain_row[...], gain_pad], axis=1)

    def window(p):
        first = p * width + b * HEAD
        start = jnp.minimum(first // PAD * PAD, 3 * width - 2 * PAD)
        return pl.multiple_of(start, PAD), first - start

    wins = [
        pltpu.make_async_copy(
            wqkv.at[:, pl.ds(window(p)[0], 2 * PAD)], win.at[p], win_sem.at[p]
        )
        for p in range(3)
    ]
    for copy in wins:
        copy.start()
    act_copy = rcopy(act, actbuf.at[img], act_sem.at[0], act_sem.at[1], dev(i=other))
    act_copy.start()
    actbuf[img] = act[...]
    own_wh = whv.at[pl.ds(pl.multiple_of(img * half, 64), half)]
    wh_copy = rcopy(own_wh, own_wh, wh_sem.at[0], wh_sem.at[1], dev(i=other))
    for i in range(3):
        w_x(i).start()

    def tok_at(chunk):
        return tok_all.at[pl.ds(pl.multiple_of(chunk * TILE, TILE), TILE)]

    def tok_half(q):
        return tok_all.at[pl.ds(pl.multiple_of(q * 64, 64), 64)]

    def t_send(src, q, way, d):
        return rcopy(src, tok_half(q), tok_send.at[q, way], tok_recv.at[q], d)

    def t_wait(q):
        t_send(tok_half(q), q, 0, to_c).wait_recv()

    tok_own = pltpu.make_async_copy(tok, tok_at(b), tok_loc)
    tok_own.start()

    def t_forward(src, chunk, up, down):
        if up:

            @pl.when(z < 3)
            def _():
                t_send(src, chunk, 0, dev(k=z + 1)).start()

        if down:

            @pl.when(z > 0)
            def _():
                t_send(src, chunk, 1, dev(k=z - 1)).start()

        t_send(src, chunk, 2, dev(t=ty ^ 2)).start()
        t_send(src, chunk, 3, dev(t=ty ^ 1)).start()

    for h in range(2):
        t_forward(tok.at[pl.ds(64 * h, 64)], 2 * b + h, True, True)
    for m in range(3):
        own(m).start()

    act_copy.wait_recv()
    for i in range(2):
        modsend[i, :, 0:part] = dot_nt(actbuf[i].astype(BF16), ada[...])

    def mod_copy(p):
        return rcopy(modsend.at[p // 16], modbuf.at[me], mod_s.at[p], mod_r.at[me], dev_flat(p))

    loop(1, 32, lambda k: mod_copy(lax.rem(me + k, 32)).start())
    modbuf[me] = modsend[img]
    for p in range(3):
        wins[p].wait()
        shift = 2 * PAD - window(p)[1]
        cols_p = pltpu.roll(win[p].astype(F32), shift, 1)[:, 0:PAD]
        at_lane = lax.broadcasted_iota(jnp.int32, (half, PAD), 1)
        own_wh[:, p * PAD : (p + 1) * PAD] = jnp.where(at_lane < HEAD, cols_p, 0.0).astype(BF16)
    wh_copy.start()
    for i in range(3, len(chunks)):
        w_x(i).start()

    for s in (1, 2, 3):
        for h in range(2):

            @pl.when(z - s >= 0)
            def _():
                q = 2 * (b - s) + h
                t_wait(q)
                t_forward(tok_half(q), q, True, False)

            @pl.when(z + s <= 3)
            def _():
                q = 2 * (b + s) + h
                t_wait(q)
                t_forward(tok_half(q), q, False, True)

    x_arrived(0, 1, 2)

    def t_y(k):
        q = (ty ^ 2) * 8 + k
        t_wait(q)
        t_send(tok_half(q), q, 3, to_c).start()

    loop(0, 8, t_y)
    hop_arrived(0)
    loop(0, 8, lambda k: t_wait((ty ^ 1) * 8 + k))
    loop(0, 8, lambda k: t_wait((ty ^ 3) * 8 + k))

    def t_drain(k):
        q, zz = ty * 8 + k, k // 2
        ref = tok_half(q)

        @pl.when((zz <= z) & (z < 3))
        def _():
            t_send(ref, q, 0, to_c).wait_send()

        @pl.when((zz >= z) & (z > 0))
        def _():
            t_send(ref, q, 1, to_c).wait_send()

        t_send(ref, q, 2, to_c).wait_send()
        t_send(ref, q, 3, to_c).wait_send()
        away = (ty ^ 2) * 8 + k
        t_send(tok_half(away), away, 3, to_c).wait_send()

    loop(0, 8, t_drain)
    tok_own.wait()

    def mod_wait(k):
        p = lax.rem(me + k, 32)
        rcopy(
            modsend.at[0], modbuf.at[p], mod_s.at[p], mod_r.at[p], dev_flat(p)
        ).wait()

    loop(1, 32, mod_wait)
    for s in range(32):
        modv[:, s * part : (s + 1) * part] = modbuf[s, :, 0:part]
    shift1, scale1, gate1, shift2, scale2, gate2 = [
        functools.partial(lambda k: modv[0:1, k * width : (k + 1) * width], k) for k in range(6)
    ]
    wh_copy.wait()

    height, wide = grid_h[0], grid_w[0]
    local = lax.broadcasted_iota(jnp.int32, (TILE, PAD), 0)
    lane = lax.broadcasted_iota(jnp.int32, (TILE, PAD), 1)

    def tile_layout(t):
        row_tile, col_tile = t // 4, lax.rem(t, 4)
        top = row_tile * height // 4
        rows = (row_tile + 1) * height // 4 - top
        left = col_tile * wide // 4
        span = (col_tile + 1) * wide // 4 - left
        spans = jnp.full((TILE, PAD), span, jnp.int32)
        quot = jnp.floor((local.astype(F32) + 0.5) / spans.astype(F32)).astype(jnp.int32)
        valid = local < jnp.full((TILE, PAD), rows * span, jnp.int32)
        row = jnp.where(valid, top + quot, 0)
        col = jnp.where(valid, left + local - quot * spans, 0)
        return valid, row, col

    def rope(n, c, s1, s2):
        return n * c + pltpu.roll(n, PAD - 18, 1) * s1 + pltpu.roll(n, 18, 1) * s2

    def unrope(d, c, s1, s2):
        return d * c + pltpu.roll(d * s1, 18, 1) + pltpu.roll(d * s2, PAD - 18, 1)

    def split_sin(sine):
        first = (lane < 18) | ((lane >= 36) & (lane < 54))
        return jnp.where(first, -sine, 0.0), jnp.where(first, 0.0, sine)

    def head_rows(t):
        valid, row, col = tile_layout(t)
        hot = jnp.where((lane == row) | (lane - 64 == col), 1.0, 0.0)
        angles = lax.dot_general(
            hot, tab[...], (((1,), (0,)), ((), ())),
            precision=HIGH, preferred_element_type=F32,
        )
        c, sine = angles[:, 0:PAD], angles[:, PAD : 2 * PAD]
        cosv[t] = c
        sinv[t] = sine
        s1, s2 = split_sin(sine)
        at = pl.ds(pl.multiple_of(t * TILE, TILE), TILE)
        x = tok_all[at, :].astype(F32)
        r = lax.rsqrt(jnp.mean(x * x, axis=1, keepdims=True) + EPS)
        h1 = ((x * r) * (1.0 + scale1()) + shift1()).astype(BF16)
        tok_all[at, :] = h1
        qkv = dot(h1, whv[...])
        q_r, k_r, v_r = qkv[:, 0:PAD], qkv[:, PAD : 2 * PAD], qkv[:, 2 * PAD : 3 * PAD]
        qraw[t] = q_r
        kraw[t] = k_r

        def normed(v, gain):
            rr = lax.rsqrt(jnp.sum(v * v, axis=1, keepdims=True) * (1.0 / HEAD) + EPS)
            return v * rr * gain[0:1, :]

        q_f = rope(normed(q_r, q_gain), c, s1, s2) * HEAD ** (-0.5)
        k_f = rope(normed(k_r, k_gain), c, s1, s2)
        qa[t] = jnp.where(lane == HEAD, 1.0, q_f).astype(BF16)
        k_f = jnp.where(lane == HEAD, jnp.where(valid, 0.0, -30000.0), k_f)
        k_f = jnp.where((lane > HEAD) & (lane < HEAD + 4), 1.0, k_f)
        ka[t] = k_f.astype(BF16)
        kt[:, pl.ds(pl.multiple_of(t * TILE, TILE), TILE)] = k_f.T.astype(BF16)
        va[t] = jnp.where((lane >= HEAD) & (lane < HEAD + 3), 1.0, v_r).astype(BF16)

    x_arrived(3, 4)
    hop_arrived(1, 2)
    loop(0, 8, head_rows)
    x_arrived(5, 6)
    hop_arrived(3, 4)
    loop(8, 16, head_rows)
    x_arrived(7)
    far_arrived(1, 2)
    hop_arrived(5, 6)

    def head_lanes(h):
        return attn_in.at[:, pl.ds(pl.multiple_of(h * PAD, PAD), PAD)]

    def at_copy(t):
        return rcopy(attn_send.at[t], head_lanes(b), at_s.at[t], at_r.at[b], dev_tile(t))

    def attend(k):
        q2 = qa[pl.ds(2 * k, 2)].reshape(2 * TILE, PAD)
        p = jnp.exp(dot(q2, kt[...])).astype(BF16)
        o = dot(p, va[...].reshape(16 * TILE, PAD))
        total = o[:, HEAD : HEAD + 1]
        o = o / total
        lse = jnp.log(total)
        q3 = put_split3(q2.astype(F32), -lse, HEAD + 1)
        o16 = o.astype(BF16)
        for u in range(2):
            t = 2 * k + u
            rows = slice(u * TILE, (u + 1) * TILE)
            onorm[t] = o[rows]
            qa[t] = q3[rows].astype(BF16)
            qt[:, pl.ds(pl.multiple_of(t * TILE, TILE), TILE)] = q3[rows].T.astype(BF16)
            attn_send[t] = o16[rows]

            @pl.when(t != b)
            def _():
                at_copy(t).start()

    loop(0, 8, attend)
    head_lanes(b)[...] = attn_send[b]
    x_arrived(8, 9, 10)
    far_arrived(3, 4)
    hop_arrived(7)

    def at_wait(k):
        p = lax.rem(b + k, 16)
        rcopy(attn_send.at[p], head_lanes(p), at_s.at[p], at_r.at[p], dev_tile(p)).wait()

    loop(1, 16, at_wait)

    def put_halves(ref, value):
        pad = jnp.zeros((TILE, 5 * PAD - half), F32)
        for k in range(2):
            piece = jnp.concatenate([value[:, k * half : (k + 1) * half], pad], axis=1)
            ref[:, k * 5 * PAD : (k + 1) * 5 * PAD] = piece.astype(BF16)

    def put_blocks(ref, value):
        pad = jnp.zeros((TILE, PAD - HEAD), F32)
        for k in range(16):
            zz = k % 4
            to = 4 * (k // 4) + 2 * (zz % 2) + zz // 2
            piece = jnp.concatenate([value[:, k * HEAD : (k + 1) * HEAD], pad], axis=1)
            ref[:, to * PAD : (to + 1) * PAD] = piece.astype(BF16)

    l_src, l_all = (l_mid, l_h2s, l_attns), (lb_down, lb_up, lb_out)
    r_src, r_all = (attn_in, r_gu, r_branchs), (rb_down, rb_up, rb_out)

    def slot_rows(i, t):
        return pl.ds(pl.multiple_of((i * 4 + t) * TILE, TILE), TILE)

    def lanes_at(k, n):
        return pl.ds(pl.multiple_of(k * n, PAD), n)

    def g_left(m, k, src, i, t, d):
        dst = l_all[m].at[slot_rows(i, t)]
        return rcopy(dst if src is None else src, dst, gl_s.at[m, k], gl_r.at[m, i * 4 + t], d)

    def g_right(m, k, src, i, t, d):
        n = r_src[m].shape[1] // 4
        dst = r_all[m].at[slot_rows(i, t)]
        if k in (2, 4, 5, 6):
            dst = r_all[m].at[slot_rows(i, t), lanes_at(1 - c, n)]
        return rcopy(dst if src is None else src, dst, gr_s.at[m, k], gr_r.at[m, i * 4 + t], d)

    def l_part(m, k):
        return l_src[m].at[:, lanes_at(k, l_src[m].shape[1] // 2)]

    def r_part(m, k, n):
        return r_src[m].at[:, lanes_at(k, n * (r_src[m].shape[1] // 4))]

    def g_first(m):
        return [
            g_left(m, 0, l_part(m, other), img, ty, to_x),
            g_right(m, 0, r_part(m, 1 - y, 2), img, ty, to_y),
            g_left(m, 1, l_part(m, img), img, ty, to_y),
            g_right(m, 1, r_part(m, y, 2), img, ty, to_x),
            g_left(m, 2, l_part(m, img), img, ty, to_c),
            g_right(m, 2, r_part(m, ty ^ 1, 1), img, ty, to_c),
        ]

    def g_own(m):
        n = r_src[m].shape[1] // 4
        rows = slot_rows(img, ty)
        return [
            pltpu.make_async_copy(l_part(m, img), l_all[m].at[rows], g_loc.at[m, 0]),
            pltpu.make_async_copy(
                r_part(m, ty, 1), r_all[m].at[rows, lanes_at(c, n)], g_loc.at[m, 1]
            ),
        ]

    def gl_x(m):
        g_first(m)[0].start()

    def gl_yc(m):
        g_first(m)[2].start()
        g_first(m)[4].start()
        g_own(m)[0].start()

    def gr_x(m):
        g_first(m)[3].start()

    def gr_yc(m):
        if m != 1:
            g_first(m)[1].start()
        g_first(m)[5].start()
        g_own(m)[1].start()

    def gu_lanes(i, k, base=0):
        n = hidden // 4
        return pl.ds(pl.multiple_of(base + lax.rem(2 * i + k, 4) * n, PAD), n)

    def gu_copy(w, k):
        dst = rb_up.at[slot_rows(img, ty ^ 2 if w == 2 else ty), gu_lanes(img, k)]
        src = dst
        if w < 2:
            src = r_gu.at[:, gu_lanes(img, k, (1 - y if w == 0 else y) * hidden)]
        return rcopy(src, dst, gu_s.at[w, k], gu_r.at[w, k], to_y if w == 0 else to_x)

    def gu_wait(w, k):
        i, t = (img, ty ^ 2) if w == 0 else (other, ty if w == 1 else ty ^ 2)
        ref = rb_up.at[slot_rows(i, t), gu_lanes(i, k)]
        rcopy(ref, ref, gu_s.at[w, k], gu_r.at[w, k], to_x).wait_recv()

    def gu_hop(k):
        gu_wait(0, k)
        gu_copy(2, k).start()

    def gl_hop(m):
        g_left(m, 0, None, other, ty, to_x).wait_recv()
        g_left(m, 3, None, other, ty, to_y).start()
        g_left(m, 4, None, other, ty, to_c).start()

    def gl_across(m):
        g_left(m, 1, None, img, ty ^ 2, to_y).wait_recv()
        g_left(m, 5, None, img, ty ^ 2, to_c).start()

    def gr_hop(m):
        if m != 1:
            g_right(m, 0, None, img, ty ^ 2, to_y).wait_recv()
            g_right(m, 3, None, img, ty ^ 2, to_x).start()
        g_right(m, 4, None, img, ty ^ 2, to_c).start()
        if m != 1:
            g_right(m, 1, None, other, ty, to_x).wait_recv()
        else:
            for k in range(4):
                gu_wait(1, k)
        g_right(m, 5, None, other, ty, to_c).start()

    def gl_hop2(m):
        g_left(m, 3, None, other, ty ^ 2, to_y).wait_recv()
        g_left(m, 6, None, other, ty ^ 2, to_c).start()

    def gr_hop2(m):
        if m != 1:
            g_right(m, 3, None, other, ty ^ 2, to_x).wait_recv()
        else:
            for k in range(4):
                gu_wait(2, k)
        g_right(m, 6, None, other, ty ^ 2, to_c).start()

    def g_done(m):
        n = r_src[m].shape[1] // 4
        for i in range(2):
            for t in (ty ^ 1, ty ^ 3):
                g_left(m, 2, None, i, t, to_c).wait_recv()
                ref = r_all[m].at[slot_rows(i, t), lanes_at(c, n)]
                rcopy(ref, ref, gr_s.at[m, 2], gr_r.at[m, i * 4 + t], to_c).wait_recv()
        for copy in g_own(m):
            copy.wait()

    def g_drain(m):
        for k, copy in enumerate(g_first(m)):
            if m != 1 or k not in (1, 3):
                copy.wait_send()
        for k, i, t in ((3, other, ty), (4, other, ty), (5, img, ty ^ 2), (6, other, ty ^ 2)):
            g_left(m, k, None, i, t, to_c).wait_send()
        for k, i, t in ((3, img, ty ^ 2), (4, img, ty ^ 2), (5, other, ty), (6, other, ty ^ 2)):
            if m != 1 or k != 3:
                g_right(m, k, None, i, t, to_c).wait_send()
        if m == 1:
            for w in range(3):
                for k in range(4):
                    gu_copy(w, k).wait_send()

    attn = jnp.concatenate(
        [attn_in[:, h * PAD : h * PAD + HEAD].astype(F32) for h in range(16)], axis=1
    )
    l_attn[...] = attn.astype(BF16)
    put_halves(l_attns, attn)
    own(OUT).wait()
    w_done(0)
    own_valid = tile_layout(b)[0]
    keep = jnp.where(own_valid, 1.0, 0.0)[:, 0:1]
    cols = width // 3

    def project(k):
        at = pl.ds(pl.multiple_of(k * cols, PAD), cols)
        branchv[:, at] = dot(l_attn[...], woutv[:, at])

    loop(0, 3, project)
    far_arrived(5, 6)
    x = tok[...].astype(F32)
    x1 = x + keep * gate1() * branchv[...]
    x1v[...] = x1
    r = lax.rsqrt(jnp.mean(x1 * x1, axis=1, keepdims=True) + EPS)
    h2_rows = (x1 * r) * (1.0 + scale2()) + shift2()
    l_h2[...] = h2_rows.astype(BF16)
    put_halves(l_h2s, h2_rows)
    d_ffn = cot[...].astype(F32) * keep * gate2()
    r_ffn[...] = d_ffn.astype(BF16)
    put_blocks(attn_in, d_ffn)
    ffnv[...] = jnp.zeros_like(ffnv)
    dh2v[...] = jnp.zeros_like(dh2v)
    own(UP).wait()
    own(DOWN).wait()
    step = 256

    def mlp(j):
        g_at = pl.ds(pl.multiple_of(j, step), step)
        u_at = pl.ds(pl.multiple_of(hidden + j, step), step)
        h2 = l_h2[...]
        gate = dot(h2, wupv[:, g_at])
        up = dot(h2, wupv[:, u_at])
        sig = 1.0 / (1.0 + jnp.exp(-gate))
        act_g = gate * sig
        mid = (act_g * up).astype(BF16)
        l_mid[:, g_at] = mid
        w3 = wdownv[g_at, :]
        ffnv[...] += dot(mid, w3)
        d_mid = dot_nt(r_ffn[...], w3)
        d_gate = (d_mid * up * (sig + gate * sig * (1.0 - sig))).astype(BF16)
        d_up = (d_mid * act_g).astype(BF16)
        r_gu[:, g_at] = d_gate
        r_gu[:, u_at] = d_up
        dh2v[...] += dot_nt(d_gate, wupv[:, g_at]) + dot_nt(d_up, wupv[:, u_at])

    def mlp_quarter(k):
        first = lax.rem(2 * img + k, 4) * (hidden // 4)
        loop(0, hidden // 4 // step, lambda j: mlp(first + j * step))

    gl_x(1)
    w_done(1, 2)
    mlp_quarter(0)
    gu_copy(1, 0).start()
    far_arrived(7)
    hop_arrived(8, 9)
    w_done(3, 4)
    mlp_quarter(1)
    gu_copy(1, 1).start()
    hop_arrived(10)
    far_arrived(8, 9)
    w_done(5, 6, 7)
    mlp_quarter(2)
    gu_copy(1, 2).start()
    gu_copy(0, 0).start()
    far_arrived(10)
    w_done(8, 9, 10)
    mlp_quarter(3)
    gu_copy(1, 3).start()
    gu_copy(0, 1).start()
    ffn = ffnv[...]
    g = cot[...].astype(F32)
    x1 = x1v[...]
    mixed[...] = (x1 + keep * gate2() * ffn).astype(BF16)

    def dmod_put(k, row):
        dmod[0:1, k * width : (k + 1) * width] = row

    def colsum(v):
        return jnp.sum(v, axis=0, keepdims=True)

    dmod_put(5, colsum(g * keep * ffn))
    d_h2 = dh2v[...]
    norm2 = x1 * r
    dmod_put(4, colsum(d_h2 * norm2))
    dmod_put(3, colsum(d_h2))
    d_n2 = d_h2 * (1.0 + scale2())
    d_x1 = g + r * (d_n2 - norm2 * jnp.mean(d_n2 * norm2, axis=1, keepdims=True))
    dmod_put(2, colsum(d_x1 * keep * branchv[...]))
    x1v[...] = d_x1
    d_branch = d_x1 * keep * gate1()
    r_branch[...] = d_branch.astype(BF16)
    put_blocks(r_branchs, d_branch)

    def unproject(k):
        at = pl.ds(pl.multiple_of(k * cols, PAD), cols)
        branchv[:, at] = dot_nt(r_branch[...], woutv[at, :])

    loop(0, 3, unproject)

    zeros = jnp.zeros((TILE, PAD - HEAD), F32)
    d_attn = branchv[...]
    for h in range(16):
        attn_send[h] = jnp.concatenate(
            [d_attn[:, h * HEAD : (h + 1) * HEAD], zeros], axis=1
        ).astype(BF16)

    def do_copy(t):
        return rcopy(attn_send.at[t], do_in.at[b], do_s.at[t], do_r.at[b], dev_tile(t))

    loop(1, 16, lambda k: do_copy(lax.rem(b + k, 16)).start())
    do_in[b] = attn_send[b]
    gu_copy(0, 2).start()
    gu_copy(0, 3).start()
    x_arrived(11)
    gl_yc(1)
    gl_hop(1)
    gr_yc(1)
    gu_hop(0)
    gu_hop(1)
    gl_x(2)
    gl_yc(2)
    gr_yc(0)
    gr_yc(2)
    gl_yc(0)

    def do_wait(k):
        p = lax.rem(b + k, 16)
        rcopy(attn_send.at[p], do_in.at[p], do_s.at[p], do_r.at[p], dev_tile(p)).wait()

    loop(1, 16, do_wait)
    gu_hop(2)
    x_arrived(12)

    def delta(t):
        d = do_in[t].astype(F32)
        dsum = jnp.sum(jnp.where(lane < HEAD, d * onorm[t], 0.0), axis=1, keepdims=True)
        d = put_split3(d, -dsum, HEAD)
        do_in[t] = d.astype(BF16)
        dot_t[:, pl.ds(pl.multiple_of(t * TILE, TILE), TILE)] = d.T.astype(BF16)

    loop(0, 16, delta)
    gu_hop(3)
    gr_x(0)
    gl_x(0)
    gr_x(2)
    gl_hop(2)
    dqt[...] = jnp.zeros_like(dqt)

    high, low = z // 2, lax.rem(z, 2)
    l0 = 3 * width

    def z_load(m):
        kl, n = l_all[m].shape[1], r_src[m].shape[1] // 4
        copies = [
            pltpu.make_async_copy(
                l_all[m], wupv.at[pl.ds(0, 8 * TILE), pl.ds(l0, kl)], z_loc.at[0]
            ),
            pltpu.make_async_copy(
                r_all[m].at[:, lanes_at(c, n)],
                wupv.at[pl.ds(0, 8 * TILE), pl.ds(l0 + kl, n)],
                z_loc.at[1],
            ),
        ]
        for copy in copies:
            copy.start()
        for copy in copies:
            copy.wait()

    def z_copies(m):
        if m == 0:
            sent = [kt.at[pl.ds(0, 80), pl.ds(0, 12 * PAD)], qt.at[pl.ds(0, 80), pl.ds(0, 12 * PAD)]]
        elif m == 1:
            sent = [wupv.at[pl.ds(k * half, half), pl.ds(44 * PAD, 3 * PAD)] for k in range(2)]
        else:
            sent = [tok_all.at[pl.ds(640 + 128 * k, 80), pl.ds(0, 5 * PAD)] for k in range(2)]
        return [
            rcopy(sent[k], za[m].at[k], za_s.at[m, k], za_r.at[m, k], dev(k=z ^ 1))
            for k in range(2)
        ]

    za, zb = (za_down, za_up, za_out), (zb_down, zb_up, zb_out)
    z_rest = (
        dot_t.at[pl.ds(0, 80), pl.ds(0, 12 * PAD)],
        wdownv.at[pl.ds(19 * TILE, half), pl.ds(0, 3 * PAD)],
        tok_all.at[pl.ds(896, 80), pl.ds(0, 5 * PAD)],
    )
    z_own = (dqt.at[pl.ds(0, 80), pl.ds(0, 12 * PAD)], up_grad, z_out)

    def z_copy2(m):
        return rcopy(z_rest[m], zb[m], zb_s.at[m], zb_r.at[m], dev(k=z ^ 2))

    def z_product(m):
        kl = l_all[m].shape[1]
        sent = [copy.src_ref for copy in z_copies(m)]
        if m == 1:

            def turn(k):
                at = pl.ds(pl.multiple_of(k * TILE, TILE), TILE)
                woutv[0 : 5 * PAD, at] = wupv[at, l0 : l0 + kl].astype(F32).T.astype(BF16)

            loop(0, 8, turn)

            def block(zz):
                at = pl.ds(pl.multiple_of(l0 + kl + zz * 3 * PAD, PAD), 3 * PAD)
                return dot(woutv[0:half, 0 : 8 * TILE], wupv[0 : 8 * TILE, at])

            for k in range(2):
                sent[k][...] = block(2 * k + 1 - low).astype(BF16)
            for copy in z_copies(m):
                copy.start()
            z_rest[m][...] = block(2 * (1 - high) + low).astype(BF16)
            z_own[m][...] = block(z)
            return

        def pair(k):
            at = pl.ds(pl.multiple_of(l0 + kl + k * 2 * PAD, PAD), 2 * PAD)
            return dot_tn(wupv[0 : 8 * TILE, at], wupv[0 : 8 * TILE, l0 : l0 + kl])

        both = pair(1 - low)
        for k in range(2):
            sent[k][...] = both[k * PAD : k * PAD + 80].astype(BF16)
        for copy in z_copies(m):
            copy.start()
        both = pair(low)
        first, second = both[0:80], both[PAD : PAD + 80]
        z_rest[m][...] = jnp.where(high == 0, second, first).astype(BF16)
        z_own[m][...] = jnp.where(high == 0, first, second)

    def z_second(m):
        for copy in z_copies(m):
            copy.wait()
        rest = z_rest[m][...].astype(F32) + za[m][1 - high].astype(F32)
        z_rest[m][...] = rest.astype(BF16)
        z_copy2(m).start()
        z_own[m][...] += za[m][high].astype(F32)

    def z_last(m):
        z_copy2(m).wait()
        z_own[m][...] += zb[m][...].astype(F32)

    gain_grad[...] = jnp.zeros_like(gain_grad)
    for i in range(11):
        w_drain(i)

    def kv_send(k, u):
        at = pl.ds(pl.multiple_of(k * 2 * HEAD, 16), 2 * HEAD)
        return wdownv.at[at, pl.ds((3 + u) * PAD, PAD)]

    def q_send(k, u):
        at = pl.ds(pl.multiple_of(width + k * 80, 16), 80)
        return wdownv.at[at, pl.ds((3 + u) * PAD, PAD)]

    def kv_copy(k, u):
        t = 2 * k + u
        return rcopy(kv_send(k, u), dkv_in.at[b], dkv_s.at[t], dkv_r.at[b], dev_tile(t))

    def q_copy(k, u):
        t = 2 * k + u
        return rcopy(q_send(k, u), dq_in.at[b], dq_s.at[t], dq_r.at[b], dev_tile(t))

    def head_back(d, v, gain, row, t):
        c_, (s1, s2) = cosv[t], split_sin(sinv[t])
        d = unrope(d, c_, s1, s2)
        rr = lax.rsqrt(jnp.sum(v * v, axis=1, keepdims=True) * (1.0 / HEAD) + EPS)
        n = v * rr
        gain_grad[row : row + 1, :] += colsum(d * n)
        dn = d * gain[0:1, :]
        return rr * (dn - n * (jnp.sum(dn * n, axis=1, keepdims=True) * (1.0 / HEAD)))

    def send_tile(k, u, copy, keep_own):
        copy_ = copy(k, u)

        @pl.when(2 * k + u != b)
        def _():
            copy_.start()

        @pl.when(2 * k + u == b)
        def _():
            keep_own[b] = copy_.src_ref[...]

    def attend_back(k):
        two = pl.ds(2 * k, 2)
        p = jnp.exp(dot(ka[two].reshape(2 * TILE, PAD), qt[...]))
        ds = (p * dot(va[two].reshape(2 * TILE, PAD), dot_t[...])).astype(BF16)
        d_k2 = dot(ds, qa[...].reshape(16 * TILE, PAD))
        d_v2 = dot(p.astype(BF16), do_in[...].reshape(16 * TILE, PAD))
        at = pl.ds(pl.multiple_of(k * 2 * TILE, 2 * TILE), 2 * TILE)
        dqt[...] += dot(kt[:, at], ds)
        for u in range(2):
            t = 2 * k + u
            rows = slice(u * TILE, (u + 1) * TILE)
            d_k = head_back(d_k2[rows], kraw[t], k_gain, 1, t)
            d_v = jnp.where(lane < HEAD, d_v2[rows], 0.0)
            at = pl.ds(pl.multiple_of(t * TILE, TILE), TILE)
            wdownv[at, PAD : 3 * PAD] = jnp.concatenate([d_k, d_v], axis=1).astype(BF16)
            turned = jnp.concatenate([d_k.T[0:HEAD], d_v.T[0:HEAD]], axis=0)
            kv_send(k, u)[...] = turned.astype(BF16)
            send_tile(k, u, kv_copy, dkv_in)

    loop(0, 4, attend_back)
    gl_across(1)
    gr_hop(1)
    hop_arrived(11)
    loop(4, 6, attend_back)
    gl_hop2(1)
    gr_hop2(1)
    g_done(1)
    z_load(1)
    z_product(1)
    loop(6, 8, attend_back)
    gl_hop(0)
    gr_hop(0)

    def heads_back(k):
        for u in range(2):
            t = 2 * k + u
            at = pl.ds(pl.multiple_of(t * TILE, TILE), TILE)
            d_q = dqt[:, at].T * HEAD ** (-0.5)
            d_q = head_back(d_q, qraw[t], q_gain, 0, t)
            wdownv[at, 0:PAD] = d_q.astype(BF16)
            q_send(k, u)[...] = d_q.T[0:80].astype(BF16)
            send_tile(k, u, q_copy, dq_in)

    loop(0, 8, heads_back)
    gr_hop(2)
    w_done(11, 12)
    w_drain(11)
    w_drain(12)


    sums_t = (branchv, ffnv, dh2v)
    for ref in sums_t:
        ref[...] = jnp.zeros((PAD, width), F32)

    def dw_rows(k):
        at = pl.ds(pl.multiple_of(k * 2 * TILE, TILE), 2 * TILE)
        term = dot_tn(wdownv[at, 0 : 3 * PAD], tok_all[at, :])
        for p in range(3):
            sums_t[p][...] += term[p * PAD : (p + 1) * PAD]

    loop(0, 8, dw_rows)
    half_pad = jnp.zeros((80, 5 * PAD - half), F32)
    for p in range(3):
        for i in range(2):
            piece = sums_t[p][0:80, i * half : (i + 1) * half]
            at = slice((3 * i + p) * 80, (3 * i + p + 1) * 80)
            tok_all[at, 0 : 5 * PAD] = jnp.concatenate([piece, half_pad], axis=1).astype(BF16)

    def dw_half(i):
        return tok_all.at[pl.ds(pl.multiple_of(i * 240, 16), 240), pl.ds(0, 5 * PAD)]

    dw_copy = rcopy(dw_half(other), dw_in, dw_sem.at[0], dw_sem.at[1], dev(i=other))
    dw_copy.start()

    loads = [
        pltpu.make_async_copy(
            src, wupv.at[pl.ds(owner * half, half), pl.ds(0, 3 * width)], loc.at[k]
        )
        for k, (src, owner) in enumerate(
            ((wqkv, img), (qkv_hbm.at[pl.ds(other * half, half)], other))
        )
    ]
    for load in loads:
        load.start()

    def dq_wait(k):
        p = lax.rem(b + k, 16)
        kv, q_ = dkv_in.at[p], dq_in.at[p]
        rcopy(kv, kv, dkv_s.at[p], dkv_r.at[p], dev_tile(p)).wait()
        rcopy(q_, q_, dq_s.at[p], dq_r.at[p], dev_tile(p)).wait()

    z_second(1)
    loop(1, 16, dq_wait)
    for m in (0, 2):
        gl_across(m)
        gl_hop2(m)
        gr_hop2(m)
    g_done(0)
    z_load(0)
    z_product(0)
    for load in loads:
        load.wait()

    def own_part(p):
        return slice(16 * TILE + p * TILE, 16 * TILE + (p + 1) * TILE)

    for p in range(3):
        got, r0 = (dq_in, 0) if p == 0 else (dkv_in, (p - 1) * HEAD)
        turned = jnp.concatenate(
            [got[h].astype(F32)[r0 : r0 + HEAD] for h in range(16)], axis=0
        )
        wdownv[own_part(p), :] = turned.T.astype(BF16)

    def h1_back(k):
        at = pl.ds(pl.multiple_of(k * cols, PAD), cols)
        dh2v[:, at] = sum(
            dot_nt(wdownv[own_part(p), :], wupv[at, p * width : (p + 1) * width])
            for p in range(3)
        )

    loop(0, 3, h1_back)
    d_h1 = dh2v[...]
    x = tok[...].astype(F32)
    r1 = lax.rsqrt(jnp.mean(x * x, axis=1, keepdims=True) + EPS)
    norm1 = x * r1
    dmod_put(1, colsum(d_h1 * norm1))
    dmod_put(0, colsum(d_h1))
    d_n1 = d_h1 * (1.0 + scale1())
    back = r1 * (d_n1 - norm1 * jnp.mean(d_n1 * norm1, axis=1, keepdims=True))
    tgrad[...] = (x1v[...] + back).astype(BF16)

    dsend[...] = jnp.zeros_like(dsend)
    for s in range(32):
        dsend[s, 0:1, 0:part] = dmod[0:1, s * part : (s + 1) * part]
        dsend[s, 1:3, 0:PAD] = gain_grad[0:2, :]

    def dm_copy(p):
        return rcopy(dsend.at[p], dbuf.at[me], dm_s.at[p], dm_r.at[me], dev_flat(p))

    loop(1, 32, lambda k: dm_copy(lax.rem(me + k, 32)).start())
    dbuf[me] = dsend[me]

    g_done(2)
    z_load(2)
    z_product(2)
    dw_copy.wait()
    dw_sum = dw_half(img)[...].astype(F32) + dw_in[...].astype(F32)

    def pc_send(p):
        return tok_all.at[pl.ds(1024 + 80 * p, 80), pl.ds(0, 5 * PAD)]

    for p in range(3):
        pc_send(p)[...] = dw_sum[80 * p : 80 * (p + 1)].astype(BF16)

    def pc_copy(p):
        group = 16 * p + b
        to, slot = group // 3, lax.rem(group, 3)
        return to, rcopy(
            pc_send(p), pc_in.at[slot], pc_s.at[p], pc_r.at[slot], dev_tile(to)
        )

    for p in range(3):
        to, copy = pc_copy(p)

        @pl.when(to != b)
        def _():
            copy.start()

        @pl.when(to == b)
        def _():
            pc_in[lax.rem(16 * p + b, 3)] = pc_send(p)[...]

    z_second(0)
    z_second(2)
    z_last(1)
    z_last(0)
    z_last(2)
    g_drain(0)
    g_drain(1)
    g_drain(2)
    down_grad[...] = z_own[0][0:HEAD, :]
    out_grad[...] = z_own[2][0:HEAD, 0:half]
    for slot in range(3):
        group = 3 * b + slot
        src = lax.rem(group, 16)

        @pl.when(src != b)
        def _():
            rcopy(
                pc_send(0), pc_in.at[slot], pc_s.at[0], pc_r.at[slot], dev_tile(src)
            ).wait_recv()

    for slot in range(3):
        at = slice(slot * HEAD, (slot + 1) * HEAD)
        qkv_grad[at, :] = pc_in[slot].astype(F32)[0:HEAD, 0:half]
    for p in range(3):
        to, copy = pc_copy(p)

        @pl.when(to != b)
        def _():
            copy.wait_send()

    def dm_wait(k):
        p = lax.rem(me + k, 32)
        rcopy(dsend.at[p], dbuf.at[p], dm_s.at[p], dm_r.at[p], dev_flat(p)).wait()

    loop(1, 32, dm_wait)
    sums = [
        lax.fori_loop(1, 16, lambda s, a, i=i: a + dbuf[16 * i + s], dbuf[16 * i])
        for i in range(2)
    ]
    gain_grad[...] = jnp.where(
        lax.broadcasted_iota(jnp.int32, (8, PAD), 0) < 2,
        pltpu.roll(sums[0] + sums[1], 7, 0)[:, 0:PAD],
        0.0,
    )
    row = lax.broadcasted_iota(jnp.int32, (8, 2 * PAD), 0)
    d_two = jnp.where(row == 0, sums[0][0:1, :], jnp.where(row == 1, sums[1][0:1, :], 0.0))
    row = lax.broadcasted_iota(jnp.int32, (8, width), 0)
    a_two = jnp.where(row == 0, actbuf[0], jnp.where(row == 1, actbuf[1], 0.0))
    ada_grad[...] = dot_tn(d_two, a_two, HIGH)[0:part, :]
    act_copy.wait_send()


def rope_table():
    table = np.zeros((PAD, 2 * PAD), np.float64)
    angle = np.arange(64)[:, None] * 10000.0 ** (-np.arange(18) / 18)
    for axis in range(2):
        rows = slice(64 * axis, 64 * axis + 64)
        for quarter in range(2):
            at = 36 * axis + 18 * quarter
            table[rows, at : at + 18] = np.cos(angle)
            table[rows, PAD + at : PAD + at + 18] = np.sin(angle)
    return table.astype(np.float32)


def run_block(tokens, cotangent, act, ada, wout, wup, wdown, wqkv, q_gain, k_gain, grid_h, grid_w):
    width, hidden = tokens.shape[1], wup.shape[1] // 2
    half, part = width // 2, ada.shape[0]
    vmem, any_ = pl.BlockSpec(memory_space=pltpu.VMEM), pl.BlockSpec(memory_space=pl.ANY)
    smem = pl.BlockSpec(memory_space=pltpu.SMEM)
    sds = jax.ShapeDtypeStruct
    v, dma = pltpu.VMEM, pltpu.SemaphoreType.DMA
    n_chunks = len(weight_chunks(width, hidden))
    tile16 = (16, TILE, PAD)
    out_shape = (
        sds((TILE, width), BF16),
        sds((TILE, width), BF16),
        sds((3 * HEAD, half), F32),
        sds((part, width), F32),
        sds((8, PAD), F32),
        sds((HEAD, hidden // 2), F32),
        sds((half, 3 * PAD), F32),
        sds((HEAD, half), F32),
        sds((width, 3 * width), BF16),
        sds((8 * TILE, hidden // 2), BF16),
        sds((8 * TILE, 5 * PAD), BF16),
        sds((8 * TILE, 5 * PAD), BF16),
        sds((8 * TILE, 8 * PAD), BF16),
        sds((8 * TILE, hidden), BF16),
        sds((8 * TILE, 8 * PAD), BF16),
    )
    scratch = [
        v((8, width), F32),
        v((1, PAD), F32),
        v((1, PAD), F32),
        v((3, half, 2 * PAD), BF16),
        dma((3,)),
        v((16 * TILE, width), BF16),
        v((width, 3 * PAD), BF16),
        v((width, width), BF16),
        v((width, 2 * hidden), BF16),
        v((hidden, width), BF16),
        v((2, 8, width), F32),
        v((2, 8, 2 * PAD), F32),
        v((32, 8, 2 * PAD), F32),
        v((8, 6 * width), F32),
        v(tile16, F32),
        v(tile16, F32),
        v(tile16, F32),
        v(tile16, F32),
        v(tile16, BF16),
        v(tile16, BF16),
        v(tile16, BF16),
        v((PAD, 16 * TILE), BF16),
        v((PAD, 16 * TILE), BF16),
        v(tile16, F32),
        v(tile16, BF16),
        v((TILE, 16 * PAD), BF16),
        v(tile16, BF16),
        v((PAD, 16 * TILE), BF16),
        v((PAD, 16 * TILE), F32),
        v((16, 2 * HEAD, PAD), BF16),
        v((16, 80, PAD), BF16),
        v((240, 5 * PAD), BF16),
        v((3, 80, 5 * PAD), BF16),
        v((TILE, width), F32),
        v((TILE, width), F32),
        v((TILE, width), F32),
        v((TILE, width), F32),
        v((8, 6 * width), F32),
        v((32, 8, 2 * PAD), F32),
        v((32, 8, 2 * PAD), F32),
        v((TILE, width), BF16),
        v((TILE, width), BF16),
        v((TILE, hidden), BF16),
        v((TILE, width), BF16),
        v((TILE, width), BF16),
        v((TILE, 2 * hidden), BF16),
        v((TILE, 10 * PAD), BF16),
        v((TILE, 10 * PAD), BF16),
        v((TILE, 16 * PAD), BF16),
        v((2, 80, hidden // 2), BF16),
        v((2, half, 3 * PAD), BF16),
        v((2, 80, 5 * PAD), BF16),
        v((80, hidden // 2), BF16),
        v((half, 3 * PAD), BF16),
        v((80, 5 * PAD), BF16),
        v((80, 5 * PAD), F32),
        dma((3, 8)),
        dma((3, 8)),
        dma((3, 8)),
        dma((3, 8)),
        dma((3, 4)),
        dma((3, 4)),
        dma((3, 2)),
        dma((3, 2)),
        dma((3, 2)),
        dma((3,)),
        dma((3,)),
        dma((2,)),
        dma((32, 4)),
        dma((32,)),
        dma,
        dma((n_chunks, 10)),
        dma((n_chunks, 10)),
        dma((4,)),
        dma((2,)),
        dma((2,)),
        dma((32,)),
        dma((32,)),
        dma((16,)),
        dma((16,)),
        dma((16,)),
        dma((16,)),
        dma((16,)),
        dma((16,)),
        dma((16,)),
        dma((16,)),
        dma((2,)),
        dma((3,)),
        dma((3,)),
        dma((32,)),
        dma((32,)),
        dma((2,)),
    ]
    return pl.pallas_call(
        block_kernel,
        out_shape=out_shape,
        in_specs=[vmem] * 4 + [any_] * 4 + [vmem] * 3 + [smem] * 2,
        out_specs=[vmem] * 8 + [any_] * 7,
        scratch_shapes=scratch,
        compiler_params=pltpu.CompilerParams(
            collective_id=0, has_side_effects=True, vmem_limit_bytes=VMEM_LIMIT
        ),
    )(
        tokens, cotangent, act, ada, wout, wup, wdown, wqkv, q_gain, k_gain, rope_table(),
        grid_h, grid_w,
    )


def fast_body(
    tokens,
    cotangent,
    class_embed,
    timestep,
    grid_height,
    grid_width,
    qkv_weight,
    out_weight,
    up_weight,
    down_weight,
    ada_weight,
    q_gain,
    k_gain,
):
    width = tokens.shape[2]
    act = jax.nn.silu(class_embed + time_embed(timestep, width)).astype(BF16).astype(F32)
    (mixed, tgrad, qkv_grad, ada_grad, gains, down_grad, up_grad, out_grad) = (
        run_block(
            tokens[0],
            cotangent[0],
            act,
            ada_weight,
            out_weight,
            up_weight,
            down_weight,
            qkv_weight,
            q_gain[None],
            k_gain[None],
            grid_height,
            grid_width,
        )[:8]
    )
    return (
        mixed[None],
        tgrad[None],
        qkv_grad.T,
        out_grad.T,
        up_grad,
        down_grad.T,
        ada_grad,
        gains[0, :HEAD],
        gains[1, :HEAD],
    )


def solution(mesh):
    in_specs = (
        P("img", ("ty", "tx"), None),
        P("img", ("ty", "tx"), None),
        P("img", None),
        P("img"),
        P("img"),
        P("img"),
        P("img", None),
        P("img", None),
        P("img", None),
        P("img", None),
        P(("img", "ty", "tx"), None),
        P(),
        P(),
    )
    out_specs = (
        P("img", ("ty", "tx"), None),
        P("img", ("ty", "tx"), None),
        P("img", ("ty", "tx")),
        P("img", ("ty", "tx")),
        P("img", ("ty", "tx")),
        P("img", ("ty", "tx")),
        P(("img", "ty", "tx"), None),
        P(),
        P(),
    )
    shape = dict(mesh.shape)
    fast = (shape["img"], shape["ty"], shape["tx"]) == (2, 4, 4)
    body = fast_body if fast else general_body
    return jax.shard_map(body, mesh=mesh, in_specs=in_specs, out_specs=out_specs, check_vma=False)
```

```python
import functools

import jax
import jax.numpy as jnp
import numpy as np
from jax import lax
from jax.experimental import pallas as pl
from jax.experimental.pallas import tpu as pltpu
from jax.sharding import PartitionSpec as P

HEADS = 16
HEAD = 72


EPS = 1e-06
HIGH = lax.Precision.HIGHEST


def layout(slot, height, width, cap, rows_tiles, cols_tiles):
    tile = slot // cap
    row_tile = tile // cols_tiles
    col_tile = tile % cols_tiles
    local = slot % cap
    top = row_tile * height // rows_tiles
    bottom = (row_tile + 1) * height // rows_tiles
    left = col_tile * width // cols_tiles
    right = (col_tile + 1) * width // cols_tiles
    span = right - left
    valid = local < (bottom - top) * span
    row = jnp.where(valid, top + local // span, 0)
    col = jnp.where(valid, left + local % span, 0)
    return (valid, row, col)


def time_embed(step, dim):
    half = dim // 2
    freq = jnp.exp(-jnp.log(10000.0) * jnp.arange(half, dtype=jnp.float32) / half)
    angle = step.astype(jnp.float32)[:, None] * freq
    return jnp.concatenate([jnp.cos(angle), jnp.sin(angle)], axis=-1)


def rotate(part, position):
    quarter = part.shape[-1] // 2
    freq = jnp.exp(-jnp.log(10000.0) * jnp.arange(quarter, dtype=jnp.float32) / quarter)
    angle = position.astype(jnp.float32)[..., None, None] * freq
    first, second = (part[..., :quarter], part[..., quarter:])
    cosine, sine = (jnp.cos(angle), jnp.sin(angle))
    return jnp.concatenate(
        [first * cosine - second * sine, second * cosine + first * sine], axis=-1
    )


def rope(heads, row, col):
    half = heads.shape[-1] // 2
    return jnp.concatenate(
        [rotate(heads[..., :half], row), rotate(heads[..., half:], col)], axis=-1
    )


def head_norm(value, gain):
    return value * lax.rsqrt(jnp.mean(value * value, axis=-1, keepdims=True) + EPS) * gain


def rms(value):
    return value * lax.rsqrt(jnp.mean(value * value, axis=-1, keepdims=True) + EPS)


def flat_rows(value):
    return value.reshape(-1, value.shape[-1])


def outer_sum(left, right):
    return lax.dot_general(
        flat_rows(left),
        flat_rows(right),
        (((0,), (0,)), ((), ())),
        preferred_element_type=jnp.float32,
    )


def times_transposed(left, weight):
    return lax.dot_general(
        left, weight, (((left.ndim - 1,), (1,)), ((), ())), preferred_element_type=jnp.float32
    )


def masked_scores(query, keys_all, key_valid):
    scores = jnp.einsum("qhd,khd->hqk", query, keys_all, preferred_element_type=jnp.float32)
    return jnp.where(key_valid[None, None, :], scores, -1e30)


def general_body(
    tokens,
    cotangent,
    class_embed,
    timestep,
    grid_height,
    grid_width,
    qkv_weight,
    out_weight,
    up_weight,
    down_weight,
    ada_weight,
    q_gain,
    k_gain,
):
    images, slots_dev, width = tokens.shape
    rows_tiles = lax.axis_size("ty")
    cols_tiles = lax.axis_size("tx")
    slots_all = slots_dev * rows_tiles * cols_tiles
    own_slot = lax.axis_index(("ty", "tx")) * slots_dev + jnp.arange(slots_dev, dtype=jnp.int32)
    all_slot = jnp.arange(slots_all, dtype=jnp.int32)
    valid_q, row_q, col_q = jax.vmap(
        lambda h, w: layout(own_slot, h, w, slots_dev, rows_tiles, cols_tiles)
    )(grid_height, grid_width)
    valid_k = jax.vmap(lambda h, w: layout(all_slot, h, w, slots_dev, rows_tiles, cols_tiles)[0])(
        grid_height, grid_width
    )
    keep = valid_q.astype(jnp.float32)[..., None]
    act = jax.nn.silu(class_embed + time_embed(timestep, width)).astype(jnp.bfloat16)
    mod = lax.dot_general(
        act,
        lax.all_gather(ada_weight, ("img", "ty", "tx"), axis=0, tiled=True),
        (((1,), (1,)), ((), ())),
        preferred_element_type=jnp.float32,
    )
    shift1, scale1, gate1, shift2, scale2, gate2 = [
        part[:, None, :] for part in jnp.split(mod, 6, axis=1)
    ]
    wqkv, wout, w12, w3 = (
        lax.all_gather(qkv_weight, "img", axis=0, tiled=True),
        lax.all_gather(out_weight, "img", axis=0, tiled=True),
        lax.all_gather(up_weight, "img", axis=0, tiled=True),
        lax.all_gather(down_weight, "img", axis=0, tiled=True),
    )
    xf = tokens.astype(jnp.float32)
    norm1, pull_norm1 = jax.vjp(rms, xf)
    h1 = (norm1 * (1.0 + scale1) + shift1).astype(jnp.bfloat16)
    qkv = jnp.dot(h1, wqkv, preferred_element_type=jnp.float32).reshape(
        images, slots_dev, 3, HEADS, HEAD
    )

    def finish(query_raw, key_raw, query_gain, key_gain):
        query = rope(head_norm(query_raw, query_gain), row_q, col_q) * HEAD ** (-0.5)
        return (query, rope(head_norm(key_raw, key_gain), row_q, col_q))

    (query_f, key_f), pull_heads = jax.vjp(finish, qkv[:, :, 0], qkv[:, :, 1], q_gain, k_gain)
    query_b = query_f.astype(jnp.bfloat16)
    key_b = key_f.astype(jnp.bfloat16)
    value_b = qkv[:, :, 2].astype(jnp.bfloat16)
    keys_all, values_all = (
        lax.all_gather(key_b, ("ty", "tx"), axis=1, tiled=True),
        lax.all_gather(value_b, ("ty", "tx"), axis=1, tiled=True),
    )
    index = 0
    scores = masked_scores(query_b[index], keys_all[index], valid_k[index])
    top = jnp.max(scores, axis=-1, keepdims=True)
    lse = top + jnp.log(jnp.sum(jnp.exp(scores - top), axis=-1, keepdims=True))
    prob = jnp.exp(scores - lse).astype(jnp.bfloat16)
    attn_list = [
        jnp.einsum("hqk,khd->qhd", prob, values_all[index], preferred_element_type=jnp.float32)
    ]
    lse_list = [lse]
    attn = jnp.stack(attn_list).reshape(images, slots_dev, width).astype(jnp.bfloat16)
    branch = jnp.dot(attn, wout, preferred_element_type=jnp.float32)
    x1 = xf + keep * gate1 * branch
    norm2, pull_norm2 = jax.vjp(rms, x1)
    h2 = (norm2 * (1.0 + scale2) + shift2).astype(jnp.bfloat16)
    gate_up = jnp.dot(h2, w12, preferred_element_type=jnp.float32)
    hidden = gate_up.shape[-1] // 2
    gate_part, up_part = (gate_up[..., :hidden], gate_up[..., hidden:])
    sig = jax.nn.sigmoid(gate_part)
    silu_gate = gate_part * sig
    mid = (silu_gate * up_part).astype(jnp.bfloat16)
    ffn = jnp.dot(mid, w3, preferred_element_type=jnp.float32)
    mixed = (x1 + keep * gate2 * ffn).astype(jnp.bfloat16)
    grad_out = cotangent.astype(jnp.float32)
    d_gate2 = jnp.sum(grad_out * keep * ffn, axis=1)
    d_ffn = (grad_out * keep * gate2).astype(jnp.bfloat16)
    term_down = outer_sum(mid, d_ffn)
    d_mid = times_transposed(d_ffn, w3)
    d_gate = d_mid * up_part * (sig + gate_part * sig * (1.0 - sig))
    d_up = d_mid * silu_gate
    d_gate_up = jnp.concatenate([d_gate, d_up], axis=-1).astype(jnp.bfloat16)
    term_up = outer_sum(h2, d_gate_up)
    d_h2 = times_transposed(d_gate_up, w12)
    d_scale2 = jnp.sum(d_h2 * norm2, axis=1)
    d_shift2 = jnp.sum(d_h2, axis=1)
    d_x1 = grad_out + pull_norm2(d_h2 * (1.0 + scale2))[0]
    d_gate1 = jnp.sum(d_x1 * keep * branch, axis=1)
    d_branch = (d_x1 * keep * gate1).astype(jnp.bfloat16)
    term_out = outer_sum(attn, d_branch)
    d_attn = (
        times_transposed(d_branch, wout)
        .astype(jnp.bfloat16)
        .reshape(images, slots_dev, HEADS, HEAD)
    )
    keys_back, values_back = (
        lax.all_gather(key_b, ("ty", "tx"), axis=1, tiled=True),
        lax.all_gather(value_b, ("ty", "tx"), axis=1, tiled=True),
    )
    index = 0
    scores = masked_scores(query_b[index], keys_back[index], valid_k[index])
    prob = jnp.exp(scores - lse_list[index])
    d_prob = jnp.einsum(
        "qhd,khd->hqk", d_attn[index], values_back[index], preferred_element_type=jnp.float32
    )
    delta = jnp.sum(prob * d_prob, axis=-1, keepdims=True)
    d_scores = (prob * (d_prob - delta)).astype(jnp.bfloat16)
    dq_list = [
        jnp.einsum("hqk,khd->qhd", d_scores, keys_back[index], preferred_element_type=jnp.float32)
    ]
    dk_list = [
        jnp.einsum("hqk,qhd->khd", d_scores, query_b[index], preferred_element_type=jnp.float32)
    ]
    dv_list = [
        jnp.einsum(
            "hqk,qhd->khd",
            prob.astype(jnp.bfloat16),
            d_attn[index],
            preferred_element_type=jnp.float32,
        )
    ]
    d_key, d_value = (
        lax.psum_scatter(
            jnp.stack(dk_list).astype(jnp.bfloat16), ("ty", "tx"), scatter_dimension=1, tiled=True
        ).astype(jnp.float32),
        lax.psum_scatter(
            jnp.stack(dv_list).astype(jnp.bfloat16), ("ty", "tx"), scatter_dimension=1, tiled=True
        ).astype(jnp.float32),
    )
    d_query_raw, d_key_raw, d_q_gain, d_k_gain = pull_heads((jnp.stack(dq_list), d_key))
    d_qkv = (
        jnp.stack([d_query_raw, d_key_raw, d_value], axis=2)
        .reshape(images, slots_dev, 3 * width)
        .astype(jnp.bfloat16)
    )
    term_qkv = outer_sum(h1, d_qkv)
    d_h1 = times_transposed(d_qkv, wqkv)
    d_scale1 = jnp.sum(d_h1 * norm1, axis=1)
    d_shift1 = jnp.sum(d_h1, axis=1)
    tokens_grad = (d_x1 + pull_norm1(d_h1 * (1.0 + scale1))[0]).astype(jnp.bfloat16)
    d_mod = jnp.concatenate([d_shift1, d_scale1, d_gate1, d_shift2, d_scale2, d_gate2], axis=1)
    act_f = act.astype(jnp.float32)
    ada_grad = lax.psum_scatter(
        lax.dot_general(
            d_mod,
            act_f,
            (((0,), (0,)), ((), ())),
            precision=HIGH,
            preferred_element_type=jnp.float32,
        ),
        ("img", "ty", "tx"),
        scatter_dimension=0,
        tiled=True,
    )
    q_gain_grad, k_gain_grad = lax.psum((d_q_gain, d_k_gain), ("img", "ty", "tx"))
    parts = (
        lax.psum_scatter(
            term_qkv.astype(jnp.bfloat16), ("ty", "tx"), scatter_dimension=1, tiled=True
        ).astype(jnp.float32),
        lax.psum_scatter(
            term_out.astype(jnp.bfloat16), ("ty", "tx"), scatter_dimension=1, tiled=True
        ).astype(jnp.float32),
        lax.psum_scatter(
            term_up.astype(jnp.bfloat16), ("ty", "tx"), scatter_dimension=1, tiled=True
        ).astype(jnp.float32),
        lax.psum_scatter(
            term_down.astype(jnp.bfloat16), ("ty", "tx"), scatter_dimension=1, tiled=True
        ).astype(jnp.float32),
    )
    grads = (
        lax.psum_scatter(
            parts[0].astype(jnp.bfloat16), "img", scatter_dimension=0, tiled=True
        ).astype(jnp.float32),
        lax.psum_scatter(
            parts[1].astype(jnp.bfloat16), "img", scatter_dimension=0, tiled=True
        ).astype(jnp.float32),
        lax.psum_scatter(
            parts[2].astype(jnp.bfloat16), "img", scatter_dimension=0, tiled=True
        ).astype(jnp.float32),
        lax.psum_scatter(
            parts[3].astype(jnp.bfloat16), "img", scatter_dimension=0, tiled=True
        ).astype(jnp.float32),
    )
    return (
        mixed,
        tokens_grad,
        grads[0],
        grads[1],
        grads[2],
        grads[3],
        ada_grad,
        q_gain_grad,
        k_gain_grad,
    )


VMEM_LIMIT = 63 << 20
MESH = pl.DeviceIdType.MESH
PAD = 128
TILE = 128
F32 = jnp.float32
BF16 = jnp.bfloat16


def dot(a, b):
    return lax.dot_general(a, b, (((1,), (0,)), ((), ())), preferred_element_type=F32)


def dot_nt(a, b):
    return lax.dot_general(a, b, (((1,), (1,)), ((), ())), preferred_element_type=F32)


def dot_tn(a, b, precision=None):
    return lax.dot_general(
        a, b, (((0,), (0,)), ((), ())), preferred_element_type=F32, precision=precision
    )


def lanes(shape):
    return lax.broadcasted_iota(jnp.int32, shape, len(shape) - 1)


def split3(value):
    high = value.astype(BF16)
    rest = value - high.astype(F32)
    mid = rest.astype(BF16)
    low = (rest - mid.astype(F32)).astype(BF16)
    return (high, mid, low)


def put_split3(tile, value, lane0):
    at = lanes(tile.shape)
    for k, term in enumerate(split3(value)):
        tile = jnp.where(at == lane0 + k, jnp.broadcast_to(term.astype(F32), tile.shape), tile)
    return tile


OUT, UP, DOWN, QKV = range(4)


def weight_chunks(width, hidden):
    half = width // 2
    quarter = hidden // 4

    def up(k):
        return [(UP, 2 * k + u, 0, half, quarter, "yz") for u in range(2)]

    return (
        [(OUT, 0, 0, half, width, "z")]
        + up(0)
        + up(1)
        + up(2)
        + [(DOWN, 0, 0, quarter, width, "yz")]
        + up(3)
        + [(DOWN, 0, quarter, quarter, width, "yz")]
        + [(QKV, 0, 0, half, 14 * PAD, "z"), (QKV, 1, 0, half, 13 * PAD, "")]
    )


def block_kernel(
    tok, cot, act_row, ada, wout, wup, wdown, wqkv, q_gain_row, k_gain_row, tab, grid_h, grid_w,
    mixed, tgrad, qkv_grad, ada_grad, gain_grad, down_grad, up_grad, out_grad, qkv_hbm,
    lb_down, lb_up, lb_out, rb_down, rb_up, rb_out,
    act, q_gain, k_gain, win, win_sem, tok_all, whv, woutv, wupv, wdownv, actbuf, modsend, modbuf, modv,
    cosv, sinv, qraw, kraw, qa, ka, va, kt, qt, onorm, attn_send, attn_in,
    do_in, dot_t, dqt, dkv_in, dq_in, dw_in, pc_in,
    x1v, branchv, ffnv, dh2v, dmod, dsend, dbuf,
    l_attn, l_h2, l_mid, r_ffn, r_branch, r_gu, l_h2s, l_attns, r_branchs,
    za_down, za_up, za_out, zb_down, zb_up, zb_out, z_out,
    gl_s, gl_r, gr_s, gr_r, gu_s, gu_r, g_loc, za_s, za_r, zb_s, zb_r, z_loc,
    tok_send, tok_recv, tok_loc, w_send, w_recv, w_loc, wh_sem, act_sem, mod_s, mod_r,
    at_s, at_r, do_s, do_r, dq_s, dq_r, dkv_s, dkv_r, dw_sem, pc_s, pc_r, dm_s, dm_r, loc,
):
    img, ty, z = lax.axis_index("img"), lax.axis_index("ty"), lax.axis_index("tx")
    b = ty * 4 + z
    me = img * 16 + b
    width = tok.shape[1]
    half = width // 2
    hidden = wup.shape[1] // 2
    part = ada.shape[0]
    other = 1 - img

    def dev(i=img, t=ty, k=z):
        return {"img": i, "ty": t, "tx": k}

    def dev_flat(p):
        return dev(p // 16, lax.rem(p // 4, 4), lax.rem(p, 4))

    def dev_tile(t):
        return dev(img, t // 4, lax.rem(t, 4))

    def rcopy(src, dst, s, r, d):
        return pltpu.make_async_remote_copy(
            src_ref=src, dst_ref=dst, send_sem=s, recv_sem=r, device_id=d, device_id_type=MESH
        )

    def loop(lo, hi, f):
        def step(k, c):
            f(k)
            return c

        lax.fori_loop(lo, hi, step, 0)

    bar = pltpu.get_barrier_semaphore()
    loop(
        1, 32,
        lambda k: pl.semaphore_signal(
            bar, inc=1, device_id=dev_flat(lax.rem(me + k, 32)), device_id_type=MESH
        ),
    )
    pl.semaphore_wait(bar, 31)

    hbm = (wout, wup, wdown, wqkv)
    vm = (woutv, wupv, wdownv, qkv_hbm)
    chunks = weight_chunks(width, hidden)

    y, c, z_bit = ty // 2, lax.rem(ty, 2), lax.rem(z, 2)
    to_x, to_y, to_z, to_c = dev(i=other), dev(t=ty ^ 2), dev(k=z ^ 1), dev(t=ty ^ 1)
    OWN, FROM_Y, FROM_Z, FAR_A, FAR_B, SIBLING = range(6)

    def w_ref(ref, i, row0, im, rel, sib=False):
        m, k, r0, rows, cols, ways = chunks[i]
        yy = 1 - y if rel in (FROM_Y, FAR_A, FAR_B) else y
        zz = 1 - z_bit if rel in (FROM_Z, FAR_A, FAR_B) else z_bit
        cc = 1 - c if sib else c
        col = k * 14 * PAD if m == QKV else 0
        if m == UP:
            col = (k % 2) * hidden + lax.rem(2 * im + k // 2, 4) * (hidden // 4)
        if ways == "yz" and m == UP:
            n, p = rows // 4, 2 * yy + zz
            cols = cols // 2
            col = col + cc * cols
        elif ways == "yz":
            n, p = rows // 8, 4 * yy + 2 * zz + cc
        elif ways == "":
            n, p = rows // 2, cc
        else:
            n, p = rows // 4, 2 * (yy if ways == "y" else zz) + cc
        row, size, first = row0 + r0 + p * n, n, (n // 32 + (n // 16) % 2) * 16
        if rel == FAR_A:
            size = first
        if rel == FAR_B:
            row, size = row + first, n - first
        return ref.at[
            pl.ds(pl.multiple_of(row, 16), size), pl.ds(pl.multiple_of(col, PAD), cols)
        ]

    def w_mine(i, rel, sib=False):
        m = chunks[i][0]
        return w_ref(vm[m], i, other * hbm[m].shape[0], img, rel, sib)

    def w_x(i):
        m = chunks[i][0]
        src = w_ref(hbm[m], i, 0, other, OWN)
        dst = w_ref(vm[m], i, img * hbm[m].shape[0], other, OWN)
        return rcopy(src, dst, w_send.at[i, 0], w_recv.at[i, 0], to_x)

    def w_copy(i, slot, held, rel, to):
        ref = w_mine(i, held)
        return rcopy(ref, ref, w_send.at[i, slot], w_recv.at[i, rel], to)

    def w_wait(i, rel, sib=False):
        ref = w_mine(i, rel, sib)
        at = rel + SIBLING if sib else rel
        rcopy(ref, ref, w_send.at[i, 0], w_recv.at[i, at], to_c).wait_recv()

    def w_sends(i):
        ways = chunks[i][5]
        first = [w_copy(i, 1, OWN, SIBLING + OWN, to_c)]
        if "y" in ways:
            first.append(w_copy(i, 2, OWN, FROM_Y, to_y))
        if "z" in ways:
            first.append(w_copy(i, 3, OWN, FROM_Z, to_z))
        sends = {OWN: first}
        if "z" in ways:
            sends[FROM_Z] = [w_copy(i, 4, FROM_Z, SIBLING + FROM_Z, to_c)]
        if "y" in ways:
            sends[FROM_Y] = [w_copy(i, 5, FROM_Y, SIBLING + FROM_Y, to_c)]
        if ways == "yz":
            far_a, far_b = w_far(i)
            sends[FROM_Z].insert(0, far_a)
            sends[FROM_Y].insert(0, far_b)
            sends[FAR_A] = [w_copy(i, 8, FAR_A, SIBLING + FAR_A, to_c)]
            sends[FAR_B] = [w_copy(i, 9, FAR_B, SIBLING + FAR_B, to_c)]
        return sends

    def w_far(i):
        m, _, _, rows, _, _ = chunks[i]
        n = rows // (4 if m == UP else 8)
        first = (n // 32 + (n // 16) % 2) * 16
        a = w_mine(i, FROM_Z).at[pl.ds(0, first)]
        b_ = w_mine(i, FROM_Y).at[pl.ds(first, n - first)]
        return (
            rcopy(a, a, w_send.at[i, 6], w_recv.at[i, FAR_A], to_y),
            rcopy(b_, b_, w_send.at[i, 7], w_recv.at[i, FAR_B], to_z),
        )

    def w_pass(which, rels):
        for i in which:
            sends = w_sends(i)
            for rel in rels:
                if rel in sends:
                    w_wait(i, rel)
                    for copy in sends[rel]:
                        copy.start()

    def x_arrived(*which):
        w_pass(which, (OWN,))

    def hop_arrived(*which):
        w_pass(which, (FROM_Z, FROM_Y))

    def far_arrived(*which):
        w_pass(which, (FAR_A, FAR_B))

    def w_done(*which):
        for i in which:
            for rel in w_sends(i):
                w_wait(i, rel, True)

    def w_drain(i):
        w_x(i).wait_send()
        for copies in w_sends(i).values():
            for copy in copies:
                copy.wait_send()

    def own(m):
        rows = hbm[m].shape[0]
        return pltpu.make_async_copy(hbm[m], vm[m].at[pl.ds(img * rows, rows)], w_loc.at[m])

    act[...] = jnp.broadcast_to(act_row[...], (8, width))
    gain_pad = jnp.zeros((1, PAD - HEAD), F32)
    q_gain[...] = jnp.concatenate([q_gain_row[...], gain_pad], axis=1)
    k_gain[...] = jnp.concatenate([k_gain_row[...], gain_pad], axis=1)

    def window(p):
        first = p * width + b * HEAD
        start = jnp.minimum(first // PAD * PAD, 3 * width - 2 * PAD)
        return pl.multiple_of(start, PAD), first - start

    wins = [
        pltpu.make_async_copy(
            wqkv.at[:, pl.ds(window(p)[0], 2 * PAD)], win.at[p], win_sem.at[p]
        )
        for p in range(3)
    ]
    for copy in wins:
        copy.start()
    act_copy = rcopy(act, actbuf.at[img], act_sem.at[0], act_sem.at[1], dev(i=other))
    act_copy.start()
    actbuf[img] = act[...]
    own_wh = whv.at[pl.ds(pl.multiple_of(img * half, 64), half)]
    wh_copy = rcopy(own_wh, own_wh, wh_sem.at[0], wh_sem.at[1], dev(i=other))
    for i in range(3):
        w_x(i).start()

    def tok_at(chunk):
        return tok_all.at[pl.ds(pl.multiple_of(chunk * TILE, TILE), TILE)]

    def tok_half(q):
        return tok_all.at[pl.ds(pl.multiple_of(q * 64, 64), 64)]

    def t_send(src, q, way, d):
        return rcopy(src, tok_half(q), tok_send.at[q, way], tok_recv.at[q], d)

    def t_wait(q):
        t_send(tok_half(q), q, 0, to_c).wait_recv()

    tok_own = pltpu.make_async_copy(tok, tok_at(b), tok_loc)
    tok_own.start()

    def t_forward(src, chunk, up, down):
        if up:

            @pl.when(z < 3)
            def _():
                t_send(src, chunk, 0, dev(k=z + 1)).start()

        if down:

            @pl.when(z > 0)
            def _():
                t_send(src, chunk, 1, dev(k=z - 1)).start()

        t_send(src, chunk, 2, dev(t=ty ^ 2)).start()
        t_send(src, chunk, 3, dev(t=ty ^ 1)).start()

    for h in range(2):
        t_forward(tok.at[pl.ds(64 * h, 64)], 2 * b + h, True, True)
    for m in range(3):
        own(m).start()

    act_copy.wait_recv()
    for i in range(2):
        modsend[i, :, 0:part] = dot_nt(actbuf[i].astype(BF16), ada[...])

    def mod_copy(p):
        return rcopy(modsend.at[p // 16], modbuf.at[me], mod_s.at[p], mod_r.at[me], dev_flat(p))

    loop(1, 32, lambda k: mod_copy(lax.rem(me + k, 32)).start())
    modbuf[me] = modsend[img]
    for p in range(3):
        wins[p].wait()
        shift = lax.rem(2 * PAD - window(p)[1], 2 * PAD)
        cols_p = pltpu.roll(win[p].astype(F32), shift, 1)[:, 0:PAD]
        at_lane = lax.broadcasted_iota(jnp.int32, (half, PAD), 1)
        own_wh[:, p * PAD : (p + 1) * PAD] = jnp.where(at_lane < HEAD, cols_p, 0.0).astype(BF16)
    wh_copy.start()
    for i in range(3, len(chunks)):
        w_x(i).start()

    for s in (1, 2, 3):
        for h in range(2):

            @pl.when(z - s >= 0)
            def _():
                q = 2 * (b - s) + h
                t_wait(q)
                t_forward(tok_half(q), q, True, False)

            @pl.when(z + s <= 3)
            def _():
                q = 2 * (b + s) + h
                t_wait(q)
                t_forward(tok_half(q), q, False, True)

    x_arrived(0, 1, 2)

    def t_y(k):
        q = (ty ^ 2) * 8 + k
        t_wait(q)
        t_send(tok_half(q), q, 3, to_c).start()

    loop(0, 8, t_y)
    hop_arrived(0)
    loop(0, 8, lambda k: t_wait((ty ^ 1) * 8 + k))
    loop(0, 8, lambda k: t_wait((ty ^ 3) * 8 + k))

    def t_drain(k):
        q, zz = ty * 8 + k, k // 2
        ref = tok_half(q)

        @pl.when((zz <= z) & (z < 3))
        def _():
            t_send(ref, q, 0, to_c).wait_send()

        @pl.when((zz >= z) & (z > 0))
        def _():
            t_send(ref, q, 1, to_c).wait_send()

        t_send(ref, q, 2, to_c).wait_send()
        t_send(ref, q, 3, to_c).wait_send()
        away = (ty ^ 2) * 8 + k
        t_send(tok_half(away), away, 3, to_c).wait_send()

    loop(0, 8, t_drain)
    tok_own.wait()

    def mod_wait(k):
        p = lax.rem(me + k, 32)
        rcopy(
            modsend.at[0], modbuf.at[p], mod_s.at[p], mod_r.at[p], dev_flat(p)
        ).wait()

    loop(1, 32, mod_wait)
    for s in range(32):
        modv[:, s * part : (s + 1) * part] = modbuf[s, :, 0:part]
    shift1, scale1, gate1, shift2, scale2, gate2 = [
        functools.partial(lambda k: modv[0:1, k * width : (k + 1) * width], k) for k in range(6)
    ]
    wh_copy.wait()

    height, wide = grid_h[0], grid_w[0]
    local = lax.broadcasted_iota(jnp.int32, (TILE, PAD), 0)
    lane = lax.broadcasted_iota(jnp.int32, (TILE, PAD), 1)

    def tile_layout(t):
        row_tile, col_tile = t // 4, lax.rem(t, 4)
        top = row_tile * height // 4
        rows = (row_tile + 1) * height // 4 - top
        left = col_tile * wide // 4
        span = (col_tile + 1) * wide // 4 - left
        spans = jnp.full((TILE, PAD), span, jnp.int32)
        quot = jnp.floor((local.astype(F32) + 0.5) / spans.astype(F32)).astype(jnp.int32)
        valid = local < jnp.full((TILE, PAD), rows * span, jnp.int32)
        row = jnp.where(valid, top + quot, 0)
        col = jnp.where(valid, left + local - quot * spans, 0)
        return valid, row, col

    def rope(n, c, s1, s2):
        return n * c + pltpu.roll(n, PAD - 18, 1) * s1 + pltpu.roll(n, 18, 1) * s2

    def unrope(d, c, s1, s2):
        return d * c + pltpu.roll(d * s1, 18, 1) + pltpu.roll(d * s2, PAD - 18, 1)

    def split_sin(sine):
        first = (lane < 18) | ((lane >= 36) & (lane < 54))
        return jnp.where(first, -sine, 0.0), jnp.where(first, 0.0, sine)

    def head_rows(t):
        valid, row, col = tile_layout(t)
        hot = jnp.where((lane == row) | (lane - 64 == col), 1.0, 0.0)
        angles = lax.dot_general(
            hot, tab[...], (((1,), (0,)), ((), ())),
            precision=HIGH, preferred_element_type=F32,
        )
        c, sine = angles[:, 0:PAD], angles[:, PAD : 2 * PAD]
        cosv[t] = c
        sinv[t] = sine
        s1, s2 = split_sin(sine)
        at = pl.ds(pl.multiple_of(t * TILE, TILE), TILE)
        x = tok_all[at, :].astype(F32)
        r = lax.rsqrt(jnp.mean(x * x, axis=1, keepdims=True) + EPS)
        h1 = ((x * r) * (1.0 + scale1()) + shift1()).astype(BF16)
        tok_all[at, :] = h1
        qkv = dot(h1, whv[...])
        q_r, k_r, v_r = qkv[:, 0:PAD], qkv[:, PAD : 2 * PAD], qkv[:, 2 * PAD : 3 * PAD]
        qraw[t] = q_r
        kraw[t] = k_r

        def normed(v, gain):
            rr = lax.rsqrt(jnp.sum(v * v, axis=1, keepdims=True) * (1.0 / HEAD) + EPS)
            return v * rr * gain[0:1, :]

        q_f = rope(normed(q_r, q_gain), c, s1, s2) * HEAD ** (-0.5)
        k_f = rope(normed(k_r, k_gain), c, s1, s2)
        qa[t] = jnp.where(lane == HEAD, 1.0, q_f).astype(BF16)
        k_f = jnp.where(lane == HEAD, jnp.where(valid, 0.0, -30000.0), k_f)
        k_f = jnp.where((lane > HEAD) & (lane < HEAD + 4), 1.0, k_f)
        ka[t] = k_f.astype(BF16)
        kt[:, pl.ds(pl.multiple_of(t * TILE, TILE), TILE)] = k_f.T.astype(BF16)
        va[t] = jnp.where((lane >= HEAD) & (lane < HEAD + 3), 1.0, v_r).astype(BF16)

    x_arrived(3, 4)
    hop_arrived(1, 2)
    loop(0, 8, head_rows)
    x_arrived(5, 6)
    hop_arrived(3, 4)
    loop(8, 16, head_rows)
    x_arrived(7)
    far_arrived(1, 2)
    hop_arrived(5, 6)

    def head_lanes(h):
        return attn_in.at[:, pl.ds(pl.multiple_of(h * PAD, PAD), PAD)]

    def at_copy(t):
        return rcopy(attn_send.at[t], head_lanes(b), at_s.at[t], at_r.at[b], dev_tile(t))

    def attend(k):
        q2 = qa[pl.ds(2 * k, 2)].reshape(2 * TILE, PAD)
        p = jnp.exp(dot(q2, kt[...])).astype(BF16)
        o = dot(p, va[...].reshape(16 * TILE, PAD))
        total = o[:, HEAD : HEAD + 1]
        o = o / total
        lse = jnp.log(total)
        q3 = put_split3(q2.astype(F32), -lse, HEAD + 1)
        o16 = o.astype(BF16)
        for u in range(2):
            t = 2 * k + u
            rows = slice(u * TILE, (u + 1) * TILE)
            onorm[t] = o[rows]
            qa[t] = q3[rows].astype(BF16)
            qt[:, pl.ds(pl.multiple_of(t * TILE, TILE), TILE)] = q3[rows].T.astype(BF16)
            attn_send[t] = o16[rows]

            @pl.when(t != b)
            def _():
                at_copy(t).start()

    loop(0, 8, attend)
    head_lanes(b)[...] = attn_send[b]
    x_arrived(8, 9, 10)
    far_arrived(3, 4)
    hop_arrived(7)

    def at_wait(k):
        p = lax.rem(b + k, 16)
        rcopy(attn_send.at[p], head_lanes(p), at_s.at[p], at_r.at[p], dev_tile(p)).wait()

    loop(1, 16, at_wait)

    def put_halves(ref, value):
        pad = jnp.zeros((TILE, 5 * PAD - half), F32)
        for k in range(2):
            piece = jnp.concatenate([value[:, k * half : (k + 1) * half], pad], axis=1)
            ref[:, k * 5 * PAD : (k + 1) * 5 * PAD] = piece.astype(BF16)

    def put_blocks(ref, value):
        pad = jnp.zeros((TILE, PAD - HEAD), F32)
        for k in range(16):
            zz = k % 4
            to = 4 * (k // 4) + 2 * (zz % 2) + zz // 2
            piece = jnp.concatenate([value[:, k * HEAD : (k + 1) * HEAD], pad], axis=1)
            ref[:, to * PAD : (to + 1) * PAD] = piece.astype(BF16)

    l_src, l_all = (l_mid, l_h2s, l_attns), (lb_down, lb_up, lb_out)
    r_src, r_all = (attn_in, r_gu, r_branchs), (rb_down, rb_up, rb_out)

    def slot_rows(i, t):
        return pl.ds(pl.multiple_of((i * 4 + t) * TILE, TILE), TILE)

    def lanes_at(k, n):
        return pl.ds(pl.multiple_of(k * n, PAD), n)

    def g_left(m, k, src, i, t, d):
        dst = l_all[m].at[slot_rows(i, t)]
        return rcopy(dst if src is None else src, dst, gl_s.at[m, k], gl_r.at[m, i * 4 + t], d)

    def g_right(m, k, src, i, t, d):
        n = r_src[m].shape[1] // 4
        dst = r_all[m].at[slot_rows(i, t)]
        if k in (2, 4, 5, 6):
            dst = r_all[m].at[slot_rows(i, t), lanes_at(1 - c, n)]
        return rcopy(dst if src is None else src, dst, gr_s.at[m, k], gr_r.at[m, i * 4 + t], d)

    def l_part(m, k):
        return l_src[m].at[:, lanes_at(k, l_src[m].shape[1] // 2)]

    def r_part(m, k, n):
        return r_src[m].at[:, lanes_at(k, n * (r_src[m].shape[1] // 4))]

    def g_first(m):
        return [
            g_left(m, 0, l_part(m, other), img, ty, to_x),
            g_right(m, 0, r_part(m, 1 - y, 2), img, ty, to_y),
            g_left(m, 1, l_part(m, img), img, ty, to_y),
            g_right(m, 1, r_part(m, y, 2), img, ty, to_x),
            g_left(m, 2, l_part(m, img), img, ty, to_c),
            g_right(m, 2, r_part(m, ty ^ 1, 1), img, ty, to_c),
        ]

    def g_own(m):
        n = r_src[m].shape[1] // 4
        rows = slot_rows(img, ty)
        return [
            pltpu.make_async_copy(l_part(m, img), l_all[m].at[rows], g_loc.at[m, 0]),
            pltpu.make_async_copy(
                r_part(m, ty, 1), r_all[m].at[rows, lanes_at(c, n)], g_loc.at[m, 1]
            ),
        ]

    def gl_x(m):
        g_first(m)[0].start()

    def gl_yc(m):
        g_first(m)[2].start()
        g_first(m)[4].start()
        g_own(m)[0].start()

    def gr_x(m):
        g_first(m)[3].start()

    def gr_yc(m):
        if m != 1:
            g_first(m)[1].start()
        g_first(m)[5].start()
        g_own(m)[1].start()

    def gu_lanes(i, k, base=0):
        n = hidden // 4
        return pl.ds(pl.multiple_of(base + lax.rem(2 * i + k, 4) * n, PAD), n)

    def gu_copy(w, k):
        dst = rb_up.at[slot_rows(img, ty ^ 2 if w == 2 else ty), gu_lanes(img, k)]
        src = dst
        if w < 2:
            src = r_gu.at[:, gu_lanes(img, k, (1 - y if w == 0 else y) * hidden)]
        return rcopy(src, dst, gu_s.at[w, k], gu_r.at[w, k], to_y if w == 0 else to_x)

    def gu_wait(w, k):
        i, t = (img, ty ^ 2) if w == 0 else (other, ty if w == 1 else ty ^ 2)
        ref = rb_up.at[slot_rows(i, t), gu_lanes(i, k)]
        rcopy(ref, ref, gu_s.at[w, k], gu_r.at[w, k], to_x).wait_recv()

    def gu_hop(k):
        gu_wait(0, k)
        gu_copy(2, k).start()

    def gl_hop(m):
        g_left(m, 0, None, other, ty, to_x).wait_recv()
        g_left(m, 3, None, other, ty, to_y).start()
        g_left(m, 4, None, other, ty, to_c).start()

    def gl_across(m):
        g_left(m, 1, None, img, ty ^ 2, to_y).wait_recv()
        g_left(m, 5, None, img, ty ^ 2, to_c).start()

    def gr_hop(m):
        if m != 1:
            g_right(m, 0, None, img, ty ^ 2, to_y).wait_recv()
            g_right(m, 3, None, img, ty ^ 2, to_x).start()
        g_right(m, 4, None, img, ty ^ 2, to_c).start()
        if m != 1:
            g_right(m, 1, None, other, ty, to_x).wait_recv()
        else:
            for k in range(4):
                gu_wait(1, k)
        g_right(m, 5, None, other, ty, to_c).start()

    def gl_hop2(m):
        g_left(m, 3, None, other, ty ^ 2, to_y).wait_recv()
        g_left(m, 6, None, other, ty ^ 2, to_c).start()

    def gr_hop2(m):
        if m != 1:
            g_right(m, 3, None, other, ty ^ 2, to_x).wait_recv()
        else:
            for k in range(4):
                gu_wait(2, k)
        g_right(m, 6, None, other, ty ^ 2, to_c).start()

    def g_done(m):
        n = r_src[m].shape[1] // 4
        for i in range(2):
            for t in (ty ^ 1, ty ^ 3):
                g_left(m, 2, None, i, t, to_c).wait_recv()
                ref = r_all[m].at[slot_rows(i, t), lanes_at(c, n)]
                rcopy(ref, ref, gr_s.at[m, 2], gr_r.at[m, i * 4 + t], to_c).wait_recv()
        for copy in g_own(m):
            copy.wait()

    def g_drain(m):
        for k, copy in enumerate(g_first(m)):
            if m != 1 or k not in (1, 3):
                copy.wait_send()
        for k, i, t in ((3, other, ty), (4, other, ty), (5, img, ty ^ 2), (6, other, ty ^ 2)):
            g_left(m, k, None, i, t, to_c).wait_send()
        for k, i, t in ((3, img, ty ^ 2), (4, img, ty ^ 2), (5, other, ty), (6, other, ty ^ 2)):
            if m != 1 or k != 3:
                g_right(m, k, None, i, t, to_c).wait_send()
        if m == 1:
            for w in range(3):
                for k in range(4):
                    gu_copy(w, k).wait_send()

    attn = jnp.concatenate(
        [attn_in[:, h * PAD : h * PAD + HEAD].astype(F32) for h in range(16)], axis=1
    )
    l_attn[...] = attn.astype(BF16)
    put_halves(l_attns, attn)
    own(OUT).wait()
    w_done(0)
    own_valid = tile_layout(b)[0]
    keep = jnp.where(own_valid, 1.0, 0.0)[:, 0:1]
    cols = width // 3

    def project(k):
        at = pl.ds(pl.multiple_of(k * cols, PAD), cols)
        branchv[:, at] = dot(l_attn[...], woutv[:, at])

    loop(0, 3, project)
    far_arrived(5, 6)
    x = tok[...].astype(F32)
    x1 = x + keep * gate1() * branchv[...]
    x1v[...] = x1
    r = lax.rsqrt(jnp.mean(x1 * x1, axis=1, keepdims=True) + EPS)
    h2_rows = (x1 * r) * (1.0 + scale2()) + shift2()
    l_h2[...] = h2_rows.astype(BF16)
    put_halves(l_h2s, h2_rows)
    d_ffn = cot[...].astype(F32) * keep * gate2()
    r_ffn[...] = d_ffn.astype(BF16)
    put_blocks(attn_in, d_ffn)
    ffnv[...] = jnp.zeros_like(ffnv)
    dh2v[...] = jnp.zeros_like(dh2v)
    own(UP).wait()
    own(DOWN).wait()
    step = 256

    def mlp(j):
        g_at = pl.ds(pl.multiple_of(j, step), step)
        u_at = pl.ds(pl.multiple_of(hidden + j, step), step)
        h2 = l_h2[...]
        gate = dot(h2, wupv[:, g_at])
        up = dot(h2, wupv[:, u_at])
        sig = 1.0 / (1.0 + jnp.exp(-gate))
        act_g = gate * sig
        mid = (act_g * up).astype(BF16)
        l_mid[:, g_at] = mid
        w3 = wdownv[g_at, :]
        ffnv[...] += dot(mid, w3)
        d_mid = dot_nt(r_ffn[...], w3)
        d_gate = (d_mid * up * (sig + gate * sig * (1.0 - sig))).astype(BF16)
        d_up = (d_mid * act_g).astype(BF16)
        r_gu[:, g_at] = d_gate
        r_gu[:, u_at] = d_up
        dh2v[...] += dot_nt(d_gate, wupv[:, g_at]) + dot_nt(d_up, wupv[:, u_at])

    def mlp_quarter(k):
        first = lax.rem(2 * img + k, 4) * (hidden // 4)
        loop(0, hidden // 4 // step, lambda j: mlp(first + j * step))

    gl_x(1)
    w_done(1, 2)
    mlp_quarter(0)
    gu_copy(1, 0).start()
    far_arrived(7)
    hop_arrived(8, 9)
    w_done(3, 4)
    mlp_quarter(1)
    gu_copy(1, 1).start()
    hop_arrived(10)
    far_arrived(8, 9)
    w_done(5, 6, 7)
    mlp_quarter(2)
    gu_copy(1, 2).start()
    gu_copy(0, 0).start()
    far_arrived(10)
    w_done(8, 9, 10)
    mlp_quarter(3)
    gu_copy(1, 3).start()
    gu_copy(0, 1).start()
    ffn = ffnv[...]
    g = cot[...].astype(F32)
    x1 = x1v[...]
    mixed[...] = (x1 + keep * gate2() * ffn).astype(BF16)

    def dmod_put(k, row):
        dmod[0:1, k * width : (k + 1) * width] = row

    def colsum(v):
        return jnp.sum(v, axis=0, keepdims=True)

    dmod_put(5, colsum(g * keep * ffn))
    d_h2 = dh2v[...]
    norm2 = x1 * r
    dmod_put(4, colsum(d_h2 * norm2))
    dmod_put(3, colsum(d_h2))
    d_n2 = d_h2 * (1.0 + scale2())
    d_x1 = g + r * (d_n2 - norm2 * jnp.mean(d_n2 * norm2, axis=1, keepdims=True))
    dmod_put(2, colsum(d_x1 * keep * branchv[...]))
    x1v[...] = d_x1
    d_branch = d_x1 * keep * gate1()
    r_branch[...] = d_branch.astype(BF16)
    put_blocks(r_branchs, d_branch)

    def unproject(k):
        at = pl.ds(pl.multiple_of(k * cols, PAD), cols)
        branchv[:, at] = dot_nt(r_branch[...], woutv[at, :])

    loop(0, 3, unproject)

    zeros = jnp.zeros((TILE, PAD - HEAD), F32)
    d_attn = branchv[...]
    for h in range(16):
        attn_send[h] = jnp.concatenate(
            [d_attn[:, h * HEAD : (h + 1) * HEAD], zeros], axis=1
        ).astype(BF16)

    def do_copy(t):
        return rcopy(attn_send.at[t], do_in.at[b], do_s.at[t], do_r.at[b], dev_tile(t))

    loop(1, 16, lambda k: do_copy(lax.rem(b + k, 16)).start())
    do_in[b] = attn_send[b]
    gu_copy(0, 2).start()
    gu_copy(0, 3).start()
    x_arrived(11)
    gl_yc(1)
    gl_hop(1)
    gr_yc(1)
    gu_hop(0)
    gu_hop(1)
    gl_x(2)
    gl_yc(2)
    gr_yc(0)
    gr_yc(2)
    gl_yc(0)

    def do_wait(k):
        p = lax.rem(b + k, 16)
        rcopy(attn_send.at[p], do_in.at[p], do_s.at[p], do_r.at[p], dev_tile(p)).wait()

    loop(1, 16, do_wait)
    gu_hop(2)
    x_arrived(12)

    def delta(t):
        d = do_in[t].astype(F32)
        dsum = jnp.sum(jnp.where(lane < HEAD, d * onorm[t], 0.0), axis=1, keepdims=True)
        d = put_split3(d, -dsum, HEAD)
        do_in[t] = d.astype(BF16)
        dot_t[:, pl.ds(pl.multiple_of(t * TILE, TILE), TILE)] = d.T.astype(BF16)

    loop(0, 16, delta)
    gu_hop(3)
    gr_x(0)
    gl_x(0)
    gr_x(2)
    gl_hop(2)
    dqt[...] = jnp.zeros_like(dqt)

    high, low = z // 2, lax.rem(z, 2)
    l0 = 3 * width

    def z_load(m):
        kl, n = l_all[m].shape[1], r_src[m].shape[1] // 4
        copies = [
            pltpu.make_async_copy(
                l_all[m], wupv.at[pl.ds(0, 8 * TILE), pl.ds(l0, kl)], z_loc.at[0]
            ),
            pltpu.make_async_copy(
                r_all[m].at[:, lanes_at(c, n)],
                wupv.at[pl.ds(0, 8 * TILE), pl.ds(l0 + kl, n)],
                z_loc.at[1],
            ),
        ]
        for copy in copies:
            copy.start()
        for copy in copies:
            copy.wait()

    def z_copies(m):
        if m == 0:
            sent = [kt.at[pl.ds(0, 80), pl.ds(0, 12 * PAD)], qt.at[pl.ds(0, 80), pl.ds(0, 12 * PAD)]]
        elif m == 1:
            sent = [wupv.at[pl.ds(k * half, half), pl.ds(44 * PAD, 3 * PAD)] for k in range(2)]
        else:
            sent = [tok_all.at[pl.ds(640 + 128 * k, 80), pl.ds(0, 5 * PAD)] for k in range(2)]
        return [
            rcopy(sent[k], za[m].at[k], za_s.at[m, k], za_r.at[m, k], dev(k=z ^ 1))
            for k in range(2)
        ]

    za, zb = (za_down, za_up, za_out), (zb_down, zb_up, zb_out)
    z_rest = (
        dot_t.at[pl.ds(0, 80), pl.ds(0, 12 * PAD)],
        wdownv.at[pl.ds(19 * TILE, half), pl.ds(0, 3 * PAD)],
        tok_all.at[pl.ds(896, 80), pl.ds(0, 5 * PAD)],
    )
    z_own = (dqt.at[pl.ds(0, 80), pl.ds(0, 12 * PAD)], up_grad, z_out)

    def z_copy2(m, part=0):
        src, dst, k = z_rest[m], zb[m], m
        if m == 1:
            at = pl.ds(part * (half // 2), half // 2)
            src, dst, k = src.at[at], dst.at[at], 1 + 2 * part
        return rcopy(src, dst, zb_s.at[k], zb_r.at[k], dev(k=z ^ 2))

    def z_product(m):
        kl = l_all[m].shape[1]
        sent = [copy.src_ref for copy in z_copies(m)]
        if m == 1:

            def turn(k):
                at = pl.ds(pl.multiple_of(k * TILE, TILE), TILE)
                woutv[0 : 5 * PAD, at] = wupv[at, l0 : l0 + kl].astype(F32).T.astype(BF16)

            loop(0, 8, turn)

            def block(zz):
                at = pl.ds(pl.multiple_of(l0 + kl + zz * 3 * PAD, PAD), 3 * PAD)
                return dot(woutv[0:half, 0 : 8 * TILE], wupv[0 : 8 * TILE, at])

            for k in range(2):
                sent[k][...] = block(2 * k + 1 - low).astype(BF16)
            for copy in z_copies(m):
                copy.start()
            z_rest[m][...] = block(2 * (1 - high) + low).astype(BF16)
            z_own[m][...] = block(z)
            return

        def pair(k):
            at = pl.ds(pl.multiple_of(l0 + kl + k * 2 * PAD, PAD), 2 * PAD)
            return dot_tn(wupv[0 : 8 * TILE, at], wupv[0 : 8 * TILE, l0 : l0 + kl])

        both = pair(1 - low)
        for k in range(2):
            sent[k][...] = both[k * PAD : k * PAD + 80].astype(BF16)
        for copy in z_copies(m):
            copy.start()
        both = pair(low)
        first, second = both[0:80], both[PAD : PAD + 80]
        z_rest[m][...] = jnp.where(high == 0, second, first).astype(BF16)
        z_own[m][...] = jnp.where(high == 0, first, second)

    def z_second(m):
        for copy in z_copies(m):
            copy.wait()
        rest = z_rest[m][...].astype(F32) + za[m][1 - high].astype(F32)
        z_rest[m][...] = rest.astype(BF16)
        z_copy2(m).start()
        z_own[m][...] += za[m][high].astype(F32)

    def z_last(m):
        z_copy2(m).wait()
        if m == 1:
            z_copy2(m, 1).wait()
        z_own[m][...] += zb[m][...].astype(F32)

    gain_grad[...] = jnp.zeros_like(gain_grad)
    for i in range(11):
        w_drain(i)

    def kv_send(k, u):
        at = pl.ds(pl.multiple_of(k * 2 * HEAD, 16), 2 * HEAD)
        return wdownv.at[at, pl.ds((3 + u) * PAD, PAD)]

    def q_send(k, u):
        at = pl.ds(pl.multiple_of(width + k * 80, 16), 80)
        return wdownv.at[at, pl.ds((3 + u) * PAD, PAD)]

    def kv_copy(k, u):
        t = 2 * k + u
        return rcopy(kv_send(k, u), dkv_in.at[b], dkv_s.at[t], dkv_r.at[b], dev_tile(t))

    def q_copy(k, u):
        t = 2 * k + u
        return rcopy(q_send(k, u), dq_in.at[b], dq_s.at[t], dq_r.at[b], dev_tile(t))

    def head_back(d, v, gain, row, t):
        c_, (s1, s2) = cosv[t], split_sin(sinv[t])
        d = unrope(d, c_, s1, s2)
        rr = lax.rsqrt(jnp.sum(v * v, axis=1, keepdims=True) * (1.0 / HEAD) + EPS)
        n = v * rr
        gain_grad[row : row + 1, :] += colsum(d * n)
        dn = d * gain[0:1, :]
        return rr * (dn - n * (jnp.sum(dn * n, axis=1, keepdims=True) * (1.0 / HEAD)))

    def send_tile(k, u, copy, keep_own):
        copy_ = copy(k, u)

        @pl.when(2 * k + u != b)
        def _():
            copy_.start()

        @pl.when(2 * k + u == b)
        def _():
            keep_own[b] = copy_.src_ref[...]

    def attend_back(k):
        two = pl.ds(2 * k, 2)
        p = jnp.exp(dot(ka[two].reshape(2 * TILE, PAD), qt[...]))
        ds = (p * dot(va[two].reshape(2 * TILE, PAD), dot_t[...])).astype(BF16)
        d_k2 = dot(ds, qa[...].reshape(16 * TILE, PAD))
        d_v2 = dot(p.astype(BF16), do_in[...].reshape(16 * TILE, PAD))
        at = pl.ds(pl.multiple_of(k * 2 * TILE, 2 * TILE), 2 * TILE)
        dqt[...] += dot(kt[:, at], ds)
        for u in range(2):
            t = 2 * k + u
            rows = slice(u * TILE, (u + 1) * TILE)
            d_k = head_back(d_k2[rows], kraw[t], k_gain, 1, t)
            d_v = jnp.where(lane < HEAD, d_v2[rows], 0.0)
            at = pl.ds(pl.multiple_of(t * TILE, TILE), TILE)
            wdownv[at, PAD : 3 * PAD] = jnp.concatenate([d_k, d_v], axis=1).astype(BF16)
            turned = jnp.concatenate([d_k.T[0:HEAD], d_v.T[0:HEAD]], axis=0)
            kv_send(k, u)[...] = turned.astype(BF16)
            send_tile(k, u, kv_copy, dkv_in)

    loop(0, 4, attend_back)
    gl_across(1)
    gr_hop(1)
    hop_arrived(11)
    loop(4, 6, attend_back)
    gl_hop2(1)
    gr_hop2(1)
    g_done(1)
    z_load(1)
    z_product(1)
    loop(6, 8, attend_back)
    gl_hop(0)
    gr_hop(0)

    def heads_back(k):
        for u in range(2):
            t = 2 * k + u
            at = pl.ds(pl.multiple_of(t * TILE, TILE), TILE)
            d_q = dqt[:, at].T * HEAD ** (-0.5)
            d_q = head_back(d_q, qraw[t], q_gain, 0, t)
            wdownv[at, 0:PAD] = d_q.astype(BF16)
            q_send(k, u)[...] = d_q.T[0:80].astype(BF16)
            send_tile(k, u, q_copy, dq_in)

    loop(0, 8, heads_back)
    gr_hop(2)
    w_done(11, 12)
    w_drain(11)
    w_drain(12)


    sums_t = (branchv, ffnv, dh2v)
    for ref in sums_t:
        ref[...] = jnp.zeros((PAD, width), F32)

    def dw_rows(k):
        at = pl.ds(pl.multiple_of(k * 2 * TILE, TILE), 2 * TILE)
        term = dot_tn(wdownv[at, 0 : 3 * PAD], tok_all[at, :])
        for p in range(3):
            sums_t[p][...] += term[p * PAD : (p + 1) * PAD]

    loop(0, 8, dw_rows)
    half_pad = jnp.zeros((80, 5 * PAD - half), F32)
    for p in range(3):
        for i in range(2):
            piece = sums_t[p][0:80, i * half : (i + 1) * half]
            at = slice((3 * i + p) * 80, (3 * i + p + 1) * 80)
            tok_all[at, 0 : 5 * PAD] = jnp.concatenate([piece, half_pad], axis=1).astype(BF16)

    def dw_half(i):
        return tok_all.at[pl.ds(pl.multiple_of(i * 240, 16), 240), pl.ds(0, 5 * PAD)]

    dw_copy = rcopy(dw_half(other), dw_in, dw_sem.at[0], dw_sem.at[1], dev(i=other))
    dw_copy.start()

    loads = [
        pltpu.make_async_copy(
            src, wupv.at[pl.ds(owner * half, half), pl.ds(0, 3 * width)], loc.at[k]
        )
        for k, (src, owner) in enumerate(
            ((wqkv, img), (qkv_hbm.at[pl.ds(other * half, half)], other))
        )
    ]
    for load in loads:
        load.start()

    def dq_wait(k):
        p = lax.rem(b + k, 16)
        kv, q_ = dkv_in.at[p], dq_in.at[p]
        rcopy(kv, kv, dkv_s.at[p], dkv_r.at[p], dev_tile(p)).wait()
        rcopy(q_, q_, dq_s.at[p], dq_r.at[p], dev_tile(p)).wait()

    z_second(1)
    loop(1, 16, dq_wait)
    for m in (0, 2):
        gl_across(m)
        gl_hop2(m)
        gr_hop2(m)
    g_done(0)
    z_load(0)
    z_product(0)
    z_copy2(1, 1).start()
    for load in loads:
        load.wait()

    def own_part(p):
        return slice(16 * TILE + p * TILE, 16 * TILE + (p + 1) * TILE)

    for p in range(3):
        got, r0 = (dq_in, 0) if p == 0 else (dkv_in, (p - 1) * HEAD)
        turned = jnp.concatenate(
            [got[h].astype(F32)[r0 : r0 + HEAD] for h in range(16)], axis=0
        )
        wdownv[own_part(p), :] = turned.T.astype(BF16)

    def h1_back(k):
        at = pl.ds(pl.multiple_of(k * cols, PAD), cols)
        dh2v[:, at] = sum(
            dot_nt(wdownv[own_part(p), :], wupv[at, p * width : (p + 1) * width])
            for p in range(3)
        )

    loop(0, 3, h1_back)
    d_h1 = dh2v[...]
    x = tok[...].astype(F32)
    r1 = lax.rsqrt(jnp.mean(x * x, axis=1, keepdims=True) + EPS)
    norm1 = x * r1
    dmod_put(1, colsum(d_h1 * norm1))
    dmod_put(0, colsum(d_h1))
    d_n1 = d_h1 * (1.0 + scale1())
    back = r1 * (d_n1 - norm1 * jnp.mean(d_n1 * norm1, axis=1, keepdims=True))
    tgrad[...] = (x1v[...] + back).astype(BF16)

    dsend[...] = jnp.zeros_like(dsend)
    for s in range(32):
        dsend[s, 0:1, 0:part] = dmod[0:1, s * part : (s + 1) * part]
        dsend[s, 1:3, 0:PAD] = gain_grad[0:2, :]

    def dm_copy(p):
        return rcopy(dsend.at[p], dbuf.at[me], dm_s.at[p], dm_r.at[me], dev_flat(p))

    loop(1, 32, lambda k: dm_copy(lax.rem(me + k, 32)).start())
    dbuf[me] = dsend[me]

    g_done(2)
    z_load(2)
    z_product(2)
    dw_copy.wait()
    dw_sum = dw_half(img)[...].astype(F32) + dw_in[...].astype(F32)

    def pc_send(p):
        return tok_all.at[pl.ds(1024 + 80 * p, 80), pl.ds(0, 5 * PAD)]

    for p in range(3):
        pc_send(p)[...] = dw_sum[80 * p : 80 * (p + 1)].astype(BF16)

    def pc_copy(p):
        group = 16 * p + b
        to, slot = group // 3, lax.rem(group, 3)
        return to, rcopy(
            pc_send(p), pc_in.at[slot], pc_s.at[p], pc_r.at[slot], dev_tile(to)
        )

    for p in range(3):
        to, copy = pc_copy(p)

        @pl.when(to != b)
        def _():
            copy.start()

        @pl.when(to == b)
        def _():
            pc_in[lax.rem(16 * p + b, 3)] = pc_send(p)[...]

    z_second(0)
    z_second(2)
    z_last(1)
    z_last(0)
    z_last(2)
    g_drain(0)
    g_drain(1)
    g_drain(2)
    down_grad[...] = z_own[0][0:HEAD, :]
    out_grad[...] = z_own[2][0:HEAD, 0:half]
    for slot in range(3):
        group = 3 * b + slot
        src = lax.rem(group, 16)

        @pl.when(src != b)
        def _():
            rcopy(
                pc_send(0), pc_in.at[slot], pc_s.at[0], pc_r.at[slot], dev_tile(src)
            ).wait_recv()

    for slot in range(3):
        at = slice(slot * HEAD, (slot + 1) * HEAD)
        qkv_grad[at, :] = pc_in[slot].astype(F32)[0:HEAD, 0:half]
    for p in range(3):
        to, copy = pc_copy(p)

        @pl.when(to != b)
        def _():
            copy.wait_send()

    def dm_wait(k):
        p = lax.rem(me + k, 32)
        rcopy(dsend.at[p], dbuf.at[p], dm_s.at[p], dm_r.at[p], dev_flat(p)).wait()

    loop(1, 32, dm_wait)
    sums = [
        lax.fori_loop(1, 16, lambda s, a, i=i: a + dbuf[16 * i + s], dbuf[16 * i])
        for i in range(2)
    ]
    gain_grad[...] = jnp.where(
        lax.broadcasted_iota(jnp.int32, (8, PAD), 0) < 2,
        pltpu.roll(sums[0] + sums[1], 7, 0)[:, 0:PAD],
        0.0,
    )
    row = lax.broadcasted_iota(jnp.int32, (8, 2 * PAD), 0)
    d_two = jnp.where(row == 0, sums[0][0:1, :], jnp.where(row == 1, sums[1][0:1, :], 0.0))
    row = lax.broadcasted_iota(jnp.int32, (8, width), 0)
    a_two = jnp.where(row == 0, actbuf[0], jnp.where(row == 1, actbuf[1], 0.0))
    ada_grad[...] = dot_tn(d_two, a_two, HIGH)[0:part, :]
    act_copy.wait_send()


def rope_table():
    table = np.zeros((PAD, 2 * PAD), np.float64)
    angle = np.arange(64)[:, None] * 10000.0 ** (-np.arange(18) / 18)
    for axis in range(2):
        rows = slice(64 * axis, 64 * axis + 64)
        for quarter in range(2):
            at = 36 * axis + 18 * quarter
            table[rows, at : at + 18] = np.cos(angle)
            table[rows, PAD + at : PAD + at + 18] = np.sin(angle)
    return table.astype(np.float32)


def run_block(tokens, cotangent, act, ada, wout, wup, wdown, wqkv, q_gain, k_gain, grid_h, grid_w):
    width, hidden = tokens.shape[1], wup.shape[1] // 2
    half, part = width // 2, ada.shape[0]
    vmem, any_ = pl.BlockSpec(memory_space=pltpu.VMEM), pl.BlockSpec(memory_space=pl.ANY)
    smem = pl.BlockSpec(memory_space=pltpu.SMEM)
    sds = jax.ShapeDtypeStruct
    v, dma = pltpu.VMEM, pltpu.SemaphoreType.DMA
    n_chunks = len(weight_chunks(width, hidden))
    tile16 = (16, TILE, PAD)
    out_shape = (
        sds((TILE, width), BF16),
        sds((TILE, width), BF16),
        sds((3 * HEAD, half), F32),
        sds((part, width), F32),
        sds((8, PAD), F32),
        sds((HEAD, hidden // 2), F32),
        sds((half, 3 * PAD), F32),
        sds((HEAD, half), F32),
        sds((width, 3 * width), BF16),
        sds((8 * TILE, hidden // 2), BF16),
        sds((8 * TILE, 5 * PAD), BF16),
        sds((8 * TILE, 5 * PAD), BF16),
        sds((8 * TILE, 8 * PAD), BF16),
        sds((8 * TILE, hidden), BF16),
        sds((8 * TILE, 8 * PAD), BF16),
    )
    scratch = [
        v((8, width), F32),
        v((1, PAD), F32),
        v((1, PAD), F32),
        v((3, half, 2 * PAD), BF16),
        dma((3,)),
        v((16 * TILE, width), BF16),
        v((width, 3 * PAD), BF16),
        v((width, width), BF16),
        v((width, 2 * hidden), BF16),
        v((hidden, width), BF16),
        v((2, 8, width), F32),
        v((2, 8, 2 * PAD), F32),
        v((32, 8, 2 * PAD), F32),
        v((8, 6 * width), F32),
        v(tile16, F32),
        v(tile16, F32),
        v(tile16, F32),
        v(tile16, F32),
        v(tile16, BF16),
        v(tile16, BF16),
        v(tile16, BF16),
        v((PAD, 16 * TILE), BF16),
        v((PAD, 16 * TILE), BF16),
        v(tile16, F32),
        v(tile16, BF16),
        v((TILE, 16 * PAD), BF16),
        v(tile16, BF16),
        v((PAD, 16 * TILE), BF16),
        v((PAD, 16 * TILE), F32),
        v((16, 2 * HEAD, PAD), BF16),
        v((16, 80, PAD), BF16),
        v((240, 5 * PAD), BF16),
        v((3, 80, 5 * PAD), BF16),
        v((TILE, width), F32),
        v((TILE, width), F32),
        v((TILE, width), F32),
        v((TILE, width), F32),
        v((8, 6 * width), F32),
        v((32, 8, 2 * PAD), F32),
        v((32, 8, 2 * PAD), F32),
        v((TILE, width), BF16),
        v((TILE, width), BF16),
        v((TILE, hidden), BF16),
        v((TILE, width), BF16),
        v((TILE, width), BF16),
        v((TILE, 2 * hidden), BF16),
        v((TILE, 10 * PAD), BF16),
        v((TILE, 10 * PAD), BF16),
        v((TILE, 16 * PAD), BF16),
        v((2, 80, hidden // 2), BF16),
        v((2, half, 3 * PAD), BF16),
        v((2, 80, 5 * PAD), BF16),
        v((80, hidden // 2), BF16),
        v((half, 3 * PAD), BF16),
        v((80, 5 * PAD), BF16),
        v((80, 5 * PAD), F32),
        dma((3, 8)),
        dma((3, 8)),
        dma((3, 8)),
        dma((3, 8)),
        dma((3, 4)),
        dma((3, 4)),
        dma((3, 2)),
        dma((3, 2)),
        dma((3, 2)),
        dma((4,)),
        dma((4,)),
        dma((2,)),
        dma((32, 4)),
        dma((32,)),
        dma,
        dma((n_chunks, 10)),
        dma((n_chunks, 10)),
        dma((4,)),
        dma((2,)),
        dma((2,)),
        dma((32,)),
        dma((32,)),
        dma((16,)),
        dma((16,)),
        dma((16,)),
        dma((16,)),
        dma((16,)),
        dma((16,)),
        dma((16,)),
        dma((16,)),
        dma((2,)),
        dma((3,)),
        dma((3,)),
        dma((32,)),
        dma((32,)),
        dma((2,)),
    ]
    return pl.pallas_call(
        block_kernel,
        out_shape=out_shape,
        in_specs=[vmem] * 4 + [any_] * 4 + [vmem] * 3 + [smem] * 2,
        out_specs=[vmem] * 8 + [any_] * 7,
        scratch_shapes=scratch,
        compiler_params=pltpu.CompilerParams(
            collective_id=0, has_side_effects=True, vmem_limit_bytes=VMEM_LIMIT
        ),
    )(
        tokens, cotangent, act, ada, wout, wup, wdown, wqkv, q_gain, k_gain, rope_table(),
        grid_h, grid_w,
    )


def fast_body(
    tokens,
    cotangent,
    class_embed,
    timestep,
    grid_height,
    grid_width,
    qkv_weight,
    out_weight,
    up_weight,
    down_weight,
    ada_weight,
    q_gain,
    k_gain,
):
    width = tokens.shape[2]
    act = jax.nn.silu(class_embed + time_embed(timestep, width)).astype(BF16).astype(F32)
    (mixed, tgrad, qkv_grad, ada_grad, gains, down_grad, up_grad, out_grad) = (
        run_block(
            tokens[0],
            cotangent[0],
            act,
            ada_weight,
            out_weight,
            up_weight,
            down_weight,
            qkv_weight,
            q_gain[None],
            k_gain[None],
            grid_height,
            grid_width,
        )[:8]
    )
    return (
        mixed[None],
        tgrad[None],
        qkv_grad.T,
        out_grad.T,
        up_grad,
        down_grad.T,
        ada_grad,
        gains[0, :HEAD],
        gains[1, :HEAD],
    )


def solution(mesh):
    in_specs = (
        P("img", ("ty", "tx"), None),
        P("img", ("ty", "tx"), None),
        P("img", None),
        P("img"),
        P("img"),
        P("img"),
        P("img", None),
        P("img", None),
        P("img", None),
        P("img", None),
        P(("img", "ty", "tx"), None),
        P(),
        P(),
    )
    out_specs = (
        P("img", ("ty", "tx"), None),
        P("img", ("ty", "tx"), None),
        P("img", ("ty", "tx")),
        P("img", ("ty", "tx")),
        P("img", ("ty", "tx")),
        P("img", ("ty", "tx")),
        P(("img", "ty", "tx"), None),
        P(),
        P(),
    )
    shape = dict(mesh.shape)
    fast = (shape["img"], shape["ty"], shape["tx"]) == (2, 4, 4)
    body = fast_body if fast else general_body
    return jax.shard_map(body, mesh=mesh, in_specs=in_specs, out_specs=out_specs, check_vma=False)
```
